32 devices in a mesh: pool: 16 (over z, x, core), head: 2 (over y).
Axes of the slice: x: 2, y: 2, z: 4, core: 2. Of those that a mesh axis runs over, the one named last changes fastest.
Arguments:
- queries: bfloat16 [16, 128, 4096], P('pool', None, 'head'), may hold values from -128 to 128
- request_keys: bfloat16 [16, 128, 1024], P('pool', None, 'head'), may hold values from -8 to 8
- request_values: bfloat16 [16, 128, 1024], P('pool', None, 'head'), may hold values from -6 to 6
- cache_keys: bfloat16 [32, 8, 128, 128], P('pool', 'head'), may hold values from -6 to 6
- cache_values: bfloat16 [32, 8, 128, 128], P('pool', 'head'), may hold values from -6 to 6
- passage_ids: int32 [16, 16], P('pool'), may hold values from 0 to 31, as said below
- passage_order: int32 [16, 16], P('pool'), may hold values from 0 to 15, each once within a row
- out_weight: bfloat16 [4096, 4096], P(('head', 'pool')), may hold values from -6 to 6
Outputs:
- mixed: bfloat16 [16, 128, 4096], P('pool', None, 'head')
The draws below stay inside these ranges and needn't reach their ends.
Inputs may be any that keep to these rules, and one draw needn't show every extreme that they name: `passage_ids`: the 16 passages of one request are held by 16 different indices of pool, one passage of each index; passage i is held by index i // 2.
All inputs are finite; a program needn't handle non-finite values.
Results may differ from the reference program's by a relative error of at most 0.012.
Values may be sent and summed in bfloat16 or wider, within the bound.
No kernel may reach another device: no remote copies, remote signals or barrier semaphores. Data moves between devices by JAX's collectives and lax.ppermute only.
A program may use at most 128 MiB of HBM per device.

```python
import jax
import jax.numpy as jnp
from jax import lax

HD = 128
KVH = 8
QH = 32
D_OUT = 4096
Q_LEN = 128
PASS_LEN = 128
PASS_DEV = 2
K_SEL = 16
REQUESTS = 16
PASSAGES = 32


def shared_keys(key):
    common = jax.random.normal(key, (REQUESTS, Q_LEN, KVH * HD), jnp.float32)
    return jnp.clip(common, -6.0, 6.0)


def draw_request_keys(key, part):
    common = shared_keys(key)
    return common.astype(jnp.bfloat16)


def draw_queries(key, part):
    key = jax.random.fold_in(key, 5)
    values = jnp.clip(jax.random.normal(key, (REQUESTS, Q_LEN, QH * HD), jnp.float32), -6.0, 6.0)
    return values.astype(jnp.bfloat16)


def draw_passage_ids(key, part):
    key = jax.random.fold_in(key, 7)
    owners = PASSAGES // PASS_DEV
    subkeys = jax.random.split(key, REQUESTS + 1)
    chosen = jax.vmap(lambda single: jax.random.permutation(single, owners)[:K_SEL])(subkeys[:REQUESTS])
    within = jax.random.randint(subkeys[REQUESTS], (REQUESTS, K_SEL), 0, PASS_DEV)
    return (chosen * PASS_DEV + within).astype(jnp.int32)


def levels(rng, dims, cuts, least, largest):
    def one(axis_at, blocks):
        steps = jax.random.uniform(jax.random.fold_in(jax.random.fold_in(rng, 6), axis_at), (blocks,), jnp.float32, least / len(cuts), largest / len(cuts))
        return jnp.repeat(jnp.exp(steps), dims[axis_at] // blocks).reshape((-1,) + (1,) * (len(dims) - axis_at - 1))

    level = one(*cuts[0])
    for cut in cuts[1:]:
        level = level * one(*cut)
    return level


def bell_draw(own_key, dims, scale, reach, pieces=(), held_as=jnp.bfloat16):
    values = scale * jax.random.normal(own_key, dims, jnp.float32)
    if pieces:
        values = values * levels(own_key, dims, pieces, -0.22, 0.18)
    return jnp.clip(values, -reach, reach).astype(held_as)


def setup_inputs(seed: int = 0) -> dict:
    keys = jax.random.split(jax.random.key(seed), 9)
    return {
        "queries": draw_queries(jax.random.fold_in(keys[8], 71), 0),
        "request_keys": draw_request_keys(jax.random.fold_in(keys[8], 71), 0),
        "request_values": bell_draw(keys[2], (REQUESTS, Q_LEN, KVH * HD), 1.0, 6.0, ((0, 16), (2, 2))),
        "cache_keys": bell_draw(keys[3], (PASSAGES, KVH, PASS_LEN, HD), 1.0, 6.0, ((0, 16), (1, 2))),
        "cache_values": bell_draw(keys[4], (PASSAGES, KVH, PASS_LEN, HD), 1.0, 6.0, ((0, 16), (1, 2))),
        "passage_ids": draw_passage_ids(jax.random.fold_in(keys[8], 71), 0),
        "passage_order": jax.vmap(lambda own: jax.random.permutation(own, K_SEL))(jax.random.split(keys[6], REQUESTS)).reshape((REQUESTS, K_SEL)).astype(jnp.int32),
        "out_weight": bell_draw(keys[7], (QH * HD, D_OUT), (max(1, QH * HD // (K_SEL * PASS_LEN + Q_LEN))) ** -0.5, 6.0, ((0, 32),)),
    }


def frequency_table():
    pair_index = jnp.arange(HD // 2, dtype=jnp.float32)
    return jnp.exp(pair_index * (-2.0 / HD) * jnp.log(jnp.float32(500000.0)))


def reposition(vectors, offset):
    angles = offset.astype(jnp.float32) * frequency_table()
    cosine = jnp.cos(angles)
    sine_term = jnp.sin(angles)
    front_half = vectors[..., : HD // 2]
    back_half = vectors[..., HD // 2:]
    return jnp.concatenate([front_half * cosine - back_half * sine_term, back_half * cosine + front_half * sine_term], axis=-1)


def reference(queries, request_keys, request_values, cache_keys, cache_values, passage_ids, passage_order, out_weight):
    groups = QH // KVH
    context = K_SEL * PASS_LEN

    def one_request(inputs):
        query_block, own_keys, own_values, passage, ranking = inputs
        picked_keys = jnp.take(cache_keys, passage, axis=0).astype(jnp.float32)
        offsets = (ranking * PASS_LEN).astype(jnp.int32)
        placed = lax.optimization_barrier(jax.vmap(reposition)(picked_keys, offsets).astype(jnp.bfloat16))
        picked_values = jnp.take(cache_values, passage, axis=0)
        keys_all = jnp.concatenate([placed.transpose(1, 0, 2, 3).reshape(KVH, context, HD), own_keys.reshape(Q_LEN, KVH, HD).transpose(1, 0, 2)], axis=1)
        values_all = jnp.concatenate([picked_values.transpose(1, 0, 2, 3).reshape(KVH, context, HD), own_values.reshape(Q_LEN, KVH, HD).transpose(1, 0, 2)], axis=1)
        query_rows = query_block.reshape(Q_LEN, KVH, groups, HD).transpose(1, 0, 2, 3).reshape(KVH, Q_LEN * groups, HD)
        scores = jnp.einsum("hrd,hkd->hrk", query_rows.astype(jnp.float32), keys_all.astype(jnp.float32)) * (HD ** -0.5)
        query_token = jnp.arange(Q_LEN * groups) // groups
        column = jnp.arange(context + Q_LEN) - context
        allowed = column[None, :] <= query_token[:, None]
        scores = jnp.where(allowed[None], scores, -jnp.inf)
        row_peak = jnp.max(scores, axis=-1, keepdims=True)
        exponent = jnp.exp(scores - row_peak)
        row_total = jnp.sum(exponent, axis=-1, keepdims=True)
        weights = lax.optimization_barrier(exponent.astype(jnp.bfloat16))
        heads_out = jnp.einsum("hrk,hkd->hrd", weights.astype(jnp.float32), values_all.astype(jnp.float32)) / row_total
        heads_out = heads_out.astype(jnp.bfloat16).reshape(KVH, Q_LEN, groups, HD).transpose(1, 0, 2, 3)
        return heads_out.reshape(Q_LEN, QH * HD)

    attended = lax.map(one_request, (queries, request_keys, request_values, passage_ids, passage_order))
    projected = jnp.dot(attended.reshape(REQUESTS * Q_LEN, QH * HD), out_weight, preferred_element_type=jnp.float32)
    return projected.astype(jnp.bfloat16).reshape(REQUESTS, Q_LEN, D_OUT)
```

```python
import functools
import math

import jax
import jax.numpy as jnp
from jax import lax
from jax.experimental import pallas as pl
from jax.experimental.pallas import tpu as pltpu
from jax.sharding import PartitionSpec as P

CORES = 2
ROWS = 4
LANES = 128
MIB = 1024 * 1024


def frequency_table(head_dim):
    pair_index = jnp.arange(head_dim // 2, dtype=jnp.float32)
    return jnp.exp(pair_index * (-2.0 / head_dim) * jnp.log(jnp.float32(500000.0)))


def reposition(vectors, offset, head_dim):
    angles = offset.astype(jnp.float32) * frequency_table(head_dim)
    cosine = jnp.cos(angles)
    sine_term = jnp.sin(angles)
    front_half = vectors[..., : head_dim // 2]
    back_half = vectors[..., head_dim // 2 :]
    return jnp.concatenate(
        [front_half * cosine - back_half * sine_term, back_half * cosine + front_half * sine_term],
        axis=-1,
    )


def absorb(state, query_rows, keys_block, values_block, allowed):
    running_peak, running_total, running_sum = state
    scores = jnp.einsum(
        "hrd,hnd->hrn", query_rows, keys_block, preferred_element_type=jnp.float32
    ) * query_rows.shape[2] ** (-0.5)
    if allowed is not None:
        scores = jnp.where(allowed[None], scores, -jnp.inf)
    new_peak = jnp.maximum(running_peak, jnp.max(scores, axis=-1))
    factor = jnp.exp(running_peak - new_peak)
    exponent = jnp.exp(scores - new_peak[..., None])
    weights = exponent.astype(jnp.bfloat16)
    new_total = running_total * factor + jnp.sum(exponent, axis=-1)
    new_sum = running_sum * factor[..., None] + jnp.einsum(
        "hrn,hnd->hrd", weights, values_block, preferred_element_type=jnp.float32
    )
    return (new_peak, new_total, new_sum)


def plain_body(
    queries,
    request_keys,
    request_values,
    cache_keys,
    cache_values,
    passage_ids,
    passage_order,
    out_weight,
):
    owned, kv_local, pass_len, head_dim = cache_keys.shape
    query_len = queries.shape[1]
    groups = queries.shape[2] // (kv_local * head_dim)
    row_count = query_len * groups
    query_rows = (
        queries[0]
        .reshape(query_len, kv_local, groups, head_dim)
        .transpose(1, 0, 2, 3)
        .reshape(kv_local, row_count, head_dim)
    )
    own_keys = request_keys[0].reshape(query_len, kv_local, head_dim).transpose(1, 0, 2)
    own_values = request_values[0].reshape(query_len, kv_local, head_dim).transpose(1, 0, 2)
    query_token = jnp.arange(row_count) // groups
    causal = jnp.arange(query_len)[None, :] <= query_token[:, None]
    state = (
        jnp.full((kv_local, row_count), -jnp.inf, jnp.float32),
        jnp.zeros((kv_local, row_count), jnp.float32),
        jnp.zeros((kv_local, row_count, head_dim), jnp.float32),
    )
    state = absorb(state, query_rows, own_keys, own_values, causal)
    slots = passage_ids[0]
    offsets = passage_order[0] * pass_len
    piece_keys = lax.all_gather(cache_keys, "pool", axis=0, tiled=True)
    piece_values = lax.all_gather(cache_values, "pool", axis=0, tiled=True)

    def visit_one(position, current):
        matches = slots == position
        offset = jnp.sum(jnp.where(matches, offsets, 0))

        def absorb_one(inner):
            placed = reposition(piece_keys[position].astype(jnp.float32), offset, head_dim).astype(
                jnp.bfloat16
            )
            return absorb(inner, query_rows, placed, piece_values[position], None)

        return lax.cond(jnp.any(matches), absorb_one, lambda inner: inner, current)

    state = lax.fori_loop(0, piece_keys.shape[0], visit_one, state)
    running_peak, running_total, running_sum = state
    attended = (running_sum / running_total[..., None]).astype(jnp.bfloat16)
    attended = (
        attended.reshape(kv_local, query_len, groups, head_dim)
        .transpose(1, 0, 2, 3)
        .reshape(query_len, kv_local * groups * head_dim)
    )
    partial_value = jnp.dot(
        attended,
        lax.all_gather(out_weight, "pool", axis=0, tiled=True),
        preferred_element_type=jnp.float32,
    )
    summed = lax.psum_scatter(
        partial_value.astype(jnp.bfloat16), "head", scatter_dimension=1, tiled=True
    )
    return summed[None]


def ring_order(chips):
    columns = chips // ROWS
    cells = []
    for row in range(ROWS):
        across = range(1, columns) if row % 2 == 0 else range(columns - 1, 0, -1)
        cells += [row * columns + column for column in across]
    return cells + [row * columns for row in reversed(range(ROWS))]


def shift(value, order, step):
    chips = len(order)
    pairs = [
        (order[at] * CORES + core, order[(at + step) % chips] * CORES + core)
        for at in range(chips)
        for core in range(CORES)
    ]
    return lax.ppermute(value, "pool", pairs)


def swap_core(value, pool):
    return lax.ppermute(value, "pool", [(at, at ^ 1) for at in range(pool)])


def ring_gather(halves, order, after=None):
    chips = len(order)
    pieces = {0: halves}
    ahead, back = halves, halves
    for step in range(1, chips // 2):
        ahead = tuple(shift(half, order, 1) for half in ahead)
        back = tuple(shift(half, order, -1) for half in back)
        pieces[step], pieces[chips - step] = ahead, back
    pieces[chips // 2] = (shift(ahead[0], order, 1), shift(back[1], order, -1))
    return pieces


def attend_kernel(
    pieces,
    owned,
    ids,
    ranks,
    homes,
    own_queries,
    other_queries,
    request_keys,
    request_values,
    cosine,
    sine,
    *refs,
):
    key_pieces, value_pieces = refs[:pieces], refs[pieces : 2 * pieces]
    own_sum, other_sum, own_stats, other_stats = refs[2 * pieces : 2 * pieces + 4]
    keys, values, within, rank_of, key_sem, value_sem = refs[2 * pieces + 4 :]
    slots = ids.shape[1]
    kv_local, _, head_dim = keys.shape[1:]
    length = key_pieces[0].shape[2]
    tokens = own_queries.shape[0]
    groups = own_queries.shape[1] // (kv_local * head_dim)
    factor = math.log2(math.e) / math.sqrt(head_dim)

    for request in range(CORES):
        for slot in range(slots):
            passage = ids[request, slot]
            holder = lax.div(passage, owned)
            within[request, holder] = passage - holder * owned
            rank_of[request, holder] = ranks[request, slot]

    def copies(request, piece):
        at = within[request, homes[piece]]
        rows = pl.ds(piece * length, length)
        return (
            pltpu.make_async_copy(
                key_pieces[piece].at[at], keys.at[request, :, rows], key_sem.at[request, piece]
            ),
            pltpu.make_async_copy(
                value_pieces[piece].at[at], values.at[request, :, rows], value_sem.at[request, piece]
            ),
        )

    for request in range(CORES):
        for piece in range(pieces):
            for copy in copies(request, piece):
                copy.start()

    own_stats[...] = jnp.zeros_like(own_stats)
    other_stats[...] = jnp.zeros_like(other_stats)
    lane = lax.broadcasted_iota(jnp.int32, (tokens, LANES), 1)
    heads = kv_local * groups

    for request in range(CORES):
        queries = own_queries if request == 0 else other_queries
        sums = own_sum if request == 0 else other_sum
        stats = own_stats if request == 0 else other_stats
        for piece in range(pieces):
            key_copy, value_copy = copies(request, piece)
            key_copy.wait()
            value_copy.wait()
            rank = rank_of[request, homes[piece]]
            cos = cosine[pl.ds(rank, 1), :]
            sin = sine[pl.ds(rank, 1), :]
            for head in range(kv_local):
                rows = pl.ds(piece * length, length)
                block = keys[request, head, rows, :].astype(jnp.float32)
                turned = block * cos + pltpu.roll(block, head_dim // 2, 1) * sin
                keys[request, head, rows, :] = turned.astype(jnp.bfloat16)

        @pl.loop(0, kv_local)
        def _(head):
            first = pl.multiple_of(head * groups * head_dim, groups * head_dim)
            rows = jnp.concatenate(
                [queries[:, pl.ds(first + g * head_dim, head_dim)] for g in range(groups)], axis=0
            )
            scores = lax.dot_general(
                rows, keys[request, head], (((1,), (1,)), ((), ())), preferred_element_type=jnp.float32
            )
            peak = jnp.max(scores, axis=1, keepdims=True)
            if request == 0:
                own = pl.ds(pl.multiple_of(head * head_dim, head_dim), head_dim)
                near = lax.dot_general(
                    rows,
                    request_keys[:, own],
                    (((1,), (1,)), ((), ())),
                    preferred_element_type=jnp.float32,
                )
                token = lax.rem(lax.broadcasted_iota(jnp.int32, near.shape, 0), tokens)
                column = lax.broadcasted_iota(jnp.int32, near.shape, 1)
                near = jnp.where(column <= token, near, -jnp.inf)
                peak = jnp.maximum(peak, jnp.max(near, axis=1, keepdims=True))
            exponent = jnp.exp2((scores - peak) * factor)
            total = jnp.sum(exponent, axis=1, keepdims=True)
            summed = jnp.dot(
                exponent.astype(jnp.bfloat16),
                values[request, head],
                preferred_element_type=jnp.float32,
            )
            if request == 0:
                exponent = jnp.exp2((near - peak) * factor)
                total = total + jnp.sum(exponent, axis=1, keepdims=True)
                summed = summed + jnp.dot(
                    exponent.astype(jnp.bfloat16),
                    request_values[:, own],
                    preferred_element_type=jnp.float32,
                )
            for g in range(groups):
                part = slice(g * tokens, (g + 1) * tokens)
                sums[:, pl.ds(first + g * head_dim, head_dim)] = summed[part]
                at = head * groups + g
                held = jnp.where(lane == at, peak[part], stats[...])
                stats[...] = jnp.where(lane == heads + at, total[part], held)


def attend(ids, ranks, homes, queries, own_keys, own_values, cosine, sine, key_pieces, value_pieces):
    pieces = len(key_pieces)
    owned, kv_local, length, head_dim = key_pieces[0].shape
    tokens, features = queries[0].shape
    holders = ids.shape[1]
    smem = pl.BlockSpec(memory_space=pltpu.SMEM)
    vmem = pl.BlockSpec(memory_space=pltpu.VMEM)
    keys_seen = pieces * length
    scores = CORES * tokens * (features // head_dim) * keys_seen
    return pl.pallas_call(
        functools.partial(attend_kernel, pieces, owned),
        out_shape=[jax.ShapeDtypeStruct((tokens, features), jnp.float32)] * 2
        + [jax.ShapeDtypeStruct((tokens, LANES), jnp.float32)] * 2,
        in_specs=[smem] * 3 + [vmem] * 6 + [pl.BlockSpec(memory_space=pl.ANY)] * (2 * pieces),
        out_specs=[vmem] * 4,
        scratch_shapes=[
            pltpu.VMEM((CORES, kv_local, keys_seen, head_dim), jnp.bfloat16),
            pltpu.VMEM((CORES, kv_local, keys_seen, head_dim), jnp.bfloat16),
            pltpu.SMEM((CORES, holders), jnp.int32),
            pltpu.SMEM((CORES, holders), jnp.int32),
            pltpu.SemaphoreType.DMA((CORES, pieces)),
            pltpu.SemaphoreType.DMA((CORES, pieces)),
        ],
        compiler_params=pltpu.CompilerParams(vmem_limit_bytes=40 * MIB),
        cost_estimate=pl.CostEstimate(
            flops=4 * scores * head_dim, bytes_accessed=8 * MIB, transcendentals=scores
        ),
        name="attend",
    )(ids, ranks, homes, *queries, own_keys, own_values, cosine, sine, *key_pieces, *value_pieces)


def combine_kernel(head_dim, sums, stats, sums_in, stats_in, attended):
    heads = sums.shape[1] // head_dim
    factor = math.log2(math.e) / math.sqrt(head_dim)
    for head in range(heads):
        columns = slice(head * head_dim, (head + 1) * head_dim)
        peak_a, peak_b = stats[:, head : head + 1], stats_in[:, head : head + 1]
        at = heads + head
        total_a, total_b = stats[:, at : at + 1], stats_in[:, at : at + 1]
        peak = jnp.maximum(peak_a, peak_b)
        part_a = jnp.exp2((peak_a - peak) * factor)
        part_b = jnp.exp2((peak_b - peak) * factor)
        total = total_a * part_a + total_b * part_b
        value = sums[:, columns] * part_a + sums_in[:, columns] * part_b
        attended[:, columns] = (value / total).astype(attended.dtype)


def combine(head_dim, sums, stats, sums_in, stats_in):
    vmem = pl.BlockSpec(memory_space=pltpu.VMEM)
    return pl.pallas_call(
        functools.partial(combine_kernel, head_dim),
        out_shape=jax.ShapeDtypeStruct(sums.shape, jnp.bfloat16),
        in_specs=[vmem] * 4,
        out_specs=vmem,
        compiler_params=pltpu.CompilerParams(vmem_limit_bytes=24 * MIB),
        cost_estimate=pl.CostEstimate(
            flops=4 * sums.size, bytes_accessed=10 * sums.size, transcendentals=0
        ),
        name="combine",
    )(sums, stats, sums_in, stats_in)


def project_kernel(pieces, groups, start, homes, *refs):
    rows = refs[:groups]
    blocks = refs[groups : groups + 2 * pieces]
    refs = refs[groups + 2 * pieces :]
    base = None
    if start:
        base, refs = refs[0], refs[1:]
    result, own, other, sems = refs[:4]
    total = refs[4] if len(refs) > 4 else result
    span = own.shape[2]

    copies = [
        (
            pltpu.make_async_copy(blocks[2 * at], own.at[at], sems.at[0, at]),
            pltpu.make_async_copy(blocks[2 * at + 1], other.at[at], sems.at[1, at]),
        )
        for at in range(pieces)
    ]
    for pair in copies:
        for copy in pair:
            copy.start()
    for at in range(pieces):
        for copy in copies[at]:
            copy.wait()
        near = pl.ds(pl.multiple_of(homes[2 * at] * span, span), span)
        far = pl.ds(pl.multiple_of(homes[2 * at + 1] * span, span), span)
        value = None
        for group in range(groups):
            left = jnp.concatenate([rows[group][:, near], rows[group][:, far]], axis=1)
            right = jnp.concatenate([own[at, group], other[at, group]], axis=0)
            more = jnp.dot(left, right, preferred_element_type=jnp.float32)
            value = more if value is None else value + more
        if at == 0 and base is not None:
            value = value + base[...]
        elif at > 0:
            value = value + total[...]
        if at == pieces - 1:
            result[...] = value.astype(result.dtype)
        else:
            total[...] = value


def project(homes, rows, pieces, base, dtype):
    groups = len(rows)
    tokens = rows[0].shape[0]
    _, span, width = pieces[0][0].shape
    vmem = pl.BlockSpec(memory_space=pltpu.VMEM)
    count = len(pieces)
    held = pltpu.VMEM((count, groups, span, width), pieces[0][0].dtype)
    extra = [pltpu.VMEM((tokens, width), jnp.float32)] if dtype != jnp.float32 else []
    return pl.pallas_call(
        functools.partial(project_kernel, count, groups, base is not None),
        out_shape=jax.ShapeDtypeStruct((tokens, width), dtype),
        in_specs=[pl.BlockSpec(memory_space=pltpu.SMEM)]
        + [vmem] * groups
        + [pl.BlockSpec(memory_space=pl.ANY)] * (2 * count)
        + ([vmem] if base is not None else []),
        out_specs=vmem,
        scratch_shapes=[held, held, pltpu.SemaphoreType.DMA((2, count))] + extra,
        compiler_params=pltpu.CompilerParams(vmem_limit_bytes=40 * MIB),
        cost_estimate=pl.CostEstimate(
            flops=4 * count * groups * tokens * span * width,
            bytes_accessed=4 * count * groups * span * width + 4 * tokens * width,
            transcendentals=0,
        ),
        name="project",
    )(homes, *rows, *[half for piece in pieces for half in piece], *([base] if base is not None else []))


def rotation_tables(ranks, length, head_dim):
    offsets = (jnp.arange(ranks) * length).astype(jnp.float32)
    angles = offsets[:, None] * frequency_table(head_dim)[None, :]
    cosine, sine = jnp.cos(angles), jnp.sin(angles)
    return (
        jnp.concatenate([cosine, cosine], axis=1),
        jnp.concatenate([-sine, sine], axis=1),
    )


def ring_body(
    pool,
    heads_axis,
    queries,
    request_keys,
    request_values,
    cache_keys,
    cache_values,
    passage_ids,
    passage_order,
    out_weight,
):
    owned, kv_local, pass_len, head_dim = cache_keys.shape
    tokens = queries.shape[1]
    chips = pool // CORES
    order = ring_order(chips)
    me = lax.axis_index("pool")
    plane = lax.axis_index("head")
    core = lax.rem(me, CORES)
    place_of = [order.index(chip) for chip in range(chips)]
    place = jnp.asarray(place_of, jnp.int32)[lax.div(me, CORES)]
    behind = jnp.asarray(order, jnp.int32)[lax.rem(place + chips - jnp.arange(chips), chips)]
    homes = behind * CORES + core
    others = behind * CORES + (1 - core)

    passages = ring_gather((cache_keys, cache_values), order)

    picks = jnp.concatenate([passage_ids, passage_order], axis=0)
    picks_in = swap_core(picks, pool)
    ids = jnp.stack([picks[0], picks_in[0]])
    ranks = jnp.stack([picks[1], picks_in[1]])
    other_queries = swap_core(queries[0], pool)

    width = out_weight.shape[1] // (heads_axis * CORES)

    def columns(to_plane, to_core):
        return lax.dynamic_slice_in_dim(
            out_weight, (to_plane * CORES + to_core) * width, width, axis=1
        )

    def sent_to(step):
        target = lax.rem(plane + step, heads_axis)
        near, far = columns(target, core), columns(target, 1 - core)
        if step:
            pairs = [(at, (at + step) % heads_axis) for at in range(heads_axis)]
            near = lax.ppermute(near, "head", pairs)
            far = lax.ppermute(far, "head", pairs)
        return near, far

    blocks = [sent_to(step) for step in range(heads_axis)]
    near = jnp.stack([pair[0] for pair in blocks])
    far = swap_core(jnp.stack([pair[1] for pair in blocks]), pool)
    middle = passages[chips // 2 - 1] + passages[chips // 2 + 1]
    near, far, *middle = lax.optimization_barrier((near, far) + middle)
    passages[chips // 2 - 1], passages[chips // 2 + 1] = tuple(middle[:2]), tuple(middle[2:])
    weights = ring_gather((near, far), order)

    cosine, sine = rotation_tables(passage_ids.shape[1], pass_len, head_dim)
    own_sum, other_sum, own_stats, other_stats = attend(
        ids,
        ranks,
        homes,
        (queries[0], other_queries),
        request_keys[0],
        request_values[0],
        cosine,
        sine,
        [passages[at][0] for at in range(chips)],
        [passages[at][1] for at in range(chips)],
    )
    attended = combine(
        head_dim, own_sum, own_stats, swap_core(other_sum, pool), swap_core(other_stats, pool)
    )

    rows = []
    for step in range(heads_axis):
        pairs = [(at, (at + step) % heads_axis) for at in range(heads_axis)]
        mine = lax.ppermute(attended, "head", pairs) if step else attended
        rows.append(jnp.concatenate([mine, swap_core(mine, pool)], axis=0))

    def some(total, places, dtype):
        table = jnp.stack(
            [table[at] for at in places for table in (homes, others)]
        )
        return project(table, rows, [weights[at] for at in places], total, dtype)

    half = chips // 2
    early = [0] + [at for step in range(1, half - 1) for at in (step, chips - step)]
    total = some(None, early, jnp.float32)
    total = some(total, [half - 1, half + 1], jnp.float32)
    mixed = some(total, [half], jnp.bfloat16)
    mine, theirs = mixed[:tokens], swap_core(mixed[tokens:], pool)
    result = jnp.where(
        core == 0,
        jnp.concatenate([mine, theirs], axis=1),
        jnp.concatenate([theirs, mine], axis=1),
    )
    return result[None]


def solution(mesh):
    pool, heads_axis = mesh.shape["pool"], mesh.shape["head"]

    def body(*args):
        weight = args[-1]
        tiled = (
            weight.shape[0] % LANES == 0
            and weight.shape[1] % (heads_axis * CORES * LANES) == 0
            and pool % (CORES * ROWS) == 0
        )
        if tiled:
            return ring_body(pool, heads_axis, *args)
        return plain_body(*args)

    placed = (
        P("pool", None, "head"),
        P("pool", None, "head"),
        P("pool", None, "head"),
        P("pool", "head", None, None),
        P("pool", "head", None, None),
        P("pool", None),
        P("pool", None),
        P(("head", "pool"), None),
    )
    return jax.shard_map(
        body, mesh=mesh, in_specs=placed, out_specs=P("pool", None, "head"), check_vma=False
    )
```

```python
import functools
import math

import jax
import jax.numpy as jnp
from jax import lax
from jax.experimental import pallas as pl
from jax.experimental.pallas import tpu as pltpu
from jax.sharding import PartitionSpec as P

CORES = 2
ROWS = 4
LANES = 128
MIB = 1024 * 1024
NEXT_CORE, NEXT_COLUMN, NEXT_ROW, FAR_ROW = 1, 2, 4, 8


def frequency_table(head_dim):
    pair_index = jnp.arange(head_dim // 2, dtype=jnp.float32)
    return jnp.exp(pair_index * (-2.0 / head_dim) * jnp.log(jnp.float32(500000.0)))


def reposition(vectors, offset, head_dim):
    angles = offset.astype(jnp.float32) * frequency_table(head_dim)
    cosine = jnp.cos(angles)
    sine_term = jnp.sin(angles)
    front_half = vectors[..., : head_dim // 2]
    back_half = vectors[..., head_dim // 2 :]
    return jnp.concatenate(
        [front_half * cosine - back_half * sine_term, back_half * cosine + front_half * sine_term],
        axis=-1,
    )


def absorb(state, query_rows, keys_block, values_block, allowed):
    running_peak, running_total, running_sum = state
    scores = jnp.einsum(
        "hrd,hnd->hrn", query_rows, keys_block, preferred_element_type=jnp.float32
    ) * query_rows.shape[2] ** (-0.5)
    if allowed is not None:
        scores = jnp.where(allowed[None], scores, -jnp.inf)
    new_peak = jnp.maximum(running_peak, jnp.max(scores, axis=-1))
    factor = jnp.exp(running_peak - new_peak)
    exponent = jnp.exp(scores - new_peak[..., None])
    weights = exponent.astype(jnp.bfloat16)
    new_total = running_total * factor + jnp.sum(exponent, axis=-1)
    new_sum = running_sum * factor[..., None] + jnp.einsum(
        "hrn,hnd->hrd", weights, values_block, preferred_element_type=jnp.float32
    )
    return (new_peak, new_total, new_sum)


def plain_body(
    queries,
    request_keys,
    request_values,
    cache_keys,
    cache_values,
    passage_ids,
    passage_order,
    out_weight,
):
    owned, kv_local, pass_len, head_dim = cache_keys.shape
    query_len = queries.shape[1]
    groups = queries.shape[2] // (kv_local * head_dim)
    row_count = query_len * groups
    query_rows = (
        queries[0]
        .reshape(query_len, kv_local, groups, head_dim)
        .transpose(1, 0, 2, 3)
        .reshape(kv_local, row_count, head_dim)
    )
    own_keys = request_keys[0].reshape(query_len, kv_local, head_dim).transpose(1, 0, 2)
    own_values = request_values[0].reshape(query_len, kv_local, head_dim).transpose(1, 0, 2)
    query_token = jnp.arange(row_count) // groups
    causal = jnp.arange(query_len)[None, :] <= query_token[:, None]
    state = (
        jnp.full((kv_local, row_count), -jnp.inf, jnp.float32),
        jnp.zeros((kv_local, row_count), jnp.float32),
        jnp.zeros((kv_local, row_count, head_dim), jnp.float32),
    )
    state = absorb(state, query_rows, own_keys, own_values, causal)
    slots = passage_ids[0]
    offsets = passage_order[0] * pass_len
    piece_keys = lax.all_gather(cache_keys, "pool", axis=0, tiled=True)
    piece_values = lax.all_gather(cache_values, "pool", axis=0, tiled=True)

    def visit_one(position, current):
        matches = slots == position
        offset = jnp.sum(jnp.where(matches, offsets, 0))

        def absorb_one(inner):
            placed = reposition(piece_keys[position].astype(jnp.float32), offset, head_dim).astype(
                jnp.bfloat16
            )
            return absorb(inner, query_rows, placed, piece_values[position], None)

        return lax.cond(jnp.any(matches), absorb_one, lambda inner: inner, current)

    state = lax.fori_loop(0, piece_keys.shape[0], visit_one, state)
    running_peak, running_total, running_sum = state
    attended = (running_sum / running_total[..., None]).astype(jnp.bfloat16)
    attended = (
        attended.reshape(kv_local, query_len, groups, head_dim)
        .transpose(1, 0, 2, 3)
        .reshape(query_len, kv_local * groups * head_dim)
    )
    partial_value = jnp.dot(
        attended,
        lax.all_gather(out_weight, "pool", axis=0, tiled=True),
        preferred_element_type=jnp.float32,
    )
    summed = lax.psum_scatter(
        partial_value.astype(jnp.bfloat16), "head", scatter_dimension=1, tiled=True
    )
    return summed[None]


def ring_order(chips):
    columns = chips // ROWS
    cells = []
    for row in range(ROWS):
        across = range(1, columns) if row % 2 == 0 else range(columns - 1, 0, -1)
        cells += [row * columns + column for column in across]
    return cells + [row * columns for row in reversed(range(ROWS))]


def shift(value, order, step):
    chips = len(order)
    pairs = [
        (order[at] * CORES + core, order[(at + step) % chips] * CORES + core)
        for at in range(chips)
        for core in range(CORES)
    ]
    return lax.ppermute(value, "pool", pairs)


def flip(value, pool, mask):
    return lax.ppermute(value, "pool", [(at, at ^ mask) for at in range(pool)])


def flip_plane(value):
    return lax.ppermute(value, "head", [(0, 1), (1, 0)])


def ring_gather(halves, order):
    chips = len(order)
    pieces = {0: halves}
    ahead, back = halves, halves
    for step in range(1, chips // 2):
        ahead = tuple(shift(half, order, 1) for half in ahead)
        back = tuple(shift(half, order, -1) for half in back)
        pieces[step], pieces[chips - step] = ahead, back
    pieces[chips // 2] = (shift(ahead[0], order, 1), shift(back[1], order, -1))
    return pieces


def attend_kernel(places, owned, first, ids, ranks, homes, own_queries, other_queries, *refs):
    pieces = len(places)
    if first:
        request_keys, request_values = refs[:2]
        states = (None, None)
        refs = refs[2:]
    else:
        states = ((refs[0], refs[2]), (refs[1], refs[3]))
        refs = refs[4:]
    cosine, sine = refs[:2]
    key_pieces, value_pieces = refs[2 : 2 + pieces], refs[2 + pieces : 2 + 2 * pieces]
    refs = refs[2 + 2 * pieces :]
    results = ((refs[0], refs[2]), (refs[1], refs[3]))
    keys, values, within, rank_of, key_sem, value_sem = refs[4:]
    slots = ids.shape[1]
    kv_local, _, head_dim = keys.shape[1:]
    length = key_pieces[0].shape[2]
    tokens = own_queries.shape[0]
    groups = own_queries.shape[1] // (kv_local * head_dim)
    heads = kv_local * groups
    factor = math.log2(math.e) / math.sqrt(head_dim)
    across = (((1,), (1,)), ((), ()))

    for request in range(CORES):
        for slot in range(slots):
            passage = ids[request, slot]
            holder = lax.div(passage, owned)
            within[request, holder] = passage - holder * owned
            rank_of[request, holder] = ranks[request, slot]

    def copies(request, piece):
        at = within[request, homes[places[piece]]]
        rows = pl.ds(piece * length, length)
        return (
            pltpu.make_async_copy(
                key_pieces[piece].at[at], keys.at[request, :, rows], key_sem.at[request, piece]
            ),
            pltpu.make_async_copy(
                value_pieces[piece].at[at], values.at[request, :, rows], value_sem.at[request, piece]
            ),
        )

    for request in range(CORES):
        for piece in range(pieces):
            for copy in copies(request, piece):
                copy.start()

    lane = lax.broadcasted_iota(jnp.int32, (tokens, LANES), 1)
    for request in range(CORES):
        queries = own_queries if request == 0 else other_queries
        sums, stats = results[request]
        state = states[request]
        near_block = first and request == 0
        for piece in range(pieces):
            for copy in copies(request, piece):
                copy.wait()
            rank = rank_of[request, homes[places[piece]]]
            cos = cosine[pl.ds(rank, 1), :]
            sin = sine[pl.ds(rank, 1), :]
            rows = pl.ds(piece * length, length)
            for head in range(kv_local):
                block = keys[request, head, rows, :].astype(jnp.float32)
                turned = block * cos + pltpu.roll(block, head_dim // 2, 1) * sin
                keys[request, head, rows, :] = turned.astype(jnp.bfloat16)

        marks = jnp.zeros((tokens, LANES), jnp.float32)
        for head in range(kv_local):
            spans = [
                slice((head * groups + g) * head_dim, (head * groups + g + 1) * head_dim)
                for g in range(groups)
            ]
            rows = jnp.concatenate([queries[:, span] for span in spans], axis=0)
            scores = lax.dot_general(
                rows, keys[request, head], across, preferred_element_type=jnp.float32
            )
            peak = jnp.max(scores, axis=1, keepdims=True)
            if near_block:
                own = slice(head * head_dim, (head + 1) * head_dim)
                near = lax.dot_general(
                    rows, request_keys[:, own], across, preferred_element_type=jnp.float32
                )
                token = lax.rem(lax.broadcasted_iota(jnp.int32, near.shape, 0), tokens)
                column = lax.broadcasted_iota(jnp.int32, near.shape, 1)
                near = jnp.where(column <= token, near, -jnp.inf)
                peak = jnp.maximum(peak, jnp.max(near, axis=1, keepdims=True))
            if state is not None:
                at = head * groups
                last = jnp.concatenate(
                    [state[1][:, at + g : at + g + 1] for g in range(groups)], axis=0
                )
                at = heads + head * groups
                last_total = jnp.concatenate(
                    [state[1][:, at + g : at + g + 1] for g in range(groups)], axis=0
                )
                peak = jnp.maximum(peak, last)
                fade = jnp.exp2((last - peak) * factor)
            exponent = jnp.exp2((scores - peak) * factor)
            total = jnp.sum(exponent, axis=1, keepdims=True)
            summed = jnp.dot(
                exponent.astype(jnp.bfloat16),
                values[request, head],
                preferred_element_type=jnp.float32,
            )
            if near_block:
                exponent = jnp.exp2((near - peak) * factor)
                total = total + jnp.sum(exponent, axis=1, keepdims=True)
                summed = summed + jnp.dot(
                    exponent.astype(jnp.bfloat16),
                    request_values[:, own],
                    preferred_element_type=jnp.float32,
                )
            if state is not None:
                total = total + last_total * fade
                summed = summed + fade * jnp.concatenate(
                    [state[0][:, span] for span in spans], axis=0
                )
            for g in range(groups):
                part = slice(g * tokens, (g + 1) * tokens)
                sums[:, spans[g]] = summed[part]
                at = head * groups + g
                marks = jnp.where(lane == at, peak[part], marks)
                marks = jnp.where(lane == heads + at, total[part], marks)
        stats[...] = marks


def attend(ids, ranks, homes, queries, tables, near, state, places, passages):
    pieces = len(places)
    key_pieces = [passages[at][0] for at in places]
    value_pieces = [passages[at][1] for at in places]
    owned, kv_local, length, head_dim = key_pieces[0].shape
    tokens, features = queries[0].shape
    holders = ids.shape[1]
    smem = pl.BlockSpec(memory_space=pltpu.SMEM)
    vmem = pl.BlockSpec(memory_space=pltpu.VMEM)
    seen = pieces * length
    scores = CORES * tokens * (features // head_dim) * seen
    held = state if near is None else near
    return pl.pallas_call(
        functools.partial(attend_kernel, tuple(places), owned, near is not None),
        out_shape=[jax.ShapeDtypeStruct((tokens, features), jnp.float32)] * 2
        + [jax.ShapeDtypeStruct((tokens, LANES), jnp.float32)] * 2,
        in_specs=[smem] * 3
        + [vmem] * (4 + len(held))
        + [pl.BlockSpec(memory_space=pl.ANY)] * (2 * pieces),
        out_specs=[vmem] * 4,
        scratch_shapes=[
            pltpu.VMEM((CORES, kv_local, seen, head_dim), jnp.bfloat16),
            pltpu.VMEM((CORES, kv_local, seen, head_dim), jnp.bfloat16),
            pltpu.SMEM((CORES, holders), jnp.int32),
            pltpu.SMEM((CORES, holders), jnp.int32),
            pltpu.SemaphoreType.DMA((CORES, pieces)),
            pltpu.SemaphoreType.DMA((CORES, pieces)),
        ],
        compiler_params=pltpu.CompilerParams(vmem_limit_bytes=32 * MIB),
        cost_estimate=pl.CostEstimate(
            flops=4 * scores * head_dim, bytes_accessed=8 * MIB, transcendentals=scores
        ),
        name="attend",
    )(ids, ranks, homes, *queries, *held, *tables, *key_pieces, *value_pieces)


def combine_kernel(head_dim, sums, stats, sums_in, stats_in, attended):
    heads = sums.shape[1] // head_dim
    factor = math.log2(math.e) / math.sqrt(head_dim)
    for head in range(heads):
        columns = slice(head * head_dim, (head + 1) * head_dim)
        peak_a, peak_b = stats[:, head : head + 1], stats_in[:, head : head + 1]
        at = heads + head
        total_a, total_b = stats[:, at : at + 1], stats_in[:, at : at + 1]
        peak = jnp.maximum(peak_a, peak_b)
        part_a = jnp.exp2((peak_a - peak) * factor)
        part_b = jnp.exp2((peak_b - peak) * factor)
        total = total_a * part_a + total_b * part_b
        value = sums[:, columns] * part_a + sums_in[:, columns] * part_b
        attended[:, columns] = (value / total).astype(attended.dtype)


def combine(head_dim, sums, stats, sums_in, stats_in):
    vmem = pl.BlockSpec(memory_space=pltpu.VMEM)
    return pl.pallas_call(
        functools.partial(combine_kernel, head_dim),
        out_shape=jax.ShapeDtypeStruct(sums.shape, jnp.bfloat16),
        in_specs=[vmem] * 4,
        out_specs=vmem,
        compiler_params=pltpu.CompilerParams(vmem_limit_bytes=24 * MIB),
        cost_estimate=pl.CostEstimate(
            flops=4 * sums.size, bytes_accessed=10 * sums.size, transcendentals=0
        ),
        name="combine",
    )(sums, stats, sums_in, stats_in)


def project_kernel(masks, based, me, own_rows, other_rows, *refs):
    blocks, refs = refs[: len(masks)], refs[len(masks) :]
    base = None
    if based:
        base, refs = refs[0], refs[1:]
    results, (held, total, sems) = refs[:-3], refs[-3:]
    span = held.shape[2]
    copies = [
        pltpu.make_async_copy(block, held.at[at], sems.at[at]) for at, block in enumerate(blocks)
    ]
    for copy in copies:
        copy.start()
    for at in range(0, len(masks), 2):
        left, right = [], []
        for part in (at, at + 1):
            copies[part].wait()
            first = pl.multiple_of(lax.bitwise_xor(me[0], masks[part]) * span, span)
            for plane, rows in enumerate((own_rows, other_rows)):
                left.append(rows[:, pl.ds(first, span)])
                right.append(held[part, plane])
        value = jnp.dot(
            jnp.concatenate(left, axis=1),
            jnp.concatenate(right, axis=0),
            preferred_element_type=jnp.float32,
        )
        if at:
            value = value + total[...]
        elif base is not None:
            value = value + base[...]
        if at + 2 < len(masks):
            total[...] = value
            continue
        tokens = results[0].shape[0]
        for part, result in enumerate(results):
            result[...] = value[part * tokens : (part + 1) * tokens].astype(result.dtype)


def project(me, rows, blocks, base, shapes):
    masks = tuple(blocks)
    tokens = rows[0].shape[0]
    planes, span, width = blocks[masks[0]].shape
    vmem = pl.BlockSpec(memory_space=pltpu.VMEM)
    return pl.pallas_call(
        functools.partial(project_kernel, masks, base is not None),
        out_shape=shapes,
        in_specs=[pl.BlockSpec(memory_space=pltpu.SMEM)]
        + [vmem] * 2
        + [pl.BlockSpec(memory_space=pl.ANY)] * len(masks)
        + ([vmem] if base is not None else []),
        out_specs=[vmem] * len(shapes),
        scratch_shapes=[
            pltpu.VMEM((len(masks), planes, span, width), jnp.bfloat16),
            pltpu.VMEM((tokens, width), jnp.float32),
            pltpu.SemaphoreType.DMA((len(masks),)),
        ],
        compiler_params=pltpu.CompilerParams(vmem_limit_bytes=32 * MIB),
        cost_estimate=pl.CostEstimate(
            flops=2 * len(masks) * planes * tokens * span * width,
            bytes_accessed=2 * len(masks) * planes * span * width + 4 * tokens * width,
            transcendentals=0,
        ),
        name="project",
    )(me, *rows, *blocks.values(), *([base] if base is not None else []))


def rotation_tables(ranks, length, head_dim):
    offsets = (jnp.arange(ranks) * length).astype(jnp.float32)
    angles = offsets[:, None] * frequency_table(head_dim)[None, :]
    cosine, sine = jnp.cos(angles), jnp.sin(angles)
    return (
        jnp.concatenate([cosine, cosine], axis=1),
        jnp.concatenate([-sine, sine], axis=1),
    )


def ring_body(
    pool,
    queries,
    request_keys,
    request_values,
    cache_keys,
    cache_values,
    passage_ids,
    passage_order,
    out_weight,
):
    owned, kv_local, pass_len, head_dim = cache_keys.shape
    tokens = queries.shape[1]
    chips = pool // CORES
    half = chips // 2
    order = ring_order(chips)
    me = lax.axis_index("pool")
    plane = lax.axis_index("head")
    core = lax.rem(me, CORES)
    odd = lax.rem(lax.div(me, NEXT_ROW), 2)
    place_of = [order.index(chip) for chip in range(chips)]
    place = jnp.asarray(place_of, jnp.int32)[lax.div(me, CORES)]
    behind = jnp.asarray(order, jnp.int32)[lax.rem(place + chips - jnp.arange(chips), chips)]
    homes = behind * CORES + core

    passages = ring_gather((cache_keys, cache_values), order)

    picks = jnp.concatenate([passage_ids, passage_order], axis=0)
    picks_in = flip(picks, pool, NEXT_CORE)
    ids = jnp.stack([picks[0], picks_in[0]])
    ranks = jnp.stack([picks[1], picks_in[1]])
    other_queries = flip(queries[0], pool, NEXT_CORE)

    span = out_weight.shape[1] // 2
    width = span // 4
    mine = lax.dynamic_slice_in_dim(out_weight, plane * span, span, axis=1)
    across = flip_plane(lax.dynamic_slice_in_dim(out_weight, (1 - plane) * span, span, axis=1))

    def columns(mask):
        at = lax.bitwise_xor(odd * 2 + core, mask) * width
        return jnp.stack(
            [lax.dynamic_slice_in_dim(value, at, width, axis=1) for value in (mine, across)]
        )

    blocks = {0: columns(0), NEXT_CORE: flip(columns(1), pool, NEXT_CORE)}
    later = {NEXT_ROW: columns(2), NEXT_ROW ^ NEXT_CORE: columns(3)}
    gate = (passages[half - 1], passages[half + 1])
    blocks, later, gate = lax.optimization_barrier((blocks, later, gate))
    passages[half - 1], passages[half + 1] = gate
    blocks.update({mask: flip(value, pool, mask) for mask, value in later.items()})
    early = dict(blocks)
    early.update({mask ^ NEXT_COLUMN: flip(blocks[mask], pool, NEXT_COLUMN) for mask in blocks})
    far = {mask ^ FAR_ROW: flip(blocks[mask], pool, FAR_ROW) for mask in blocks}
    last = {mask ^ NEXT_COLUMN: flip(far[mask], pool, NEXT_COLUMN) for mask in far}

    tables = rotation_tables(passage_ids.shape[1], pass_len, head_dim)
    both = (queries[0], other_queries)
    near = (request_keys[0], request_values[0])
    state = None
    for step in range(1, half + 1):
        places = {1: [0, 1, chips - 1], half: [half]}.get(step, [step, chips - step])
        state = attend(ids, ranks, homes, both, tables, near, state, places, passages)
        near = None
    own_sum, other_sum, own_stats, other_stats = state
    attended = combine(
        head_dim,
        own_sum,
        own_stats,
        flip(other_sum, pool, NEXT_CORE),
        flip(other_stats, pool, NEXT_CORE),
    )

    beyond = flip(attended, pool, NEXT_ROW)
    rows = []
    for pair in ((attended, beyond), (flip_plane(attended), flip_plane(beyond))):
        parts = [part for value in pair for part in (value, flip(value, pool, NEXT_CORE))]
        rows.append(jnp.concatenate(parts, axis=0))

    where = jnp.reshape(me, (1,))
    total = [jax.ShapeDtypeStruct((4 * tokens, width), jnp.float32)]
    masks = list(last)
    sums = project(where, rows, early, None, total)[0]
    middle = far | {mask: last[mask] for mask in masks[:2]}
    sums = project(where, rows, middle, sums, total)[0]
    final = {mask: last[mask] for mask in masks[2:]}
    out = project(
        where, rows, final, sums, [jax.ShapeDtypeStruct((tokens, width), jnp.bfloat16)] * 4
    )
    parts = [
        flip(value, pool, mask) if mask else value
        for value, mask in zip(out, (0, NEXT_CORE, NEXT_ROW, NEXT_ROW ^ NEXT_CORE))
    ]
    even_core = core == 0
    low = jnp.where(
        even_core, jnp.concatenate(parts[:2], axis=1), jnp.concatenate(parts[1::-1], axis=1)
    )
    high = jnp.where(
        even_core, jnp.concatenate(parts[2:], axis=1), jnp.concatenate(parts[:1:-1], axis=1)
    )
    result = jnp.where(
        odd == 0, jnp.concatenate([low, high], axis=1), jnp.concatenate([high, low], axis=1)
    )
    return result[None]


def solution(mesh):
    pool, heads_axis = mesh.shape["pool"], mesh.shape["head"]

    def body(*args):
        weight = args[-1]
        tiled = weight.shape[0] % LANES == 0 and weight.shape[1] % (8 * LANES) == 0
        if tiled and heads_axis == 2 and pool == 2 * ROWS * CORES:
            return ring_body(pool, *args)
        return plain_body(*args)

    placed = (
        P("pool", None, "head"),
        P("pool", None, "head"),
        P("pool", None, "head"),
        P("pool", "head", None, None),
        P("pool", "head", None, None),
        P("pool", None),
        P("pool", None),
        P(("head", "pool"), None),
    )
    return jax.shard_map(
        body, mesh=mesh, in_specs=placed, out_specs=P("pool", None, "head"), check_vma=False
    )
```

```python
import functools
import math

import jax
import jax.numpy as jnp
from jax import lax
from jax.experimental import pallas as pl
from jax.experimental.pallas import tpu as pltpu
from jax.sharding import PartitionSpec as P

CORES = 2
ROWS = 4
LANES = 128
MIB = 1024 * 1024
NEXT_CORE, NEXT_COLUMN, NEXT_ROW, FAR_ROW = 1, 2, 4, 8


def frequency_table(head_dim):
    pair_index = jnp.arange(head_dim // 2, dtype=jnp.float32)
    return jnp.exp(pair_index * (-2.0 / head_dim) * jnp.log(jnp.float32(500000.0)))


def reposition(vectors, offset, head_dim):
    angles = offset.astype(jnp.float32) * frequency_table(head_dim)
    cosine = jnp.cos(angles)
    sine_term = jnp.sin(angles)
    front_half = vectors[..., : head_dim // 2]
    back_half = vectors[..., head_dim // 2 :]
    return jnp.concatenate(
        [front_half * cosine - back_half * sine_term, back_half * cosine + front_half * sine_term],
        axis=-1,
    )


def absorb(state, query_rows, keys_block, values_block, allowed):
    running_peak, running_total, running_sum = state
    scores = jnp.einsum(
        "hrd,hnd->hrn", query_rows, keys_block, preferred_element_type=jnp.float32
    ) * query_rows.shape[2] ** (-0.5)
    if allowed is not None:
        scores = jnp.where(allowed[None], scores, -jnp.inf)
    new_peak = jnp.maximum(running_peak, jnp.max(scores, axis=-1))
    factor = jnp.exp(running_peak - new_peak)
    exponent = jnp.exp(scores - new_peak[..., None])
    weights = exponent.astype(jnp.bfloat16)
    new_total = running_total * factor + jnp.sum(exponent, axis=-1)
    new_sum = running_sum * factor[..., None] + jnp.einsum(
        "hrn,hnd->hrd", weights, values_block, preferred_element_type=jnp.float32
    )
    return (new_peak, new_total, new_sum)


def plain_body(
    queries,
    request_keys,
    request_values,
    cache_keys,
    cache_values,
    passage_ids,
    passage_order,
    out_weight,
):
    owned, kv_local, pass_len, head_dim = cache_keys.shape
    query_len = queries.shape[1]
    groups = queries.shape[2] // (kv_local * head_dim)
    row_count = query_len * groups
    query_rows = (
        queries[0]
        .reshape(query_len, kv_local, groups, head_dim)
        .transpose(1, 0, 2, 3)
        .reshape(kv_local, row_count, head_dim)
    )
    own_keys = request_keys[0].reshape(query_len, kv_local, head_dim).transpose(1, 0, 2)
    own_values = request_values[0].reshape(query_len, kv_local, head_dim).transpose(1, 0, 2)
    query_token = jnp.arange(row_count) // groups
    causal = jnp.arange(query_len)[None, :] <= query_token[:, None]
    state = (
        jnp.full((kv_local, row_count), -jnp.inf, jnp.float32),
        jnp.zeros((kv_local, row_count), jnp.float32),
        jnp.zeros((kv_local, row_count, head_dim), jnp.float32),
    )
    state = absorb(state, query_rows, own_keys, own_values, causal)
    slots = passage_ids[0]
    offsets = passage_order[0] * pass_len
    piece_keys = lax.all_gather(cache_keys, "pool", axis=0, tiled=True)
    piece_values = lax.all_gather(cache_values, "pool", axis=0, tiled=True)

    def visit_one(position, current):
        matches = slots == position
        offset = jnp.sum(jnp.where(matches, offsets, 0))

        def absorb_one(inner):
            placed = reposition(piece_keys[position].astype(jnp.float32), offset, head_dim).astype(
                jnp.bfloat16
            )
            return absorb(inner, query_rows, placed, piece_values[position], None)

        return lax.cond(jnp.any(matches), absorb_one, lambda inner: inner, current)

    state = lax.fori_loop(0, piece_keys.shape[0], visit_one, state)
    running_peak, running_total, running_sum = state
    attended = (running_sum / running_total[..., None]).astype(jnp.bfloat16)
    attended = (
        attended.reshape(kv_local, query_len, groups, head_dim)
        .transpose(1, 0, 2, 3)
        .reshape(query_len, kv_local * groups * head_dim)
    )
    partial_value = jnp.dot(
        attended,
        lax.all_gather(out_weight, "pool", axis=0, tiled=True),
        preferred_element_type=jnp.float32,
    )
    summed = lax.psum_scatter(
        partial_value.astype(jnp.bfloat16), "head", scatter_dimension=1, tiled=True
    )
    return summed[None]


def ring_order(chips):
    columns = chips // ROWS
    cells = []
    for row in range(ROWS):
        across = range(1, columns) if row % 2 == 0 else range(columns - 1, 0, -1)
        cells += [row * columns + column for column in across]
    return cells + [row * columns for row in reversed(range(ROWS))]


def shift(value, order, step):
    chips = len(order)
    pairs = [
        (order[at] * CORES + core, order[(at + step) % chips] * CORES + core)
        for at in range(chips)
        for core in range(CORES)
    ]
    return lax.ppermute(value, "pool", pairs)


def flip(value, pool, mask):
    return lax.ppermute(value, "pool", [(at, at ^ mask) for at in range(pool)])


def flip_plane(value):
    return lax.ppermute(value, "head", [(0, 1), (1, 0)])


def ring_gather(halves, order):
    chips = len(order)
    pieces = {0: halves}
    ahead, back = halves, halves
    for step in range(1, chips // 2):
        ahead = tuple(shift(half, order, 1) for half in ahead)
        back = tuple(shift(half, order, -1) for half in back)
        pieces[step], pieces[chips - step] = ahead, back
    pieces[chips // 2] = (shift(ahead[0], order, 1), shift(back[1], order, -1))
    return pieces


def attend_kernel(pieces, owned, ids, ranks, homes, queries, cosine, sine, *refs):
    key_pieces, value_pieces, refs = refs[:pieces], refs[pieces : 2 * pieces], refs[2 * pieces :]
    near = refs[:-8]
    sums, stats, keys, values, within, rank_of, key_sem, value_sem = refs[-8:]
    slots = ids.shape[0]
    kv_local, _, head_dim = keys.shape
    length = key_pieces[0].shape[2]
    tokens = queries.shape[0]
    groups = queries.shape[1] // (kv_local * head_dim)
    heads = kv_local * groups
    factor = math.log2(math.e) / math.sqrt(head_dim)
    across = (((1,), (1,)), ((), ()))

    for slot in range(slots):
        passage = ids[slot]
        holder = lax.div(passage, owned)
        within[holder] = passage - holder * owned
        rank_of[holder] = ranks[slot]

    def copy(source, target, sem, piece):
        rows = pl.ds(piece * length, length)
        return pltpu.make_async_copy(
            source[piece].at[within[homes[piece]]], target.at[:, rows], sem.at[piece]
        )

    key_copies = [copy(key_pieces, keys, key_sem, piece) for piece in range(pieces)]
    value_copies = [copy(value_pieces, values, value_sem, piece) for piece in range(pieces)]
    for each in key_copies + value_copies:
        each.start()
    for piece in range(pieces):
        key_copies[piece].wait()
        rank = rank_of[homes[piece]]
        cos = cosine[pl.ds(rank, 1), :]
        sin = sine[pl.ds(rank, 1), :]
        rows = pl.ds(piece * length, length)
        for head in range(kv_local):
            block = keys[head, rows, :].astype(jnp.float32)
            turned = block * cos + pltpu.roll(block, head_dim // 2, 1) * sin
            keys[head, rows, :] = turned.astype(jnp.bfloat16)
    for each in value_copies:
        each.wait()

    lane = lax.broadcasted_iota(jnp.int32, (tokens, LANES), 1)
    marks = jnp.zeros((tokens, LANES), jnp.float32)
    for head in range(kv_local):
        spans = [
            slice((head * groups + g) * head_dim, (head * groups + g + 1) * head_dim)
            for g in range(groups)
        ]
        rows = jnp.concatenate([queries[:, span] for span in spans], axis=0)
        scores = lax.dot_general(rows, keys[head], across, preferred_element_type=jnp.float32)
        peak = jnp.max(scores, axis=1, keepdims=True)
        if near:
            own = slice(head * head_dim, (head + 1) * head_dim)
            close = lax.dot_general(
                rows, near[0][:, own], across, preferred_element_type=jnp.float32
            )
            token = lax.rem(lax.broadcasted_iota(jnp.int32, close.shape, 0), tokens)
            column = lax.broadcasted_iota(jnp.int32, close.shape, 1)
            close = jnp.where(column <= token, close, -jnp.inf)
            peak = jnp.maximum(peak, jnp.max(close, axis=1, keepdims=True))
        exponent = jnp.exp2((scores - peak) * factor)
        total = jnp.sum(exponent, axis=1, keepdims=True)
        summed = jnp.dot(
            exponent.astype(jnp.bfloat16), values[head], preferred_element_type=jnp.float32
        )
        if near:
            exponent = jnp.exp2((close - peak) * factor)
            total = total + jnp.sum(exponent, axis=1, keepdims=True)
            summed = summed + jnp.dot(
                exponent.astype(jnp.bfloat16), near[1][:, own], preferred_element_type=jnp.float32
            )
        for g in range(groups):
            part = slice(g * tokens, (g + 1) * tokens)
            sums[:, spans[g]] = summed[part]
            at = head * groups + g
            marks = jnp.where(lane == at, peak[part], marks)
            marks = jnp.where(lane == heads + at, total[part], marks)
    stats[...] = marks


def attend(ids, ranks, homes, queries, tables, near, passages):
    pieces = len(passages)
    key_pieces = [passages[at][0] for at in range(pieces)]
    value_pieces = [passages[at][1] for at in range(pieces)]
    owned, kv_local, length, head_dim = key_pieces[0].shape
    tokens, features = queries.shape
    holders = ids.shape[0]
    smem = pl.BlockSpec(memory_space=pltpu.SMEM)
    vmem = pl.BlockSpec(memory_space=pltpu.VMEM)
    seen = pieces * length
    scores = tokens * (features // head_dim) * (seen + (length if near else 0))
    return pl.pallas_call(
        functools.partial(attend_kernel, pieces, owned),
        out_shape=[
            jax.ShapeDtypeStruct((tokens, features), jnp.float32),
            jax.ShapeDtypeStruct((tokens, LANES), jnp.float32),
        ],
        in_specs=[smem] * 3
        + [vmem] * 3
        + [pl.BlockSpec(memory_space=pl.ANY)] * (2 * pieces)
        + [vmem] * len(near),
        out_specs=[vmem] * 2,
        scratch_shapes=[
            pltpu.VMEM((kv_local, seen, head_dim), jnp.bfloat16),
            pltpu.VMEM((kv_local, seen, head_dim), jnp.bfloat16),
            pltpu.SMEM((holders,), jnp.int32),
            pltpu.SMEM((holders,), jnp.int32),
            pltpu.SemaphoreType.DMA((pieces,)),
            pltpu.SemaphoreType.DMA((pieces,)),
        ],
        compiler_params=pltpu.CompilerParams(vmem_limit_bytes=32 * MIB),
        cost_estimate=pl.CostEstimate(
            flops=4 * scores * head_dim, bytes_accessed=4 * MIB, transcendentals=scores
        ),
        name="attend",
    )(ids, ranks, homes, queries, *tables, *key_pieces, *value_pieces, *near)


def combine_kernel(head_dim, sums, stats, sums_in, stats_in, *attended):
    heads = sums.shape[1] // head_dim
    factor = math.log2(math.e) / math.sqrt(head_dim)
    for head in range(heads):
        columns = slice(head * head_dim, (head + 1) * head_dim)
        peak_a, peak_b = stats[:, head : head + 1], stats_in[:, head : head + 1]
        at = heads + head
        total_a, total_b = stats[:, at : at + 1], stats_in[:, at : at + 1]
        peak = jnp.maximum(peak_a, peak_b)
        part_a = jnp.exp2((peak_a - peak) * factor)
        part_b = jnp.exp2((peak_b - peak) * factor)
        total = total_a * part_a + total_b * part_b
        value = sums[:, columns] * part_a + sums_in[:, columns] * part_b
        part, at = divmod(head * len(attended), heads)
        at = at // len(attended) * head_dim
        attended[part][:, at : at + head_dim] = (value / total).astype(jnp.bfloat16)


def combine(head_dim, sums, stats, sums_in, stats_in):
    vmem = pl.BlockSpec(memory_space=pltpu.VMEM)
    return pl.pallas_call(
        functools.partial(combine_kernel, head_dim),
        out_shape=[jax.ShapeDtypeStruct((sums.shape[0], sums.shape[1] // 2), jnp.bfloat16)] * 2,
        in_specs=[vmem] * 4,
        out_specs=[vmem] * 2,
        compiler_params=pltpu.CompilerParams(vmem_limit_bytes=24 * MIB),
        cost_estimate=pl.CostEstimate(
            flops=4 * sums.size, bytes_accessed=10 * sums.size, transcendentals=0
        ),
        name="combine",
    )(sums, stats, sums_in, stats_in)


def project_kernel(masks, based, me, own_rows, other_rows, *refs):
    blocks, refs = refs[: len(masks)], refs[len(masks) :]
    base = None
    if based:
        base, refs = refs[0], refs[1:]
    results, (held, total, sems) = refs[:-3], refs[-3:]
    span = held.shape[2]
    copies = [
        pltpu.make_async_copy(block, held.at[at], sems.at[at]) for at, block in enumerate(blocks)
    ]
    for copy in copies:
        copy.start()
    for at in range(0, len(masks), 2):
        left, right = [], []
        for part in (at, at + 1):
            copies[part].wait()
            first = pl.multiple_of(lax.bitwise_xor(me[0], masks[part]) * span, span)
            for plane, rows in enumerate((own_rows, other_rows)):
                left.append(rows[:, pl.ds(first, span)])
                right.append(held[part, plane])
        value = jnp.dot(
            jnp.concatenate(left, axis=1),
            jnp.concatenate(right, axis=0),
            preferred_element_type=jnp.float32,
        )
        if at:
            value = value + total[...]
        elif base is not None:
            value = value + base[...]
        if at + 2 < len(masks):
            total[...] = value
            continue
        tokens = results[0].shape[0]
        for part, result in enumerate(results):
            result[...] = value[part * tokens : (part + 1) * tokens].astype(result.dtype)


def project(me, rows, blocks, base, shapes):
    masks = tuple(blocks)
    tokens = rows[0].shape[0]
    planes, span, width = blocks[masks[0]].shape
    vmem = pl.BlockSpec(memory_space=pltpu.VMEM)
    return pl.pallas_call(
        functools.partial(project_kernel, masks, base is not None),
        out_shape=shapes,
        in_specs=[pl.BlockSpec(memory_space=pltpu.SMEM)]
        + [vmem] * 2
        + [pl.BlockSpec(memory_space=pl.ANY)] * len(masks)
        + ([vmem] if base is not None else []),
        out_specs=[vmem] * len(shapes),
        scratch_shapes=[
            pltpu.VMEM((len(masks), planes, span, width), jnp.bfloat16),
            pltpu.VMEM((tokens, width), jnp.float32),
            pltpu.SemaphoreType.DMA((len(masks),)),
        ],
        compiler_params=pltpu.CompilerParams(vmem_limit_bytes=32 * MIB),
        cost_estimate=pl.CostEstimate(
            flops=2 * len(masks) * planes * tokens * span * width,
            bytes_accessed=2 * len(masks) * planes * span * width + 4 * tokens * width,
            transcendentals=0,
        ),
        name="project",
    )(me, *rows, *blocks.values(), *([base] if base is not None else []))


def rotation_tables(ranks, length, head_dim):
    offsets = (jnp.arange(ranks) * length).astype(jnp.float32)
    angles = offsets[:, None] * frequency_table(head_dim)[None, :]
    cosine, sine = jnp.cos(angles), jnp.sin(angles)
    return (
        jnp.concatenate([cosine, cosine], axis=1),
        jnp.concatenate([-sine, sine], axis=1),
    )


def ring_body(
    pool,
    queries,
    request_keys,
    request_values,
    cache_keys,
    cache_values,
    passage_ids,
    passage_order,
    out_weight,
):
    owned, kv_local, pass_len, head_dim = cache_keys.shape
    tokens = queries.shape[1]
    chips = pool // CORES
    half = chips // 2
    order = ring_order(chips)
    me = lax.axis_index("pool")
    plane = lax.axis_index("head")
    core = lax.rem(me, CORES)
    odd = lax.rem(lax.div(me, NEXT_ROW), 2)
    place_of = [order.index(chip) for chip in range(chips)]
    place = jnp.asarray(place_of, jnp.int32)[lax.div(me, CORES)]
    behind = jnp.asarray(order, jnp.int32)[lax.rem(place + chips - jnp.arange(chips), chips)]
    homes = behind * CORES + core

    passages = ring_gather((cache_keys, cache_values), order)
    first = (passages[1][0], passages[chips - 1][0])
    first, queries, picks, out_weight = lax.optimization_barrier(
        (first, queries[0], jnp.concatenate([passage_ids, passage_order], axis=0), out_weight)
    )
    passages[1] = (first[0], passages[1][1])
    passages[chips - 1] = (first[1], passages[chips - 1][1])

    picks_in = flip(picks, pool, NEXT_CORE)
    other_queries = flip(queries, pool, NEXT_CORE)

    span = out_weight.shape[1] // 2
    width = span // 4
    mine = lax.dynamic_slice_in_dim(out_weight, plane * span, span, axis=1)
    across = flip_plane(lax.dynamic_slice_in_dim(out_weight, (1 - plane) * span, span, axis=1))

    def columns(mask):
        at = lax.bitwise_xor(odd * 2 + core, mask) * width
        return jnp.stack(
            [lax.dynamic_slice_in_dim(value, at, width, axis=1) for value in (mine, across)]
        )

    masks = (0, NEXT_CORE, NEXT_ROW, NEXT_ROW ^ NEXT_CORE)
    blocks = [columns(0), flip(columns(1), pool, NEXT_CORE), columns(2), columns(3)]
    gate = (passages[half - 1], passages[half + 1])
    blocks, gate = lax.optimization_barrier((blocks, gate))
    passages[half - 1], passages[half + 1] = gate

    def far(at):
        return flip(blocks[at], pool, FAR_ROW)

    def beside(value):
        return flip(value, pool, NEXT_COLUMN)

    tables = rotation_tables(passage_ids.shape[1], pass_len, head_dim)
    far_blocks, side_blocks, last_blocks = [far(0)], [beside(blocks[0])], []
    blocks[2] = flip(blocks[2], pool, NEXT_ROW)
    other = attend(picks_in[0], picks_in[1], homes, other_queries, tables, (), passages)
    other, queries, blocks, far_blocks, side_blocks = lax.optimization_barrier(
        (other, queries, blocks, far_blocks, side_blocks)
    )

    far_blocks.append(far(1))
    side_blocks.append(beside(blocks[1]))
    last_blocks.append(beside(far_blocks[0]))
    blocks[3] = flip(blocks[3], pool, NEXT_ROW ^ NEXT_CORE)
    other_in = [flip(value, pool, NEXT_CORE) for value in other]
    near = (request_keys[0], request_values[0])
    own = attend(picks[0], picks[1], homes, queries, tables, near, passages)
    own, blocks, far_blocks, side_blocks, last_blocks = lax.optimization_barrier(
        (own, blocks, far_blocks, side_blocks, last_blocks)
    )

    attended = combine(head_dim, *own, *other_in)
    far_blocks.append(far(2))
    side_blocks.append(beside(blocks[2]))
    last_blocks.append(beside(far_blocks[1]))
    beyond = [flip(value, pool, NEXT_ROW) for value in attended]
    across = [flip_plane(value) for value in attended]
    beyond[0], blocks, far_blocks, side_blocks, last_blocks = lax.optimization_barrier(
        (beyond[0], blocks, far_blocks, side_blocks, last_blocks)
    )

    far_blocks.append(far(3))
    side_blocks.append(beside(blocks[3]))
    last_blocks.append(beside(far_blocks[2]))
    corner = [flip_plane(beyond[0])]
    beyond[1], far_blocks, side_blocks, last_blocks = lax.optimization_barrier(
        (beyond[1], far_blocks, side_blocks, last_blocks)
    )
    last_blocks.append(beside(far_blocks[3]))
    corner.append(flip_plane(beyond[1]))

    rows = []
    for near_part, far_part in ((attended, beyond), (across, corner)):
        parts = [jnp.concatenate(part, axis=1) for part in (near_part, far_part)]
        parts = [part for value in parts for part in (value, flip(value, pool, NEXT_CORE))]
        rows.append(jnp.concatenate(parts, axis=0))

    where = jnp.reshape(me, (1,))
    total = [jax.ShapeDtypeStruct((4 * tokens, width), jnp.float32)]
    def sources(values, mask):
        return {mask ^ masks[at]: value for at, value in values}

    chunks = list(enumerate(blocks)), list(enumerate(side_blocks))
    early = sources(chunks[0], 0) | sources(chunks[1], NEXT_COLUMN)
    sums = project(where, rows, early, None, total)[0]
    chunks = list(enumerate(far_blocks)), list(enumerate(last_blocks))
    middle = sources(chunks[0], FAR_ROW) | sources(chunks[1][:2], FAR_ROW ^ NEXT_COLUMN)
    sums = project(where, rows, middle, sums, total)[0]
    final = sources(chunks[1][2:], FAR_ROW ^ NEXT_COLUMN)
    out = project(
        where, rows, final, sums, [jax.ShapeDtypeStruct((tokens, width), jnp.bfloat16)] * 4
    )
    parts = [
        flip(value, pool, mask) if mask else value
        for value, mask in zip(out, masks)
    ]
    even_core = core == 0
    low = jnp.where(
        even_core, jnp.concatenate(parts[:2], axis=1), jnp.concatenate(parts[1::-1], axis=1)
    )
    high = jnp.where(
        even_core, jnp.concatenate(parts[2:], axis=1), jnp.concatenate(parts[:1:-1], axis=1)
    )
    result = jnp.where(
        odd == 0, jnp.concatenate([low, high], axis=1), jnp.concatenate([high, low], axis=1)
    )
    return result[None]


def solution(mesh):
    pool, heads_axis = mesh.shape["pool"], mesh.shape["head"]

    def body(*args):
        weight = args[-1]
        tiled = weight.shape[0] % LANES == 0 and weight.shape[1] % (8 * LANES) == 0
        if tiled and heads_axis == 2 and pool == 2 * ROWS * CORES:
            return ring_body(pool, *args)
        return plain_body(*args)

    placed = (
        P("pool", None, "head"),
        P("pool", None, "head"),
        P("pool", None, "head"),
        P("pool", "head", None, None),
        P("pool", "head", None, None),
        P("pool", None),
        P("pool", None),
        P(("head", "pool"), None),
    )
    return jax.shard_map(
        body, mesh=mesh, in_specs=placed, out_specs=P("pool", None, "head"), check_vma=False
    )
```

```python
import functools
import math

import jax
import jax.numpy as jnp
from jax import lax
from jax.experimental import pallas as pl
from jax.experimental.pallas import tpu as pltpu
from jax.sharding import PartitionSpec as P

CORES = 2
ROWS = 4
LANES = 128
MIB = 1024 * 1024
NEXT_CORE, NEXT_COLUMN, NEXT_ROW = 1, 2, 4


def frequency_table(head_dim):
    pair_index = jnp.arange(head_dim // 2, dtype=jnp.float32)
    return jnp.exp(pair_index * (-2.0 / head_dim) * jnp.log(jnp.float32(500000.0)))


def reposition(vectors, offset, head_dim):
    angles = offset.astype(jnp.float32) * frequency_table(head_dim)
    cosine = jnp.cos(angles)
    sine_term = jnp.sin(angles)
    front_half = vectors[..., : head_dim // 2]
    back_half = vectors[..., head_dim // 2 :]
    return jnp.concatenate(
        [front_half * cosine - back_half * sine_term, back_half * cosine + front_half * sine_term],
        axis=-1,
    )


def absorb(state, query_rows, keys_block, values_block, allowed):
    running_peak, running_total, running_sum = state
    scores = jnp.einsum(
        "hrd,hnd->hrn", query_rows, keys_block, preferred_element_type=jnp.float32
    ) * query_rows.shape[2] ** (-0.5)
    if allowed is not None:
        scores = jnp.where(allowed[None], scores, -jnp.inf)
    new_peak = jnp.maximum(running_peak, jnp.max(scores, axis=-1))
    factor = jnp.exp(running_peak - new_peak)
    exponent = jnp.exp(scores - new_peak[..., None])
    weights = exponent.astype(jnp.bfloat16)
    new_total = running_total * factor + jnp.sum(exponent, axis=-1)
    new_sum = running_sum * factor[..., None] + jnp.einsum(
        "hrn,hnd->hrd", weights, values_block, preferred_element_type=jnp.float32
    )
    return (new_peak, new_total, new_sum)


def plain_body(
    queries,
    request_keys,
    request_values,
    cache_keys,
    cache_values,
    passage_ids,
    passage_order,
    out_weight,
):
    owned, kv_local, pass_len, head_dim = cache_keys.shape
    query_len = queries.shape[1]
    groups = queries.shape[2] // (kv_local * head_dim)
    row_count = query_len * groups
    query_rows = (
        queries[0]
        .reshape(query_len, kv_local, groups, head_dim)
        .transpose(1, 0, 2, 3)
        .reshape(kv_local, row_count, head_dim)
    )
    own_keys = request_keys[0].reshape(query_len, kv_local, head_dim).transpose(1, 0, 2)
    own_values = request_values[0].reshape(query_len, kv_local, head_dim).transpose(1, 0, 2)
    query_token = jnp.arange(row_count) // groups
    causal = jnp.arange(query_len)[None, :] <= query_token[:, None]
    state = (
        jnp.full((kv_local, row_count), -jnp.inf, jnp.float32),
        jnp.zeros((kv_local, row_count), jnp.float32),
        jnp.zeros((kv_local, row_count, head_dim), jnp.float32),
    )
    state = absorb(state, query_rows, own_keys, own_values, causal)
    slots = passage_ids[0]
    offsets = passage_order[0] * pass_len
    piece_keys = lax.all_gather(cache_keys, "pool", axis=0, tiled=True)
    piece_values = lax.all_gather(cache_values, "pool", axis=0, tiled=True)

    def visit_one(position, current):
        matches = slots == position
        offset = jnp.sum(jnp.where(matches, offsets, 0))

        def absorb_one(inner):
            placed = reposition(piece_keys[position].astype(jnp.float32), offset, head_dim).astype(
                jnp.bfloat16
            )
            return absorb(inner, query_rows, placed, piece_values[position], None)

        return lax.cond(jnp.any(matches), absorb_one, lambda inner: inner, current)

    state = lax.fori_loop(0, piece_keys.shape[0], visit_one, state)
    running_peak, running_total, running_sum = state
    attended = (running_sum / running_total[..., None]).astype(jnp.bfloat16)
    attended = (
        attended.reshape(kv_local, query_len, groups, head_dim)
        .transpose(1, 0, 2, 3)
        .reshape(query_len, kv_local * groups * head_dim)
    )
    partial_value = jnp.dot(
        attended,
        lax.all_gather(out_weight, "pool", axis=0, tiled=True),
        preferred_element_type=jnp.float32,
    )
    summed = lax.psum_scatter(
        partial_value.astype(jnp.bfloat16), "head", scatter_dimension=1, tiled=True
    )
    return summed[None]


def ring_order(chips):
    columns = chips // ROWS
    cells = []
    for row in range(ROWS):
        across = range(1, columns) if row % 2 == 0 else range(columns - 1, 0, -1)
        cells += [row * columns + column for column in across]
    return cells + [row * columns for row in reversed(range(ROWS))]


def shift(value, order, step):
    chips = len(order)
    pairs = [
        (order[at] * CORES + core, order[(at + step) % chips] * CORES + core)
        for at in range(chips)
        for core in range(CORES)
    ]
    return lax.ppermute(value, "pool", pairs)


def flip(value, pool, mask):
    return lax.ppermute(value, "pool", [(at, at ^ mask) for at in range(pool)])


def along(value, pool, step, reach):
    wide = pool // ROWS
    pairs = []
    for row in range(ROWS):
        if 0 <= row - reach * step < ROWS:
            pairs += [((row - step) * wide + at, row * wide + at) for at in range(wide)]
    return lax.ppermute(value, "pool", pairs)


def flip_plane(value):
    return lax.ppermute(value, "head", [(0, 1), (1, 0)])


def ring_gather(halves, order):
    chips = len(order)
    pieces = {0: halves}
    ahead, back = halves, halves
    for step in range(1, chips // 2):
        ahead = tuple(shift(half, order, 1) for half in ahead)
        back = tuple(shift(half, order, -1) for half in back)
        pieces[step], pieces[chips - step] = ahead, back
    pieces[chips // 2] = (shift(ahead[0], order, 1), shift(back[1], order, -1))
    return pieces


def attend_kernel(pieces, owned, ids, ranks, homes, queries, cosine, sine, *refs):
    key_pieces, value_pieces, refs = refs[:pieces], refs[pieces : 2 * pieces], refs[2 * pieces :]
    near = refs[:-8]
    sums, stats, keys, values, within, rank_of, key_sem, value_sem = refs[-8:]
    slots = ids.shape[0]
    kv_local, _, head_dim = keys.shape
    length = key_pieces[0].shape[2]
    tokens = queries.shape[0]
    groups = queries.shape[1] // (kv_local * head_dim)
    heads = kv_local * groups
    factor = math.log2(math.e) / math.sqrt(head_dim)
    across = (((1,), (1,)), ((), ()))

    for slot in range(slots):
        passage = ids[slot]
        holder = lax.div(passage, owned)
        within[holder] = passage - holder * owned
        rank_of[holder] = ranks[slot]

    def copy(source, target, sem, piece):
        rows = pl.ds(piece * length, length)
        return pltpu.make_async_copy(
            source[piece].at[within[homes[piece]]], target.at[:, rows], sem.at[piece]
        )

    key_copies = [copy(key_pieces, keys, key_sem, piece) for piece in range(pieces)]
    value_copies = [copy(value_pieces, values, value_sem, piece) for piece in range(pieces)]
    for each in key_copies + value_copies:
        each.start()
    for piece in range(pieces):
        key_copies[piece].wait()
        rank = rank_of[homes[piece]]
        cos = cosine[pl.ds(rank, 1), :]
        sin = sine[pl.ds(rank, 1), :]
        rows = pl.ds(piece * length, length)
        for head in range(kv_local):
            block = keys[head, rows, :].astype(jnp.float32)
            turned = block * cos + pltpu.roll(block, head_dim // 2, 1) * sin
            keys[head, rows, :] = turned.astype(jnp.bfloat16)
    for each in value_copies:
        each.wait()

    lane = lax.broadcasted_iota(jnp.int32, (tokens, LANES), 1)
    marks = jnp.zeros((tokens, LANES), jnp.float32)
    for head in range(kv_local):
        spans = [
            slice((head * groups + g) * head_dim, (head * groups + g + 1) * head_dim)
            for g in range(groups)
        ]
        rows = jnp.concatenate([queries[:, span] for span in spans], axis=0)
        scores = lax.dot_general(rows, keys[head], across, preferred_element_type=jnp.float32)
        peak = jnp.max(scores, axis=1, keepdims=True)
        if near:
            own = slice(head * head_dim, (head + 1) * head_dim)
            close = lax.dot_general(
                rows, near[0][:, own], across, preferred_element_type=jnp.float32
            )
            token = lax.rem(lax.broadcasted_iota(jnp.int32, close.shape, 0), tokens)
            column = lax.broadcasted_iota(jnp.int32, close.shape, 1)
            close = jnp.where(column <= token, close, -jnp.inf)
            peak = jnp.maximum(peak, jnp.max(close, axis=1, keepdims=True))
        exponent = jnp.exp2((scores - peak) * factor)
        total = jnp.sum(exponent, axis=1, keepdims=True)
        summed = jnp.dot(
            exponent.astype(jnp.bfloat16), values[head], preferred_element_type=jnp.float32
        )
        if near:
            exponent = jnp.exp2((close - peak) * factor)
            total = total + jnp.sum(exponent, axis=1, keepdims=True)
            summed = summed + jnp.dot(
                exponent.astype(jnp.bfloat16), near[1][:, own], preferred_element_type=jnp.float32
            )
        for g in range(groups):
            part = slice(g * tokens, (g + 1) * tokens)
            sums[:, spans[g]] = summed[part]
            at = head * groups + g
            marks = jnp.where(lane == at, peak[part], marks)
            marks = jnp.where(lane == heads + at, total[part], marks)
    stats[...] = marks


def attend(ids, ranks, homes, queries, tables, near, passages):
    pieces = len(passages)
    key_pieces = [passages[at][0] for at in range(pieces)]
    value_pieces = [passages[at][1] for at in range(pieces)]
    owned, kv_local, length, head_dim = key_pieces[0].shape
    tokens, features = queries.shape
    holders = ids.shape[0]
    smem = pl.BlockSpec(memory_space=pltpu.SMEM)
    vmem = pl.BlockSpec(memory_space=pltpu.VMEM)
    seen = pieces * length
    scores = tokens * (features // head_dim) * (seen + (length if near else 0))
    return pl.pallas_call(
        functools.partial(attend_kernel, pieces, owned),
        out_shape=[
            jax.ShapeDtypeStruct((tokens, features), jnp.float32),
            jax.ShapeDtypeStruct((tokens, LANES), jnp.float32),
        ],
        in_specs=[smem] * 3
        + [vmem] * 3
        + [pl.BlockSpec(memory_space=pl.ANY)] * (2 * pieces)
        + [vmem] * len(near),
        out_specs=[vmem] * 2,
        scratch_shapes=[
            pltpu.VMEM((kv_local, seen, head_dim), jnp.bfloat16),
            pltpu.VMEM((kv_local, seen, head_dim), jnp.bfloat16),
            pltpu.SMEM((holders,), jnp.int32),
            pltpu.SMEM((holders,), jnp.int32),
            pltpu.SemaphoreType.DMA((pieces,)),
            pltpu.SemaphoreType.DMA((pieces,)),
        ],
        compiler_params=pltpu.CompilerParams(vmem_limit_bytes=32 * MIB),
        cost_estimate=pl.CostEstimate(
            flops=4 * scores * head_dim, bytes_accessed=4 * MIB, transcendentals=scores
        ),
        name="attend",
    )(ids, ranks, homes, queries, *tables, *key_pieces, *value_pieces, *near)


def combine_kernel(head_dim, sums, stats, sums_in, stats_in, *attended):
    heads = sums.shape[1] // head_dim
    factor = math.log2(math.e) / math.sqrt(head_dim)
    for head in range(heads):
        columns = slice(head * head_dim, (head + 1) * head_dim)
        peak_a, peak_b = stats[:, head : head + 1], stats_in[:, head : head + 1]
        at = heads + head
        total_a, total_b = stats[:, at : at + 1], stats_in[:, at : at + 1]
        peak = jnp.maximum(peak_a, peak_b)
        part_a = jnp.exp2((peak_a - peak) * factor)
        part_b = jnp.exp2((peak_b - peak) * factor)
        total = total_a * part_a + total_b * part_b
        value = sums[:, columns] * part_a + sums_in[:, columns] * part_b
        part, at = divmod(head * len(attended), heads)
        at = at // len(attended) * head_dim
        attended[part][:, at : at + head_dim] = (value / total).astype(jnp.bfloat16)


def combine(head_dim, sums, stats, sums_in, stats_in):
    vmem = pl.BlockSpec(memory_space=pltpu.VMEM)
    return pl.pallas_call(
        functools.partial(combine_kernel, head_dim),
        out_shape=[jax.ShapeDtypeStruct((sums.shape[0], sums.shape[1] // 2), jnp.bfloat16)] * 2,
        in_specs=[vmem] * 4,
        out_specs=[vmem] * 2,
        compiler_params=pltpu.CompilerParams(vmem_limit_bytes=24 * MIB),
        cost_estimate=pl.CostEstimate(
            flops=4 * sums.size, bytes_accessed=10 * sums.size, transcendentals=0
        ),
        name="combine",
    )(sums, stats, sums_in, stats_in)


def project_kernel(sources, based, place, own_rows, other_rows, *refs):
    blocks, refs = refs[: len(sources)], refs[len(sources) :]
    base = None
    if based:
        base, refs = refs[0], refs[1:]
    results, (held, total, sems) = refs[:-3], refs[-3:]
    row, inside = place[0], place[1]
    members, planes, span, _ = held.shape[1:]

    def here(step):
        return jnp.logical_and(row + step >= 0, row + step < ROWS)

    copies = [
        pltpu.make_async_copy(block, held.at[at], sems.at[at]) for at, block in enumerate(blocks)
    ]
    for step, copy in zip(sources, copies):
        pl.when(here(step))(copy.start)
    total[...] = jnp.zeros_like(total) if base is None else base[...]
    for at, step in enumerate(sources):

        @pl.when(here(step))
        def _():
            copies[at].wait()
            left, right = [], []
            for mask in range(members):
                holder = (row + step) * members + lax.bitwise_xor(inside, mask)
                first = pl.multiple_of(holder * span, span)
                for plane, rows in enumerate((own_rows, other_rows)):
                    left.append(rows[:, pl.ds(first, span)])
                    right.append(held[at, mask, plane])
            total[...] += jnp.dot(
                jnp.concatenate(left, axis=1),
                jnp.concatenate(right, axis=0),
                preferred_element_type=jnp.float32,
            )

    tokens = results[0].shape[0]
    for part, result in enumerate(results):
        result[...] = total[part * tokens : (part + 1) * tokens].astype(result.dtype)


def project(place, rows, blocks, base, shapes):
    sources = tuple(blocks)
    tokens = rows[0].shape[0]
    members, planes, span, width = blocks[sources[0]].shape
    vmem = pl.BlockSpec(memory_space=pltpu.VMEM)
    count = len(sources)
    return pl.pallas_call(
        functools.partial(project_kernel, sources, base is not None),
        out_shape=shapes,
        in_specs=[pl.BlockSpec(memory_space=pltpu.SMEM)]
        + [vmem] * 2
        + [pl.BlockSpec(memory_space=pl.ANY)] * count
        + ([vmem] if base is not None else []),
        out_specs=[vmem] * len(shapes),
        scratch_shapes=[
            pltpu.VMEM((count, members, planes, span, width), jnp.bfloat16),
            pltpu.VMEM((tokens, width), jnp.float32),
            pltpu.SemaphoreType.DMA((count,)),
        ],
        compiler_params=pltpu.CompilerParams(vmem_limit_bytes=32 * MIB),
        cost_estimate=pl.CostEstimate(
            flops=2 * count * members * planes * tokens * span * width,
            bytes_accessed=2 * count * members * planes * span * width + 4 * tokens * width,
            transcendentals=0,
        ),
        name="project",
    )(place, *rows, *blocks.values(), *([base] if base is not None else []))


def rotation_tables(ranks, length, head_dim):
    offsets = (jnp.arange(ranks) * length).astype(jnp.float32)
    angles = offsets[:, None] * frequency_table(head_dim)[None, :]
    cosine, sine = jnp.cos(angles), jnp.sin(angles)
    return (
        jnp.concatenate([cosine, cosine], axis=1),
        jnp.concatenate([-sine, sine], axis=1),
    )


def ring_body(
    pool,
    queries,
    request_keys,
    request_values,
    cache_keys,
    cache_values,
    passage_ids,
    passage_order,
    out_weight,
):
    owned, kv_local, pass_len, head_dim = cache_keys.shape
    tokens = queries.shape[1]
    chips = pool // CORES
    half = chips // 2
    order = ring_order(chips)
    me = lax.axis_index("pool")
    plane = lax.axis_index("head")
    core = lax.rem(me, CORES)
    inside = lax.rem(me, NEXT_ROW)
    place_of = [order.index(chip) for chip in range(chips)]
    place = jnp.asarray(place_of, jnp.int32)[lax.div(me, CORES)]
    behind = jnp.asarray(order, jnp.int32)[lax.rem(place + chips - jnp.arange(chips), chips)]
    homes = behind * CORES + core

    passages = ring_gather((cache_keys, cache_values), order)
    first = (passages[1][1], passages[chips - 1][1])
    first, queries, picks, out_weight = lax.optimization_barrier(
        (first, queries[0], jnp.concatenate([passage_ids, passage_order], axis=0), out_weight)
    )
    passages[1] = (passages[1][0], first[0])
    passages[chips - 1] = (passages[chips - 1][0], first[1])

    picks_in = flip(picks, pool, NEXT_CORE)
    other_queries = flip(queries, pool, NEXT_CORE)

    span = out_weight.shape[1] // 2
    width = span // NEXT_ROW
    mine = lax.dynamic_slice_in_dim(out_weight, plane * span, span, axis=1)
    across = flip_plane(lax.dynamic_slice_in_dim(out_weight, (1 - plane) * span, span, axis=1))

    def columns(mask):
        at = lax.bitwise_xor(inside, mask) * width
        return jnp.stack(
            [lax.dynamic_slice_in_dim(value, at, width, axis=1) for value in (mine, across)]
        )

    masks = range(NEXT_ROW)
    blocks = [flip(columns(mask), pool, mask) if mask else columns(mask) for mask in masks]
    lines = []
    for half_at in range(2):
        cut = slice(half_at * width // 2, (half_at + 1) * width // 2)
        lines.append({0: jnp.stack([block[:, :, cut] for block in blocks])})

    def travel(line, reach):
        line[-reach] = along(line[1 - reach], pool, 1, reach)
        line[reach] = along(line[reach - 1], pool, -1, reach)

    tables = rotation_tables(passage_ids.shape[1], pass_len, head_dim)
    for line in lines:
        travel(line, 1)
    other = attend(picks_in[0], picks_in[1], homes, other_queries, tables, (), passages)
    other, queries, lines = lax.optimization_barrier((other, queries, lines))

    for line in lines:
        travel(line, 2)
    other_in = [flip(value, pool, NEXT_CORE) for value in other]
    near = (request_keys[0], request_values[0])
    own = attend(picks[0], picks[1], homes, queries, tables, near, passages)
    own, lines[0] = lax.optimization_barrier((own, lines[0]))

    attended = combine(head_dim, *own, *other_in)
    beside = [flip(part, pool, NEXT_COLUMN) for part in attended]
    across = [flip_plane(part) for part in attended]
    across, lines[1] = lax.optimization_barrier((across, lines[1]))
    travel(lines[0], 3)
    corner = [flip(part, pool, NEXT_COLUMN) for part in across]
    corner, lines[0] = lax.optimization_barrier((corner, lines[0]))
    travel(lines[1], 3)
    rows = []
    for pair in ((attended, beside), (across, corner)):
        pair = [jnp.concatenate(value, axis=1) for value in pair]
        four = [part for value in pair for part in (value, flip(value, pool, NEXT_CORE))]
        rows.append(jnp.concatenate(four, axis=0))

    where = jnp.stack([lax.div(me, NEXT_ROW), inside])
    total = [jax.ShapeDtypeStruct((NEXT_ROW * tokens, width // 2), jnp.float32)]
    block = [jax.ShapeDtypeStruct((tokens, width // 2), jnp.bfloat16)] * NEXT_ROW
    sums = [
        project(where, rows, {step: line[step] for step in (0, -1, 1, -2, 2)}, None, total)[0]
        for line in lines
    ]
    parts = []
    for line, value in zip(lines, sums):
        out = project(where, rows, {step: line[step] for step in (-3, 3)}, value, block)
        parts.append([flip(out[mask], pool, mask) if mask else out[mask] for mask in masks])
    parts = [jnp.concatenate(pair, axis=1) for pair in zip(*parts)]
    even = lax.rem(inside, 2) == 0
    low = jnp.where(
        even, jnp.concatenate(parts[:2], axis=1), jnp.concatenate(parts[1::-1], axis=1)
    )
    high = jnp.where(
        even, jnp.concatenate(parts[2:], axis=1), jnp.concatenate(parts[:1:-1], axis=1)
    )
    result = jnp.where(
        inside < 2, jnp.concatenate([low, high], axis=1), jnp.concatenate([high, low], axis=1)
    )
    return result[None]


def solution(mesh):
    pool, heads_axis = mesh.shape["pool"], mesh.shape["head"]

    def body(*args):
        weight = args[-1]
        tiled = weight.shape[0] % LANES == 0 and weight.shape[1] % (8 * LANES) == 0
        if tiled and heads_axis == 2 and pool == 2 * ROWS * CORES:
            return ring_body(pool, *args)
        return plain_body(*args)

    placed = (
        P("pool", None, "head"),
        P("pool", None, "head"),
        P("pool", None, "head"),
        P("pool", "head", None, None),
        P("pool", "head", None, None),
        P("pool", None),
        P("pool", None),
        P(("head", "pool"), None),
    )
    return jax.shard_map(
        body, mesh=mesh, in_specs=placed, out_specs=P("pool", None, "head"), check_vma=False
    )
```

```python
import functools
import math

import jax
import jax.numpy as jnp
from jax import lax
from jax.experimental import pallas as pl
from jax.experimental.pallas import tpu as pltpu
from jax.sharding import PartitionSpec as P

CORES = 2
ROWS = 4
LANES = 128
MIB = 1024 * 1024


def frequency_table(head_dim):
    pair_index = jnp.arange(head_dim // 2, dtype=jnp.float32)
    return jnp.exp(pair_index * (-2.0 / head_dim) * jnp.log(jnp.float32(500000.0)))


def reposition(vectors, offset, head_dim):
    angles = offset.astype(jnp.float32) * frequency_table(head_dim)
    cosine = jnp.cos(angles)
    sine_term = jnp.sin(angles)
    front_half = vectors[..., : head_dim // 2]
    back_half = vectors[..., head_dim // 2 :]
    return jnp.concatenate(
        [front_half * cosine - back_half * sine_term, back_half * cosine + front_half * sine_term],
        axis=-1,
    )


def absorb(state, query_rows, keys_block, values_block, allowed):
    running_peak, running_total, running_sum = state
    scores = jnp.einsum(
        "hrd,hnd->hrn", query_rows, keys_block, preferred_element_type=jnp.float32
    ) * query_rows.shape[2] ** (-0.5)
    if allowed is not None:
        scores = jnp.where(allowed[None], scores, -jnp.inf)
    new_peak = jnp.maximum(running_peak, jnp.max(scores, axis=-1))
    factor = jnp.exp(running_peak - new_peak)
    exponent = jnp.exp(scores - new_peak[..., None])
    weights = exponent.astype(jnp.bfloat16)
    new_total = running_total * factor + jnp.sum(exponent, axis=-1)
    new_sum = running_sum * factor[..., None] + jnp.einsum(
        "hrn,hnd->hrd", weights, values_block, preferred_element_type=jnp.float32
    )
    return (new_peak, new_total, new_sum)


def plain_body(
    queries,
    request_keys,
    request_values,
    cache_keys,
    cache_values,
    passage_ids,
    passage_order,
    out_weight,
):
    owned, kv_local, pass_len, head_dim = cache_keys.shape
    query_len = queries.shape[1]
    groups = queries.shape[2] // (kv_local * head_dim)
    row_count = query_len * groups
    query_rows = (
        queries[0]
        .reshape(query_len, kv_local, groups, head_dim)
        .transpose(1, 0, 2, 3)
        .reshape(kv_local, row_count, head_dim)
    )
    own_keys = request_keys[0].reshape(query_len, kv_local, head_dim).transpose(1, 0, 2)
    own_values = request_values[0].reshape(query_len, kv_local, head_dim).transpose(1, 0, 2)
    query_token = jnp.arange(row_count) // groups
    causal = jnp.arange(query_len)[None, :] <= query_token[:, None]
    state = (
        jnp.full((kv_local, row_count), -jnp.inf, jnp.float32),
        jnp.zeros((kv_local, row_count), jnp.float32),
        jnp.zeros((kv_local, row_count, head_dim), jnp.float32),
    )
    state = absorb(state, query_rows, own_keys, own_values, causal)
    slots = passage_ids[0]
    offsets = passage_order[0] * pass_len
    piece_keys = lax.all_gather(cache_keys, "pool", axis=0, tiled=True)
    piece_values = lax.all_gather(cache_values, "pool", axis=0, tiled=True)

    def visit_one(position, current):
        matches = slots == position
        offset = jnp.sum(jnp.where(matches, offsets, 0))

        def absorb_one(inner):
            placed = reposition(piece_keys[position].astype(jnp.float32), offset, head_dim).astype(
                jnp.bfloat16
            )
            return absorb(inner, query_rows, placed, piece_values[position], None)

        return lax.cond(jnp.any(matches), absorb_one, lambda inner: inner, current)

    state = lax.fori_loop(0, piece_keys.shape[0], visit_one, state)
    running_peak, running_total, running_sum = state
    attended = (running_sum / running_total[..., None]).astype(jnp.bfloat16)
    attended = (
        attended.reshape(kv_local, query_len, groups, head_dim)
        .transpose(1, 0, 2, 3)
        .reshape(query_len, kv_local * groups * head_dim)
    )
    partial_value = jnp.dot(
        attended,
        lax.all_gather(out_weight, "pool", axis=0, tiled=True),
        preferred_element_type=jnp.float32,
    )
    summed = lax.psum_scatter(
        partial_value.astype(jnp.bfloat16), "head", scatter_dimension=1, tiled=True
    )
    return summed[None]


def ring_order(chips):
    columns = chips // ROWS
    cells = []
    for row in range(ROWS):
        across = range(1, columns) if row % 2 == 0 else range(columns - 1, 0, -1)
        cells += [row * columns + column for column in across]
    return cells + [row * columns for row in reversed(range(ROWS))]


def shift(value, order, step):
    chips = len(order)
    pairs = [
        (order[at] * CORES + core, order[(at + step) % chips] * CORES + core)
        for at in range(chips)
        for core in range(CORES)
    ]
    return lax.ppermute(value, "pool", pairs)


def onward(pieces, step, order):
    chips = len(order)
    pieces[step] = shift(pieces[step - 1], order, 1)
    pieces[chips - step] = shift(pieces[(chips - step + 1) % chips], order, -1)


def after(value, *earlier):
    return lax.optimization_barrier((value, earlier))[0]


def swap_core(value, pool):
    return lax.ppermute(value, "pool", [(at, at ^ 1) for at in range(pool)])


def swap_plane(value):
    return lax.ppermute(value, "head", [(0, 1), (1, 0)])


def holder(ring, me, back):
    chips = ring.shape[0] // 2
    chip = lax.div(me[0], CORES)
    place = lax.rem(ring[chips + chip] + chips - back, chips)
    return ring[place] * CORES + lax.rem(me[0], CORES)


def attend_kernel(pieces, owned, ids, ranks, ring, me, queries, cosine, sine, *refs):
    key_pieces, value_pieces, refs = refs[:pieces], refs[pieces : 2 * pieces], refs[2 * pieces :]
    near = refs[:-8]
    sums, stats, keys, values, within, rank_of, key_sem, value_sem = refs[-8:]
    slots = ids.shape[0]
    kv_local, _, head_dim = keys.shape
    length = key_pieces[0].shape[2]
    tokens = queries.shape[0]
    groups = queries.shape[1] // (kv_local * head_dim)
    heads = kv_local * groups
    factor = math.log2(math.e) / math.sqrt(head_dim)
    across = (((1,), (1,)), ((), ()))

    for slot in range(slots):
        passage = ids[slot]
        home = lax.div(passage, owned)
        within[home] = passage - home * owned
        rank_of[home] = ranks[slot]
    homes = [holder(ring, me, piece) for piece in range(pieces)]

    def copy(source, target, sem, piece):
        rows = pl.ds(piece * length, length)
        return pltpu.make_async_copy(
            source[piece].at[within[homes[piece]]], target.at[:, rows], sem.at[piece]
        )

    key_copies = [copy(key_pieces, keys, key_sem, piece) for piece in range(pieces)]
    value_copies = [copy(value_pieces, values, value_sem, piece) for piece in range(pieces)]
    for each in key_copies + value_copies:
        each.start()
    for piece in range(pieces):
        key_copies[piece].wait()
        rank = rank_of[homes[piece]]
        cos = cosine[pl.ds(rank, 1), :]
        sin = sine[pl.ds(rank, 1), :]
        rows = pl.ds(piece * length, length)
        for head in range(kv_local):
            block = keys[head, rows, :].astype(jnp.float32)
            turned = block * cos + pltpu.roll(block, head_dim // 2, 1) * sin
            keys[head, rows, :] = turned.astype(jnp.bfloat16)
    for each in value_copies:
        each.wait()

    lane = lax.broadcasted_iota(jnp.int32, (tokens, LANES), 1)
    marks = jnp.zeros((tokens, LANES), jnp.float32)
    for head in range(kv_local):
        spans = [
            slice((head * groups + g) * head_dim, (head * groups + g + 1) * head_dim)
            for g in range(groups)
        ]
        rows = jnp.concatenate([queries[:, span] for span in spans], axis=0)
        scores = lax.dot_general(rows, keys[head], across, preferred_element_type=jnp.float32)
        peak = jnp.max(scores, axis=1, keepdims=True)
        if near:
            own = slice(head * head_dim, (head + 1) * head_dim)
            close = lax.dot_general(
                rows, near[0][:, own], across, preferred_element_type=jnp.float32
            )
            token = lax.rem(lax.broadcasted_iota(jnp.int32, close.shape, 0), tokens)
            column = lax.broadcasted_iota(jnp.int32, close.shape, 1)
            close = jnp.where(column <= token, close, -jnp.inf)
            peak = jnp.maximum(peak, jnp.max(close, axis=1, keepdims=True))
        exponent = jnp.exp2((scores - peak) * factor)
        total = jnp.sum(exponent, axis=1, keepdims=True)
        summed = jnp.dot(
            exponent.astype(jnp.bfloat16), values[head], preferred_element_type=jnp.float32
        )
        if near:
            exponent = jnp.exp2((close - peak) * factor)
            total = total + jnp.sum(exponent, axis=1, keepdims=True)
            summed = summed + jnp.dot(
                exponent.astype(jnp.bfloat16), near[1][:, own], preferred_element_type=jnp.float32
            )
        for g in range(groups):
            part = slice(g * tokens, (g + 1) * tokens)
            sums[:, spans[g]] = summed[part]
            at = head * groups + g
            marks = jnp.where(lane == at, peak[part], marks)
            marks = jnp.where(lane == heads + at, total[part], marks)
    stats[...] = marks


def attend(ids, ranks, ring, me, queries, tables, near, passages):
    pieces = len(passages[0])
    key_pieces, value_pieces = passages
    owned, kv_local, length, head_dim = key_pieces[0].shape
    tokens, features = queries.shape
    holders = ids.shape[0]
    smem = pl.BlockSpec(memory_space=pltpu.SMEM)
    vmem = pl.BlockSpec(memory_space=pltpu.VMEM)
    seen = pieces * length
    scores = tokens * (features // head_dim) * (seen + (length if near else 0))
    return pl.pallas_call(
        functools.partial(attend_kernel, pieces, owned),
        out_shape=[
            jax.ShapeDtypeStruct((tokens, features), jnp.float32),
            jax.ShapeDtypeStruct((tokens, LANES), jnp.float32),
        ],
        in_specs=[smem] * 4
        + [vmem] * 3
        + [pl.BlockSpec(memory_space=pl.ANY)] * (2 * pieces)
        + [vmem] * len(near),
        out_specs=[vmem] * 2,
        scratch_shapes=[
            pltpu.VMEM((kv_local, seen, head_dim), jnp.bfloat16),
            pltpu.VMEM((kv_local, seen, head_dim), jnp.bfloat16),
            pltpu.SMEM((holders,), jnp.int32),
            pltpu.SMEM((holders,), jnp.int32),
            pltpu.SemaphoreType.DMA((pieces,)),
            pltpu.SemaphoreType.DMA((pieces,)),
        ],
        compiler_params=pltpu.CompilerParams(vmem_limit_bytes=32 * MIB),
        cost_estimate=pl.CostEstimate(
            flops=4 * scores * head_dim, bytes_accessed=4 * MIB, transcendentals=scores
        ),
        name="attend",
    )(ids, ranks, ring, me, queries, *tables, *key_pieces, *value_pieces, *near)


def combine_kernel(head_dim, sums, stats, sums_in, stats_in, attended):
    heads = sums.shape[1] // head_dim
    factor = math.log2(math.e) / math.sqrt(head_dim)
    for head in range(heads):
        columns = slice(head * head_dim, (head + 1) * head_dim)
        peak_a, peak_b = stats[:, head : head + 1], stats_in[:, head : head + 1]
        at = heads + head
        total_a, total_b = stats[:, at : at + 1], stats_in[:, at : at + 1]
        peak = jnp.maximum(peak_a, peak_b)
        part_a = jnp.exp2((peak_a - peak) * factor)
        part_b = jnp.exp2((peak_b - peak) * factor)
        total = total_a * part_a + total_b * part_b
        value = sums[:, columns] * part_a + sums_in[:, columns] * part_b
        attended[:, columns] = (value / total).astype(attended.dtype)


def combine(head_dim, sums, stats, sums_in, stats_in):
    vmem = pl.BlockSpec(memory_space=pltpu.VMEM)
    return pl.pallas_call(
        functools.partial(combine_kernel, head_dim),
        out_shape=jax.ShapeDtypeStruct(sums.shape, jnp.bfloat16),
        in_specs=[vmem] * 4,
        out_specs=vmem,
        compiler_params=pltpu.CompilerParams(vmem_limit_bytes=24 * MIB),
        cost_estimate=pl.CostEstimate(
            flops=4 * sums.size, bytes_accessed=10 * sums.size, transcendentals=0
        ),
        name="combine",
    )(sums, stats, sums_in, stats_in)


def project_kernel(places, based, ring, me, own_rows, other_rows, *refs):
    count = len(places)
    blocks, refs = refs[: 2 * count], refs[2 * count :]
    base = None
    if based:
        base, refs = refs[0], refs[1:]
    results, (held, total, sems) = refs[:-3], refs[-3:]
    planes, span, _ = held.shape[1:]
    copies = [
        pltpu.make_async_copy(block, held.at[at], sems.at[at]) for at, block in enumerate(blocks)
    ]
    for copy in copies:
        copy.start()
    for at, place in enumerate(places):
        home = holder(ring, me, place)
        left, right = [], []
        for part, source in enumerate((home, home + 1 - 2 * lax.rem(home, CORES))):
            copies[2 * at + part].wait()
            first = pl.multiple_of(source * span, span)
            for plane, rows in enumerate((own_rows, other_rows)):
                left.append(rows[:, pl.ds(first, span)])
                right.append(held[2 * at + part, plane])
        value = jnp.dot(
            jnp.concatenate(left, axis=1),
            jnp.concatenate(right, axis=0),
            preferred_element_type=jnp.float32,
        )
        if at:
            value = value + total[...]
        elif base is not None:
            value = value + base[...]
        if at + 1 < count:
            total[...] = value
    tokens = results[0].shape[0]
    for part, result in enumerate(results):
        result[...] = value[part * tokens : (part + 1) * tokens].astype(result.dtype)


def project(ring, me, rows, places, weights, base, shapes):
    blocks = [half[place] for place in places for half in weights]
    tokens = rows[0].shape[0]
    planes, span, width = blocks[0].shape
    smem = pl.BlockSpec(memory_space=pltpu.SMEM)
    vmem = pl.BlockSpec(memory_space=pltpu.VMEM)
    return pl.pallas_call(
        functools.partial(project_kernel, tuple(places), base is not None),
        out_shape=shapes,
        in_specs=[smem] * 2
        + [vmem] * 2
        + [pl.BlockSpec(memory_space=pl.ANY)] * len(blocks)
        + ([vmem] if base is not None else []),
        out_specs=[vmem] * len(shapes),
        scratch_shapes=[
            pltpu.VMEM((len(blocks), planes, span, width), jnp.bfloat16),
            pltpu.VMEM((tokens, width), jnp.float32),
            pltpu.SemaphoreType.DMA((len(blocks),)),
        ],
        compiler_params=pltpu.CompilerParams(vmem_limit_bytes=32 * MIB),
        cost_estimate=pl.CostEstimate(
            flops=2 * len(blocks) * planes * tokens * span * width,
            bytes_accessed=2 * len(blocks) * planes * span * width + 4 * tokens * width,
            transcendentals=0,
        ),
        name="project",
    )(ring, me, *rows, *blocks, *([base] if base is not None else []))


def rotation_tables(ranks, length, head_dim):
    offsets = (jnp.arange(ranks) * length).astype(jnp.float32)
    angles = offsets[:, None] * frequency_table(head_dim)[None, :]
    cosine, sine = jnp.cos(angles), jnp.sin(angles)
    return (
        jnp.concatenate([cosine, cosine], axis=1),
        jnp.concatenate([-sine, sine], axis=1),
    )


def ring_body(
    pool,
    queries,
    request_keys,
    request_values,
    cache_keys,
    cache_values,
    passage_ids,
    passage_order,
    out_weight,
):
    _, _, pass_len, head_dim = cache_keys.shape
    tokens = queries.shape[1]
    chips = pool // CORES
    half = chips // 2
    order = ring_order(chips)
    ring = jnp.asarray(order + [order.index(chip) for chip in range(chips)], jnp.int32)
    index = lax.axis_index("pool")
    me = jnp.reshape(index, (1,))
    core = lax.rem(index, CORES)
    plane = lax.axis_index("head")

    kept = {0: cache_keys}, {0: cache_values}
    for step in range(1, half):
        for pieces in kept:
            onward(pieces, step, order)

    span = out_weight.shape[1] // 2
    width = span // CORES
    weight = after(out_weight, kept[0][1], kept[0][chips - 1])
    mine = lax.dynamic_slice_in_dim(weight, plane * span, span, axis=1)
    across = swap_plane(lax.dynamic_slice_in_dim(weight, (1 - plane) * span, span, axis=1))

    def columns(to_core):
        return jnp.stack(
            [
                lax.dynamic_slice_in_dim(value, to_core * width, width, axis=1)
                for value in (mine, across)
            ]
        )

    heavy = {0: columns(core)}, {0: swap_core(columns(1 - core), pool)}

    queries, picks = after(
        (queries[0], jnp.concatenate([passage_ids, passage_order], axis=0)), kept[1][2]
    )
    picks_in = swap_core(picks, pool)
    other_queries = swap_core(queries, pool)

    for pieces, first in zip(kept, heavy):
        first[1] = shift(after(first[0], pieces[half - 1]), order, 1)
        first[chips - 1] = shift(after(first[0], pieces[half + 1]), order, -1)
    kept[0][half] = shift(after(kept[0][half - 1], heavy[0][1]), order, 1)
    kept[1][half] = shift(after(kept[1][half + 1], heavy[1][chips - 1]), order, -1)
    other_queries = after(other_queries, heavy[0][chips - 1], heavy[1][1])
    passages = [[pieces[at] for at in range(chips)] for pieces in kept]

    for pieces in heavy:
        onward(pieces, 2, order)
    tables = rotation_tables(passage_ids.shape[1], pass_len, head_dim)
    other = attend(picks_in[0], picks_in[1], ring, me, other_queries, tables, (), passages)
    near, far = heavy
    other, queries, near = lax.optimization_barrier((other, queries, near))
    other_in = [swap_core(value, pool) for value in other]
    own_block = (request_keys[0], request_values[0])
    own = attend(picks[0], picks[1], ring, me, queries, tables, own_block, passages)
    onward(near, 3, order)
    own, far = lax.optimization_barrier((own, far))
    onward(far, 3, order)

    attended = combine(head_dim, *own, *other_in)
    rows = []
    for value in (attended, swap_plane(attended)):
        rows.append(jnp.concatenate([value, swap_core(value, pool)], axis=0))

    near[half] = shift(near[half - 1], order, 1)
    far[half] = shift(far[half + 1], order, -1)
    sums = [jax.ShapeDtypeStruct((CORES * tokens, width), jnp.float32)]
    weights = (near, far)
    early = [0] + [at for step in range(1, half - 1) for at in (step, chips - step)]
    total = project(ring, me, rows, early, weights, None, sums)[0]
    total = project(ring, me, rows, [half - 1, half + 1], weights, total, sums)[0]
    own_out, other_out = project(
        ring, me, rows, [half], weights, total, [jax.ShapeDtypeStruct((tokens, width), jnp.bfloat16)] * 2
    )
    beside = swap_core(other_out, pool)
    result = jnp.where(
        core == 0,
        jnp.concatenate([own_out, beside], axis=1),
        jnp.concatenate([beside, own_out], axis=1),
    )
    return result[None]


def solution(mesh):
    pool, heads_axis = mesh.shape["pool"], mesh.shape["head"]

    def body(*args):
        weight = args[-1]
        tiled = weight.shape[0] % LANES == 0 and weight.shape[1] % (2 * CORES * LANES) == 0
        if tiled and heads_axis == 2 and pool % (2 * ROWS * CORES) == 0:
            return ring_body(pool, *args)
        return plain_body(*args)

    placed = (
        P("pool", None, "head"),
        P("pool", None, "head"),
        P("pool", None, "head"),
        P("pool", "head", None, None),
        P("pool", "head", None, None),
        P("pool", None),
        P("pool", None),
        P(("head", "pool"), None),
    )
    return jax.shard_map(
        body, mesh=mesh, in_specs=placed, out_specs=P("pool", None, "head"), check_vma=False
    )
```

```python
import functools
import math

import jax
import jax.numpy as jnp
from jax import lax
from jax.experimental import pallas as pl
from jax.experimental.pallas import tpu as pltpu
from jax.sharding import PartitionSpec as P

CORES = 2
ROWS = 4
LANES = 128
MIB = 1024 * 1024


def frequency_table(head_dim):
    pair_index = jnp.arange(head_dim // 2, dtype=jnp.float32)
    return jnp.exp(pair_index * (-2.0 / head_dim) * jnp.log(jnp.float32(500000.0)))


def reposition(vectors, offset, head_dim):
    angles = offset.astype(jnp.float32) * frequency_table(head_dim)
    cosine = jnp.cos(angles)
    sine_term = jnp.sin(angles)
    front_half = vectors[..., : head_dim // 2]
    back_half = vectors[..., head_dim // 2 :]
    return jnp.concatenate(
        [front_half * cosine - back_half * sine_term, back_half * cosine + front_half * sine_term],
        axis=-1,
    )


def absorb(state, query_rows, keys_block, values_block, allowed):
    running_peak, running_total, running_sum = state
    scores = jnp.einsum(
        "hrd,hnd->hrn", query_rows, keys_block, preferred_element_type=jnp.float32
    ) * query_rows.shape[2] ** (-0.5)
    if allowed is not None:
        scores = jnp.where(allowed[None], scores, -jnp.inf)
    new_peak = jnp.maximum(running_peak, jnp.max(scores, axis=-1))
    factor = jnp.exp(running_peak - new_peak)
    exponent = jnp.exp(scores - new_peak[..., None])
    weights = exponent.astype(jnp.bfloat16)
    new_total = running_total * factor + jnp.sum(exponent, axis=-1)
    new_sum = running_sum * factor[..., None] + jnp.einsum(
        "hrn,hnd->hrd", weights, values_block, preferred_element_type=jnp.float32
    )
    return (new_peak, new_total, new_sum)


def plain_body(
    queries,
    request_keys,
    request_values,
    cache_keys,
    cache_values,
    passage_ids,
    passage_order,
    out_weight,
):
    owned, kv_local, pass_len, head_dim = cache_keys.shape
    query_len = queries.shape[1]
    groups = queries.shape[2] // (kv_local * head_dim)
    row_count = query_len * groups
    query_rows = (
        queries[0]
        .reshape(query_len, kv_local, groups, head_dim)
        .transpose(1, 0, 2, 3)
        .reshape(kv_local, row_count, head_dim)
    )
    own_keys = request_keys[0].reshape(query_len, kv_local, head_dim).transpose(1, 0, 2)
    own_values = request_values[0].reshape(query_len, kv_local, head_dim).transpose(1, 0, 2)
    query_token = jnp.arange(row_count) // groups
    causal = jnp.arange(query_len)[None, :] <= query_token[:, None]
    state = (
        jnp.full((kv_local, row_count), -jnp.inf, jnp.float32),
        jnp.zeros((kv_local, row_count), jnp.float32),
        jnp.zeros((kv_local, row_count, head_dim), jnp.float32),
    )
    state = absorb(state, query_rows, own_keys, own_values, causal)
    slots = passage_ids[0]
    offsets = passage_order[0] * pass_len
    piece_keys = lax.all_gather(cache_keys, "pool", axis=0, tiled=True)
    piece_values = lax.all_gather(cache_values, "pool", axis=0, tiled=True)

    def visit_one(position, current):
        matches = slots == position
        offset = jnp.sum(jnp.where(matches, offsets, 0))

        def absorb_one(inner):
            placed = reposition(piece_keys[position].astype(jnp.float32), offset, head_dim).astype(
                jnp.bfloat16
            )
            return absorb(inner, query_rows, placed, piece_values[position], None)

        return lax.cond(jnp.any(matches), absorb_one, lambda inner: inner, current)

    state = lax.fori_loop(0, piece_keys.shape[0], visit_one, state)
    running_peak, running_total, running_sum = state
    attended = (running_sum / running_total[..., None]).astype(jnp.bfloat16)
    attended = (
        attended.reshape(kv_local, query_len, groups, head_dim)
        .transpose(1, 0, 2, 3)
        .reshape(query_len, kv_local * groups * head_dim)
    )
    partial_value = jnp.dot(
        attended,
        lax.all_gather(out_weight, "pool", axis=0, tiled=True),
        preferred_element_type=jnp.float32,
    )
    summed = lax.psum_scatter(
        partial_value.astype(jnp.bfloat16), "head", scatter_dimension=1, tiled=True
    )
    return summed[None]


def ring_order(chips):
    columns = chips // ROWS
    cells = []
    for row in range(ROWS):
        across = range(1, columns) if row % 2 == 0 else range(columns - 1, 0, -1)
        cells += [row * columns + column for column in across]
    return cells + [row * columns for row in reversed(range(ROWS))]


def shift(value, order, step):
    chips = len(order)
    pairs = [
        (order[at] * CORES + core, order[(at + step) % chips] * CORES + core)
        for at in range(chips)
        for core in range(CORES)
    ]
    return lax.ppermute(value, "pool", pairs)


def onward(pieces, step, order):
    chips = len(order)
    pieces[step] = shift(pieces[step - 1], order, 1)
    pieces[chips - step] = shift(pieces[(chips - step + 1) % chips], order, -1)


def after(value, *earlier):
    return lax.optimization_barrier((value, earlier))[0]


def swap_core(value, pool):
    return lax.ppermute(value, "pool", [(at, at ^ 1) for at in range(pool)])


def swap_plane(value):
    return lax.ppermute(value, "head", [(0, 1), (1, 0)])


def holder(ring, me, back):
    chips = ring.shape[0] // 2
    chip = lax.div(me[0], CORES)
    place = lax.rem(ring[chips + chip] + chips - back, chips)
    return ring[place] * CORES + lax.rem(me[0], CORES)


def attend_kernel(pieces, owned, ids, ranks, ring, me, queries, cosine, sine, *refs):
    key_pieces, value_pieces, refs = refs[:pieces], refs[pieces : 2 * pieces], refs[2 * pieces :]
    near = refs[:-8]
    sums, stats, keys, values, within, rank_of, key_sem, value_sem = refs[-8:]
    slots = ids.shape[0]
    kv_local, _, head_dim = keys.shape
    length = key_pieces[0].shape[2]
    tokens = queries.shape[0]
    groups = queries.shape[1] // (kv_local * head_dim)
    heads = kv_local * groups
    factor = math.log2(math.e) / math.sqrt(head_dim)
    across = (((1,), (1,)), ((), ()))

    for slot in range(slots):
        passage = ids[slot]
        home = lax.div(passage, owned)
        within[home] = passage - home * owned
        rank_of[home] = ranks[slot]
    homes = [holder(ring, me, piece) for piece in range(pieces)]

    def copy(source, target, sem, piece):
        rows = pl.ds(piece * length, length)
        return pltpu.make_async_copy(
            source[piece].at[within[homes[piece]]], target.at[:, rows], sem.at[piece]
        )

    key_copies = [copy(key_pieces, keys, key_sem, piece) for piece in range(pieces)]
    value_copies = [copy(value_pieces, values, value_sem, piece) for piece in range(pieces)]
    for each in key_copies + value_copies:
        each.start()
    for piece in range(pieces):
        key_copies[piece].wait()
        rank = rank_of[homes[piece]]
        cos = cosine[pl.ds(rank, 1), :]
        sin = sine[pl.ds(rank, 1), :]
        rows = pl.ds(piece * length, length)
        for head in range(kv_local):
            block = keys[head, rows, :].astype(jnp.float32)
            turned = block * cos + pltpu.roll(block, head_dim // 2, 1) * sin
            keys[head, rows, :] = turned.astype(jnp.bfloat16)
    for each in value_copies:
        each.wait()

    lane = lax.broadcasted_iota(jnp.int32, (tokens, LANES), 1)
    marks = jnp.zeros((tokens, LANES), jnp.float32)
    for head in range(kv_local):
        spans = [
            slice((head * groups + g) * head_dim, (head * groups + g + 1) * head_dim)
            for g in range(groups)
        ]
        rows = jnp.concatenate([queries[:, span] for span in spans], axis=0)
        scores = lax.dot_general(rows, keys[head], across, preferred_element_type=jnp.float32)
        peak = jnp.max(scores, axis=1, keepdims=True)
        if near:
            own = slice(head * head_dim, (head + 1) * head_dim)
            close = lax.dot_general(
                rows, near[0][:, own], across, preferred_element_type=jnp.float32
            )
            token = lax.rem(lax.broadcasted_iota(jnp.int32, close.shape, 0), tokens)
            column = lax.broadcasted_iota(jnp.int32, close.shape, 1)
            close = jnp.where(column <= token, close, -jnp.inf)
            peak = jnp.maximum(peak, jnp.max(close, axis=1, keepdims=True))
        exponent = jnp.exp2((scores - peak) * factor)
        total = jnp.sum(exponent, axis=1, keepdims=True)
        summed = jnp.dot(
            exponent.astype(jnp.bfloat16), values[head], preferred_element_type=jnp.float32
        )
        if near:
            exponent = jnp.exp2((close - peak) * factor)
            total = total + jnp.sum(exponent, axis=1, keepdims=True)
            summed = summed + jnp.dot(
                exponent.astype(jnp.bfloat16), near[1][:, own], preferred_element_type=jnp.float32
            )
        for g in range(groups):
            part = slice(g * tokens, (g + 1) * tokens)
            sums[:, spans[g]] = summed[part]
            at = head * groups + g
            marks = jnp.where(lane == at, peak[part], marks)
            marks = jnp.where(lane == heads + at, total[part], marks)
    stats[...] = marks


def attend(ids, ranks, ring, me, queries, tables, near, passages):
    pieces = len(passages[0])
    key_pieces, value_pieces = passages
    owned, kv_local, length, head_dim = key_pieces[0].shape
    tokens, features = queries.shape
    holders = ids.shape[0]
    smem = pl.BlockSpec(memory_space=pltpu.SMEM)
    vmem = pl.BlockSpec(memory_space=pltpu.VMEM)
    seen = pieces * length
    scores = tokens * (features // head_dim) * (seen + (length if near else 0))
    return pl.pallas_call(
        functools.partial(attend_kernel, pieces, owned),
        out_shape=[
            jax.ShapeDtypeStruct((tokens, features), jnp.float32),
            jax.ShapeDtypeStruct((tokens, LANES), jnp.float32),
        ],
        in_specs=[smem] * 4
        + [vmem] * 3
        + [pl.BlockSpec(memory_space=pl.ANY)] * (2 * pieces)
        + [vmem] * len(near),
        out_specs=[vmem] * 2,
        scratch_shapes=[
            pltpu.VMEM((kv_local, seen, head_dim), jnp.bfloat16),
            pltpu.VMEM((kv_local, seen, head_dim), jnp.bfloat16),
            pltpu.SMEM((holders,), jnp.int32),
            pltpu.SMEM((holders,), jnp.int32),
            pltpu.SemaphoreType.DMA((pieces,)),
            pltpu.SemaphoreType.DMA((pieces,)),
        ],
        compiler_params=pltpu.CompilerParams(vmem_limit_bytes=32 * MIB),
        cost_estimate=pl.CostEstimate(
            flops=4 * scores * head_dim, bytes_accessed=4 * MIB, transcendentals=scores
        ),
        name="attend",
    )(ids, ranks, ring, me, queries, *tables, *key_pieces, *value_pieces, *near)


def combine_kernel(head_dim, sums, stats, sums_in, stats_in, attended):
    heads = sums.shape[1] // head_dim
    factor = math.log2(math.e) / math.sqrt(head_dim)
    for head in range(heads):
        columns = slice(head * head_dim, (head + 1) * head_dim)
        peak_a, peak_b = stats[:, head : head + 1], stats_in[:, head : head + 1]
        at = heads + head
        total_a, total_b = stats[:, at : at + 1], stats_in[:, at : at + 1]
        peak = jnp.maximum(peak_a, peak_b)
        part_a = jnp.exp2((peak_a - peak) * factor)
        part_b = jnp.exp2((peak_b - peak) * factor)
        total = total_a * part_a + total_b * part_b
        value = sums[:, columns] * part_a + sums_in[:, columns] * part_b
        attended[:, columns] = (value / total).astype(attended.dtype)


def combine(head_dim, sums, stats, sums_in, stats_in):
    vmem = pl.BlockSpec(memory_space=pltpu.VMEM)
    return pl.pallas_call(
        functools.partial(combine_kernel, head_dim),
        out_shape=jax.ShapeDtypeStruct(sums.shape, jnp.bfloat16),
        in_specs=[vmem] * 4,
        out_specs=vmem,
        compiler_params=pltpu.CompilerParams(vmem_limit_bytes=24 * MIB),
        cost_estimate=pl.CostEstimate(
            flops=4 * sums.size, bytes_accessed=10 * sums.size, transcendentals=0
        ),
        name="combine",
    )(sums, stats, sums_in, stats_in)


def project_kernel(places, based, ring, me, own_rows, other_rows, *refs):
    count = len(places)
    blocks, refs = refs[: 2 * count], refs[2 * count :]
    base = None
    if based:
        base, refs = refs[0], refs[1:]
    results, (held, total, sems) = refs[:-3], refs[-3:]
    planes, span, _ = held.shape[1:]
    copies = [
        pltpu.make_async_copy(block, held.at[at], sems.at[at]) for at, block in enumerate(blocks)
    ]
    for copy in copies:
        copy.start()
    for at, place in enumerate(places):
        home = holder(ring, me, place)
        left, right = [], []
        for part, source in enumerate((home, home + 1 - 2 * lax.rem(home, CORES))):
            copies[2 * at + part].wait()
            first = pl.multiple_of(source * span, span)
            for plane, rows in enumerate((own_rows, other_rows)):
                left.append(rows[:, pl.ds(first, span)])
                right.append(held[2 * at + part, plane])
        value = jnp.dot(
            jnp.concatenate(left, axis=1),
            jnp.concatenate(right, axis=0),
            preferred_element_type=jnp.float32,
        )
        if at:
            value = value + total[...]
        elif base is not None:
            value = value + base[...]
        if at + 1 < count:
            total[...] = value
    tokens = results[0].shape[0]
    for part, result in enumerate(results):
        result[...] = value[part * tokens : (part + 1) * tokens].astype(result.dtype)


def project(ring, me, rows, places, weights, base, shapes):
    blocks = [half[place] for place in places for half in weights]
    tokens = rows[0].shape[0]
    planes, span, width = blocks[0].shape
    smem = pl.BlockSpec(memory_space=pltpu.SMEM)
    vmem = pl.BlockSpec(memory_space=pltpu.VMEM)
    return pl.pallas_call(
        functools.partial(project_kernel, tuple(places), base is not None),
        out_shape=shapes,
        in_specs=[smem] * 2
        + [vmem] * 2
        + [pl.BlockSpec(memory_space=pl.ANY)] * len(blocks)
        + ([vmem] if base is not None else []),
        out_specs=[vmem] * len(shapes),
        scratch_shapes=[
            pltpu.VMEM((len(blocks), planes, span, width), jnp.bfloat16),
            pltpu.VMEM((tokens, width), jnp.float32),
            pltpu.SemaphoreType.DMA((len(blocks),)),
        ],
        compiler_params=pltpu.CompilerParams(vmem_limit_bytes=32 * MIB),
        cost_estimate=pl.CostEstimate(
            flops=2 * len(blocks) * planes * tokens * span * width,
            bytes_accessed=2 * len(blocks) * planes * span * width + 4 * tokens * width,
            transcendentals=0,
        ),
        name="project",
    )(ring, me, *rows, *blocks, *([base] if base is not None else []))


def rotation_tables(ranks, length, head_dim):
    offsets = (jnp.arange(ranks) * length).astype(jnp.float32)
    angles = offsets[:, None] * frequency_table(head_dim)[None, :]
    cosine, sine = jnp.cos(angles), jnp.sin(angles)
    return (
        jnp.concatenate([cosine, cosine], axis=1),
        jnp.concatenate([-sine, sine], axis=1),
    )


def ring_body(
    pool,
    queries,
    request_keys,
    request_values,
    cache_keys,
    cache_values,
    passage_ids,
    passage_order,
    out_weight,
):
    _, _, pass_len, head_dim = cache_keys.shape
    tokens = queries.shape[1]
    chips = pool // CORES
    half = chips // 2
    order = ring_order(chips)
    ring = jnp.asarray(order + [order.index(chip) for chip in range(chips)], jnp.int32)
    index = lax.axis_index("pool")
    me = jnp.reshape(index, (1,))
    core = lax.rem(index, CORES)
    plane = lax.axis_index("head")

    kept = {0: cache_keys}, {0: cache_values}
    for step in range(1, half):
        for pieces in kept:
            onward(pieces, step, order)
    kept[0][half] = shift(kept[0][half - 1], order, 1)
    kept[1][half] = shift(kept[1][half + 1], order, -1)
    passages = [[pieces[at] for at in range(chips)] for pieces in kept]

    weight, queries, picks = after(
        (out_weight, queries[0], jnp.concatenate([passage_ids, passage_order], axis=0)),
        *[pieces[at] for pieces in kept for at in (2, chips - 2)],
    )

    span = out_weight.shape[1] // 2
    width = span // CORES
    mine = lax.dynamic_slice_in_dim(weight, plane * span, span, axis=1)
    across = swap_plane(lax.dynamic_slice_in_dim(weight, (1 - plane) * span, span, axis=1))

    def columns(to_core):
        return jnp.stack(
            [
                lax.dynamic_slice_in_dim(value, to_core * width, width, axis=1)
                for value in (mine, across)
            ]
        )

    near, far = heavy = {0: columns(core)}, {0: swap_core(columns(1 - core), pool)}
    for step in range(1, half):
        for pieces in heavy:
            onward(pieces, step, order)

    picks_in = swap_core(picks, pool)
    other_queries = swap_core(queries, pool)
    tables = rotation_tables(passage_ids.shape[1], pass_len, head_dim)
    other = attend(picks_in[0], picks_in[1], ring, me, other_queries, tables, (), passages)
    own_block = (request_keys[0], request_values[0])
    own = attend(picks[0], picks[1], ring, me, queries, tables, own_block, passages)
    other, own = after(
        (other, own), *[pieces[at] for pieces in heavy for at in (1, chips - 1)]
    )
    other_in = [swap_core(value, pool) for value in other]

    attended = combine(head_dim, *own, *other_in)
    rows = []
    for value in (attended, swap_plane(attended)):
        rows.append(jnp.concatenate([value, swap_core(value, pool)], axis=0))

    near[half] = shift(near[half - 1], order, 1)
    far[half] = shift(far[half + 1], order, -1)
    sums = [jax.ShapeDtypeStruct((CORES * tokens, width), jnp.float32)]
    weights = (near, far)
    early = [0] + [at for step in range(1, half - 1) for at in (step, chips - step)]
    total = project(ring, me, rows, early, weights, None, sums)[0]
    total = project(ring, me, rows, [half - 1, half + 1], weights, total, sums)[0]
    own_out, other_out = project(
        ring, me, rows, [half], weights, total, [jax.ShapeDtypeStruct((tokens, width), jnp.bfloat16)] * 2
    )
    beside = swap_core(other_out, pool)
    result = jnp.where(
        core == 0,
        jnp.concatenate([own_out, beside], axis=1),
        jnp.concatenate([beside, own_out], axis=1),
    )
    return result[None]


def solution(mesh):
    pool, heads_axis = mesh.shape["pool"], mesh.shape["head"]

    def body(*args):
        weight = args[-1]
        tiled = weight.shape[0] % LANES == 0 and weight.shape[1] % (2 * CORES * LANES) == 0
        if tiled and heads_axis == 2 and pool % (2 * ROWS * CORES) == 0:
            return ring_body(pool, *args)
        return plain_body(*args)

    placed = (
        P("pool", None, "head"),
        P("pool", None, "head"),
        P("pool", None, "head"),
        P("pool", "head", None, None),
        P("pool", "head", None, None),
        P("pool", None),
        P("pool", None),
        P(("head", "pool"), None),
    )
    return jax.shard_map(
        body, mesh=mesh, in_specs=placed, out_specs=P("pool", None, "head"), check_vma=False
    )
```

```python
import functools
import math

import jax
import jax.numpy as jnp
from jax import lax
from jax.experimental import pallas as pl
from jax.experimental.pallas import tpu as pltpu
from jax.sharding import PartitionSpec as P

CORES = 2
ROWS = 4
LANES = 128
MIB = 1024 * 1024


def frequency_table(head_dim):
    pair_index = jnp.arange(head_dim // 2, dtype=jnp.float32)
    return jnp.exp(pair_index * (-2.0 / head_dim) * jnp.log(jnp.float32(500000.0)))


def reposition(vectors, offset, head_dim):
    angles = offset.astype(jnp.float32) * frequency_table(head_dim)
    cosine = jnp.cos(angles)
    sine_term = jnp.sin(angles)
    front_half = vectors[..., : head_dim // 2]
    back_half = vectors[..., head_dim // 2 :]
    return jnp.concatenate(
        [front_half * cosine - back_half * sine_term, back_half * cosine + front_half * sine_term],
        axis=-1,
    )


def absorb(state, query_rows, keys_block, values_block, allowed):
    running_peak, running_total, running_sum = state
    scores = jnp.einsum(
        "hrd,hnd->hrn", query_rows, keys_block, preferred_element_type=jnp.float32
    ) * query_rows.shape[2] ** (-0.5)
    if allowed is not None:
        scores = jnp.where(allowed[None], scores, -jnp.inf)
    new_peak = jnp.maximum(running_peak, jnp.max(scores, axis=-1))
    factor = jnp.exp(running_peak - new_peak)
    exponent = jnp.exp(scores - new_peak[..., None])
    weights = exponent.astype(jnp.bfloat16)
    new_total = running_total * factor + jnp.sum(exponent, axis=-1)
    new_sum = running_sum * factor[..., None] + jnp.einsum(
        "hrn,hnd->hrd", weights, values_block, preferred_element_type=jnp.float32
    )
    return (new_peak, new_total, new_sum)


def plain_body(
    queries,
    request_keys,
    request_values,
    cache_keys,
    cache_values,
    passage_ids,
    passage_order,
    out_weight,
):
    owned, kv_local, pass_len, head_dim = cache_keys.shape
    query_len = queries.shape[1]
    groups = queries.shape[2] // (kv_local * head_dim)
    row_count = query_len * groups
    query_rows = (
        queries[0]
        .reshape(query_len, kv_local, groups, head_dim)
        .transpose(1, 0, 2, 3)
        .reshape(kv_local, row_count, head_dim)
    )
    own_keys = request_keys[0].reshape(query_len, kv_local, head_dim).transpose(1, 0, 2)
    own_values = request_values[0].reshape(query_len, kv_local, head_dim).transpose(1, 0, 2)
    query_token = jnp.arange(row_count) // groups
    causal = jnp.arange(query_len)[None, :] <= query_token[:, None]
    state = (
        jnp.full((kv_local, row_count), -jnp.inf, jnp.float32),
        jnp.zeros((kv_local, row_count), jnp.float32),
        jnp.zeros((kv_local, row_count, head_dim), jnp.float32),
    )
    state = absorb(state, query_rows, own_keys, own_values, causal)
    slots = passage_ids[0]
    offsets = passage_order[0] * pass_len
    piece_keys = lax.all_gather(cache_keys, "pool", axis=0, tiled=True)
    piece_values = lax.all_gather(cache_values, "pool", axis=0, tiled=True)

    def visit_one(position, current):
        matches = slots == position
        offset = jnp.sum(jnp.where(matches, offsets, 0))

        def absorb_one(inner):
            placed = reposition(piece_keys[position].astype(jnp.float32), offset, head_dim).astype(
                jnp.bfloat16
            )
            return absorb(inner, query_rows, placed, piece_values[position], None)

        return lax.cond(jnp.any(matches), absorb_one, lambda inner: inner, current)

    state = lax.fori_loop(0, piece_keys.shape[0], visit_one, state)
    running_peak, running_total, running_sum = state
    attended = (running_sum / running_total[..., None]).astype(jnp.bfloat16)
    attended = (
        attended.reshape(kv_local, query_len, groups, head_dim)
        .transpose(1, 0, 2, 3)
        .reshape(query_len, kv_local * groups * head_dim)
    )
    partial_value = jnp.dot(
        attended,
        lax.all_gather(out_weight, "pool", axis=0, tiled=True),
        preferred_element_type=jnp.float32,
    )
    summed = lax.psum_scatter(
        partial_value.astype(jnp.bfloat16), "head", scatter_dimension=1, tiled=True
    )
    return summed[None]


def ring_order(chips):
    columns = chips // ROWS
    cells = []
    for row in range(ROWS):
        across = range(1, columns) if row % 2 == 0 else range(columns - 1, 0, -1)
        cells += [row * columns + column for column in across]
    return cells + [row * columns for row in reversed(range(ROWS))]


def shift(value, order, step):
    chips = len(order)
    pairs = [
        (order[at] * CORES + core, order[(at + step) % chips] * CORES + core)
        for at in range(chips)
        for core in range(CORES)
    ]
    return lax.ppermute(value, "pool", pairs)


def onward(pieces, step, order):
    chips = len(order)
    pieces[step] = shift(pieces[step - 1], order, 1)
    pieces[chips - step] = shift(pieces[(chips - step + 1) % chips], order, -1)


def after(value, *earlier):
    return lax.optimization_barrier((value, earlier))[0]


def swap_core(value, pool):
    return lax.ppermute(value, "pool", [(at, at ^ 1) for at in range(pool)])


def swap_plane(value):
    return lax.ppermute(value, "head", [(0, 1), (1, 0)])


def holder(ring, me, back):
    chips = ring.shape[0] // 2
    chip = lax.div(me[0], CORES)
    place = lax.rem(ring[chips + chip] + chips - back, chips)
    return ring[place] * CORES + lax.rem(me[0], CORES)


def attend_kernel(pieces, owned, ids, ranks, me, queries, cosine, sine, all_keys, all_values, *refs):
    near = refs[:-8]
    sums, stats, keys, values, within, rank_of, key_sem, value_sem = refs[-8:]
    slots = ids.shape[0]
    kv_local, _, head_dim = keys.shape
    length = all_keys.shape[2]
    tokens = queries.shape[0]
    groups = queries.shape[1] // (kv_local * head_dim)
    heads = kv_local * groups
    factor = math.log2(math.e) / math.sqrt(head_dim)
    across = (((1,), (1,)), ((), ()))

    for slot in range(slots):
        passage = ids[slot]
        home = lax.div(passage, owned)
        within[home] = passage - home * owned
        rank_of[home] = ranks[slot]
    homes = [piece * CORES + lax.rem(me[0], CORES) for piece in range(pieces)]

    def copy(source, target, sem, piece):
        rows = pl.ds(piece * length, length)
        return pltpu.make_async_copy(
            source.at[piece * owned + within[homes[piece]]], target.at[:, rows], sem.at[piece]
        )

    key_copies = [copy(all_keys, keys, key_sem, piece) for piece in range(pieces)]
    value_copies = [copy(all_values, values, value_sem, piece) for piece in range(pieces)]
    for each in key_copies + value_copies:
        each.start()
    for piece in range(pieces):
        key_copies[piece].wait()
        rank = rank_of[homes[piece]]
        cos = cosine[pl.ds(rank, 1), :]
        sin = sine[pl.ds(rank, 1), :]
        rows = pl.ds(piece * length, length)
        for head in range(kv_local):
            block = keys[head, rows, :].astype(jnp.float32)
            turned = block * cos + pltpu.roll(block, head_dim // 2, 1) * sin
            keys[head, rows, :] = turned.astype(jnp.bfloat16)
    for each in value_copies:
        each.wait()

    lane = lax.broadcasted_iota(jnp.int32, (tokens, LANES), 1)
    marks = jnp.zeros((tokens, LANES), jnp.float32)
    for head in range(kv_local):
        spans = [
            slice((head * groups + g) * head_dim, (head * groups + g + 1) * head_dim)
            for g in range(groups)
        ]
        rows = jnp.concatenate([queries[:, span] for span in spans], axis=0)
        scores = lax.dot_general(rows, keys[head], across, preferred_element_type=jnp.float32)
        peak = jnp.max(scores, axis=1, keepdims=True)
        if near:
            own = slice(head * head_dim, (head + 1) * head_dim)
            close = lax.dot_general(
                rows, near[0][:, own], across, preferred_element_type=jnp.float32
            )
            token = lax.rem(lax.broadcasted_iota(jnp.int32, close.shape, 0), tokens)
            column = lax.broadcasted_iota(jnp.int32, close.shape, 1)
            close = jnp.where(column <= token, close, -jnp.inf)
            peak = jnp.maximum(peak, jnp.max(close, axis=1, keepdims=True))
        exponent = jnp.exp2((scores - peak) * factor)
        total = jnp.sum(exponent, axis=1, keepdims=True)
        summed = jnp.dot(
            exponent.astype(jnp.bfloat16), values[head], preferred_element_type=jnp.float32
        )
        if near:
            exponent = jnp.exp2((close - peak) * factor)
            total = total + jnp.sum(exponent, axis=1, keepdims=True)
            summed = summed + jnp.dot(
                exponent.astype(jnp.bfloat16), near[1][:, own], preferred_element_type=jnp.float32
            )
        for g in range(groups):
            part = slice(g * tokens, (g + 1) * tokens)
            sums[:, spans[g]] = summed[part]
            at = head * groups + g
            marks = jnp.where(lane == at, peak[part], marks)
            marks = jnp.where(lane == heads + at, total[part], marks)
    stats[...] = marks


def attend(ids, ranks, me, queries, tables, near, pieces, passages):
    gathered, kv_local, length, head_dim = passages[0].shape
    owned = gathered // pieces
    tokens, features = queries.shape
    holders = ids.shape[0]
    smem = pl.BlockSpec(memory_space=pltpu.SMEM)
    vmem = pl.BlockSpec(memory_space=pltpu.VMEM)
    seen = pieces * length
    scores = tokens * (features // head_dim) * (seen + (length if near else 0))
    return pl.pallas_call(
        functools.partial(attend_kernel, pieces, owned),
        out_shape=[
            jax.ShapeDtypeStruct((tokens, features), jnp.float32),
            jax.ShapeDtypeStruct((tokens, LANES), jnp.float32),
        ],
        in_specs=[smem] * 3
        + [vmem] * 3
        + [pl.BlockSpec(memory_space=pl.ANY)] * 2
        + [vmem] * len(near),
        out_specs=[vmem] * 2,
        scratch_shapes=[
            pltpu.VMEM((kv_local, seen, head_dim), jnp.bfloat16),
            pltpu.VMEM((kv_local, seen, head_dim), jnp.bfloat16),
            pltpu.SMEM((holders,), jnp.int32),
            pltpu.SMEM((holders,), jnp.int32),
            pltpu.SemaphoreType.DMA((pieces,)),
            pltpu.SemaphoreType.DMA((pieces,)),
        ],
        compiler_params=pltpu.CompilerParams(vmem_limit_bytes=32 * MIB),
        cost_estimate=pl.CostEstimate(
            flops=4 * scores * head_dim, bytes_accessed=4 * MIB, transcendentals=scores
        ),
        name="attend",
    )(ids, ranks, me, queries, *tables, *passages, *near)


def combine_kernel(head_dim, sums, stats, sums_in, stats_in, attended):
    heads = sums.shape[1] // head_dim
    factor = math.log2(math.e) / math.sqrt(head_dim)
    for head in range(heads):
        columns = slice(head * head_dim, (head + 1) * head_dim)
        peak_a, peak_b = stats[:, head : head + 1], stats_in[:, head : head + 1]
        at = heads + head
        total_a, total_b = stats[:, at : at + 1], stats_in[:, at : at + 1]
        peak = jnp.maximum(peak_a, peak_b)
        part_a = jnp.exp2((peak_a - peak) * factor)
        part_b = jnp.exp2((peak_b - peak) * factor)
        total = total_a * part_a + total_b * part_b
        value = sums[:, columns] * part_a + sums_in[:, columns] * part_b
        attended[:, columns] = (value / total).astype(attended.dtype)


def combine(head_dim, sums, stats, sums_in, stats_in):
    vmem = pl.BlockSpec(memory_space=pltpu.VMEM)
    return pl.pallas_call(
        functools.partial(combine_kernel, head_dim),
        out_shape=jax.ShapeDtypeStruct(sums.shape, jnp.bfloat16),
        in_specs=[vmem] * 4,
        out_specs=vmem,
        compiler_params=pltpu.CompilerParams(vmem_limit_bytes=24 * MIB),
        cost_estimate=pl.CostEstimate(
            flops=4 * sums.size, bytes_accessed=10 * sums.size, transcendentals=0
        ),
        name="combine",
    )(sums, stats, sums_in, stats_in)


def project_kernel(places, based, ring, me, own_rows, other_rows, *refs):
    count = len(places)
    blocks, refs = refs[: 2 * count], refs[2 * count :]
    base = None
    if based:
        base, refs = refs[0], refs[1:]
    results, (held, total, sems) = refs[:-3], refs[-3:]
    planes, span, _ = held.shape[1:]
    copies = [
        pltpu.make_async_copy(block, held.at[at], sems.at[at]) for at, block in enumerate(blocks)
    ]
    for copy in copies:
        copy.start()
    for at, place in enumerate(places):
        home = holder(ring, me, place)
        left, right = [], []
        for part, source in enumerate((home, home + 1 - 2 * lax.rem(home, CORES))):
            copies[2 * at + part].wait()
            first = pl.multiple_of(source * span, span)
            for plane, rows in enumerate((own_rows, other_rows)):
                left.append(rows[:, pl.ds(first, span)])
                right.append(held[2 * at + part, plane])
        value = jnp.dot(
            jnp.concatenate(left, axis=1),
            jnp.concatenate(right, axis=0),
            preferred_element_type=jnp.float32,
        )
        if at:
            value = value + total[...]
        elif base is not None:
            value = value + base[...]
        if at + 1 < count:
            total[...] = value
    tokens = results[0].shape[0]
    for part, result in enumerate(results):
        result[...] = value[part * tokens : (part + 1) * tokens].astype(result.dtype)


def project(ring, me, rows, places, weights, base, shapes):
    blocks = [half[place] for place in places for half in weights]
    tokens = rows[0].shape[0]
    planes, span, width = blocks[0].shape
    smem = pl.BlockSpec(memory_space=pltpu.SMEM)
    vmem = pl.BlockSpec(memory_space=pltpu.VMEM)
    return pl.pallas_call(
        functools.partial(project_kernel, tuple(places), base is not None),
        out_shape=shapes,
        in_specs=[smem] * 2
        + [vmem] * 2
        + [pl.BlockSpec(memory_space=pl.ANY)] * len(blocks)
        + ([vmem] if base is not None else []),
        out_specs=[vmem] * len(shapes),
        scratch_shapes=[
            pltpu.VMEM((len(blocks), planes, span, width), jnp.bfloat16),
            pltpu.VMEM((tokens, width), jnp.float32),
            pltpu.SemaphoreType.DMA((len(blocks),)),
        ],
        compiler_params=pltpu.CompilerParams(vmem_limit_bytes=32 * MIB),
        cost_estimate=pl.CostEstimate(
            flops=2 * len(blocks) * planes * tokens * span * width,
            bytes_accessed=2 * len(blocks) * planes * span * width + 4 * tokens * width,
            transcendentals=0,
        ),
        name="project",
    )(ring, me, *rows, *blocks, *([base] if base is not None else []))


def rotation_tables(ranks, length, head_dim):
    offsets = (jnp.arange(ranks) * length).astype(jnp.float32)
    angles = offsets[:, None] * frequency_table(head_dim)[None, :]
    cosine, sine = jnp.cos(angles), jnp.sin(angles)
    return (
        jnp.concatenate([cosine, cosine], axis=1),
        jnp.concatenate([-sine, sine], axis=1),
    )


def ring_body(
    pool,
    queries,
    request_keys,
    request_values,
    cache_keys,
    cache_values,
    passage_ids,
    passage_order,
    out_weight,
):
    _, _, pass_len, head_dim = cache_keys.shape
    tokens = queries.shape[1]
    chips = pool // CORES
    half = chips // 2
    order = ring_order(chips)
    ring = jnp.asarray(order + [order.index(chip) for chip in range(chips)], jnp.int32)
    index = lax.axis_index("pool")
    me = jnp.reshape(index, (1,))
    core = lax.rem(index, CORES)
    plane = lax.axis_index("head")

    same_core = [list(range(at, pool, CORES)) for at in range(CORES)]
    passages = [
        lax.all_gather(value, "pool", axis=0, tiled=True, axis_index_groups=same_core)
        for value in (cache_keys, cache_values)
    ]
    weight, queries = out_weight, queries[0]
    picks = jnp.concatenate([passage_ids, passage_order], axis=0)

    span = out_weight.shape[1] // 2
    width = span // CORES
    mine = lax.dynamic_slice_in_dim(weight, plane * span, span, axis=1)
    across = swap_plane(lax.dynamic_slice_in_dim(weight, (1 - plane) * span, span, axis=1))

    def columns(to_core):
        return jnp.stack(
            [
                lax.dynamic_slice_in_dim(value, to_core * width, width, axis=1)
                for value in (mine, across)
            ]
        )

    near, far = heavy = {0: columns(core)}, {0: swap_core(columns(1 - core), pool)}
    for step in range(1, half):
        for pieces in heavy:
            onward(pieces, step, order)

    picks_in = swap_core(picks, pool)
    other_queries = swap_core(queries, pool)
    tables = rotation_tables(passage_ids.shape[1], pass_len, head_dim)
    other_queries = after(
        other_queries,
        *[pieces[at] for pieces in heavy for step in (1, 2) for at in (step, chips - step)],
    )
    other = attend(picks_in[0], picks_in[1], me, other_queries, tables, (), chips, passages)
    own_block = (request_keys[0], request_values[0])
    own = attend(picks[0], picks[1], me, queries, tables, own_block, chips, passages)
    other_in = [swap_core(value, pool) for value in other]

    attended = combine(head_dim, *own, *other_in)
    rows = []
    for value in (attended, swap_plane(attended)):
        rows.append(jnp.concatenate([value, swap_core(value, pool)], axis=0))

    near[half] = shift(near[half - 1], order, 1)
    far[half] = shift(far[half + 1], order, -1)
    sums = [jax.ShapeDtypeStruct((CORES * tokens, width), jnp.float32)]
    weights = (near, far)
    early = [0] + [at for step in range(1, half - 1) for at in (step, chips - step)]
    total = project(ring, me, rows, early, weights, None, sums)[0]
    total = project(ring, me, rows, [half - 1, half + 1], weights, total, sums)[0]
    own_out, other_out = project(
        ring, me, rows, [half], weights, total, [jax.ShapeDtypeStruct((tokens, width), jnp.bfloat16)] * 2
    )
    beside = swap_core(other_out, pool)
    result = jnp.where(
        core == 0,
        jnp.concatenate([own_out, beside], axis=1),
        jnp.concatenate([beside, own_out], axis=1),
    )
    return result[None]


def solution(mesh):
    pool, heads_axis = mesh.shape["pool"], mesh.shape["head"]

    def body(*args):
        weight = args[-1]
        tiled = weight.shape[0] % LANES == 0 and weight.shape[1] % (2 * CORES * LANES) == 0
        if tiled and heads_axis == 2 and pool % (2 * ROWS * CORES) == 0:
            return ring_body(pool, *args)
        return plain_body(*args)

    placed = (
        P("pool", None, "head"),
        P("pool", None, "head"),
        P("pool", None, "head"),
        P("pool", "head", None, None),
        P("pool", "head", None, None),
        P("pool", None),
        P("pool", None),
        P(("head", "pool"), None),
    )
    return jax.shard_map(
        body, mesh=mesh, in_specs=placed, out_specs=P("pool", None, "head"), check_vma=False
    )
```

```python
import functools
import math

import jax
import jax.numpy as jnp
from jax import lax
from jax.experimental import pallas as pl
from jax.experimental.pallas import tpu as pltpu
from jax.sharding import PartitionSpec as P

CORES = 2
ROWS = 4
LANES = 128
MIB = 1024 * 1024


def frequency_table(head_dim):
    pair_index = jnp.arange(head_dim // 2, dtype=jnp.float32)
    return jnp.exp(pair_index * (-2.0 / head_dim) * jnp.log(jnp.float32(500000.0)))


def reposition(vectors, offset, head_dim):
    angles = offset.astype(jnp.float32) * frequency_table(head_dim)
    cosine = jnp.cos(angles)
    sine_term = jnp.sin(angles)
    front_half = vectors[..., : head_dim // 2]
    back_half = vectors[..., head_dim // 2 :]
    return jnp.concatenate(
        [front_half * cosine - back_half * sine_term, back_half * cosine + front_half * sine_term],
        axis=-1,
    )


def absorb(state, query_rows, keys_block, values_block, allowed):
    running_peak, running_total, running_sum = state
    scores = jnp.einsum(
        "hrd,hnd->hrn", query_rows, keys_block, preferred_element_type=jnp.float32
    ) * query_rows.shape[2] ** (-0.5)
    if allowed is not None:
        scores = jnp.where(allowed[None], scores, -jnp.inf)
    new_peak = jnp.maximum(running_peak, jnp.max(scores, axis=-1))
    factor = jnp.exp(running_peak - new_peak)
    exponent = jnp.exp(scores - new_peak[..., None])
    weights = exponent.astype(jnp.bfloat16)
    new_total = running_total * factor + jnp.sum(exponent, axis=-1)
    new_sum = running_sum * factor[..., None] + jnp.einsum(
        "hrn,hnd->hrd", weights, values_block, preferred_element_type=jnp.float32
    )
    return (new_peak, new_total, new_sum)


def plain_body(
    queries,
    request_keys,
    request_values,
    cache_keys,
    cache_values,
    passage_ids,
    passage_order,
    out_weight,
):
    owned, kv_local, pass_len, head_dim = cache_keys.shape
    query_len = queries.shape[1]
    groups = queries.shape[2] // (kv_local * head_dim)
    row_count = query_len * groups
    query_rows = (
        queries[0]
        .reshape(query_len, kv_local, groups, head_dim)
        .transpose(1, 0, 2, 3)
        .reshape(kv_local, row_count, head_dim)
    )
    own_keys = request_keys[0].reshape(query_len, kv_local, head_dim).transpose(1, 0, 2)
    own_values = request_values[0].reshape(query_len, kv_local, head_dim).transpose(1, 0, 2)
    query_token = jnp.arange(row_count) // groups
    causal = jnp.arange(query_len)[None, :] <= query_token[:, None]
    state = (
        jnp.full((kv_local, row_count), -jnp.inf, jnp.float32),
        jnp.zeros((kv_local, row_count), jnp.float32),
        jnp.zeros((kv_local, row_count, head_dim), jnp.float32),
    )
    state = absorb(state, query_rows, own_keys, own_values, causal)
    slots = passage_ids[0]
    offsets = passage_order[0] * pass_len
    piece_keys = lax.all_gather(cache_keys, "pool", axis=0, tiled=True)
    piece_values = lax.all_gather(cache_values, "pool", axis=0, tiled=True)

    def visit_one(position, current):
        matches = slots == position
        offset = jnp.sum(jnp.where(matches, offsets, 0))

        def absorb_one(inner):
            placed = reposition(piece_keys[position].astype(jnp.float32), offset, head_dim).astype(
                jnp.bfloat16
            )
            return absorb(inner, query_rows, placed, piece_values[position], None)

        return lax.cond(jnp.any(matches), absorb_one, lambda inner: inner, current)

    state = lax.fori_loop(0, piece_keys.shape[0], visit_one, state)
    running_peak, running_total, running_sum = state
    attended = (running_sum / running_total[..., None]).astype(jnp.bfloat16)
    attended = (
        attended.reshape(kv_local, query_len, groups, head_dim)
        .transpose(1, 0, 2, 3)
        .reshape(query_len, kv_local * groups * head_dim)
    )
    partial_value = jnp.dot(
        attended,
        lax.all_gather(out_weight, "pool", axis=0, tiled=True),
        preferred_element_type=jnp.float32,
    )
    summed = lax.psum_scatter(
        partial_value.astype(jnp.bfloat16), "head", scatter_dimension=1, tiled=True
    )
    return summed[None]


def ring_order(chips):
    columns = chips // ROWS
    cells = []
    for row in range(ROWS):
        across = range(1, columns) if row % 2 == 0 else range(columns - 1, 0, -1)
        cells += [row * columns + column for column in across]
    return cells + [row * columns for row in reversed(range(ROWS))]


def shift(value, order, step):
    chips = len(order)
    pairs = [
        (order[at] * CORES + core, order[(at + step) % chips] * CORES + core)
        for at in range(chips)
        for core in range(CORES)
    ]
    return lax.ppermute(value, "pool", pairs)


def onward(pieces, step, order):
    chips = len(order)
    pieces[step] = shift(pieces[step - 1], order, 1)
    pieces[chips - step] = shift(pieces[(chips - step + 1) % chips], order, -1)


def after(value, *earlier):
    return lax.optimization_barrier((value, earlier))[0]


def swap_core(value, pool):
    return lax.ppermute(value, "pool", [(at, at ^ 1) for at in range(pool)])


def swap_plane(value):
    return lax.ppermute(value, "head", [(0, 1), (1, 0)])


def holder(ring, me, back):
    chips = ring.shape[0] // 2
    chip = lax.div(me[0], CORES)
    place = lax.rem(ring[chips + chip] + chips - back, chips)
    return ring[place] * CORES + lax.rem(me[0], CORES)


def attend_kernel(pieces, owned, ids, ranks, ring, me, queries, cosine, sine, *refs):
    key_pieces, value_pieces, refs = refs[:pieces], refs[pieces : 2 * pieces], refs[2 * pieces :]
    near = refs[:-8]
    sums, stats, keys, values, within, rank_of, key_sem, value_sem = refs[-8:]
    slots = ids.shape[0]
    kv_local, _, head_dim = keys.shape
    length = key_pieces[0].shape[2]
    tokens = queries.shape[0]
    groups = queries.shape[1] // (kv_local * head_dim)
    heads = kv_local * groups
    factor = math.log2(math.e) / math.sqrt(head_dim)
    across = (((1,), (1,)), ((), ()))

    for slot in range(slots):
        passage = ids[slot]
        home = lax.div(passage, owned)
        within[home] = passage - home * owned
        rank_of[home] = ranks[slot]
    homes = [holder(ring, me, piece) for piece in range(pieces)]

    def copy(source, target, sem, piece):
        rows = pl.ds(piece * length, length)
        return pltpu.make_async_copy(
            source[piece].at[within[homes[piece]]], target.at[:, rows], sem.at[piece]
        )

    key_copies = [copy(key_pieces, keys, key_sem, piece) for piece in range(pieces)]
    value_copies = [copy(value_pieces, values, value_sem, piece) for piece in range(pieces)]
    for each in key_copies + value_copies:
        each.start()
    for piece in range(pieces):
        key_copies[piece].wait()
        rank = rank_of[homes[piece]]
        cos = cosine[pl.ds(rank, 1), :]
        sin = sine[pl.ds(rank, 1), :]
        rows = pl.ds(piece * length, length)
        for head in range(kv_local):
            block = keys[head, rows, :].astype(jnp.float32)
            turned = block * cos + pltpu.roll(block, head_dim // 2, 1) * sin
            keys[head, rows, :] = turned.astype(jnp.bfloat16)
    for each in value_copies:
        each.wait()

    lane = lax.broadcasted_iota(jnp.int32, (tokens, LANES), 1)
    marks = jnp.zeros((tokens, LANES), jnp.float32)
    for head in range(kv_local):
        spans = [
            slice((head * groups + g) * head_dim, (head * groups + g + 1) * head_dim)
            for g in range(groups)
        ]
        rows = jnp.concatenate([queries[:, span] for span in spans], axis=0)
        scores = lax.dot_general(rows, keys[head], across, preferred_element_type=jnp.float32)
        peak = jnp.max(scores, axis=1, keepdims=True)
        if near:
            own = slice(head * head_dim, (head + 1) * head_dim)
            close = lax.dot_general(
                rows, near[0][:, own], across, preferred_element_type=jnp.float32
            )
            token = lax.rem(lax.broadcasted_iota(jnp.int32, close.shape, 0), tokens)
            column = lax.broadcasted_iota(jnp.int32, close.shape, 1)
            close = jnp.where(column <= token, close, -jnp.inf)
            peak = jnp.maximum(peak, jnp.max(close, axis=1, keepdims=True))
        exponent = jnp.exp2((scores - peak) * factor)
        total = jnp.sum(exponent, axis=1, keepdims=True)
        summed = jnp.dot(
            exponent.astype(jnp.bfloat16), values[head], preferred_element_type=jnp.float32
        )
        if near:
            exponent = jnp.exp2((close - peak) * factor)
            total = total + jnp.sum(exponent, axis=1, keepdims=True)
            summed = summed + jnp.dot(
                exponent.astype(jnp.bfloat16), near[1][:, own], preferred_element_type=jnp.float32
            )
        for g in range(groups):
            part = slice(g * tokens, (g + 1) * tokens)
            sums[:, spans[g]] = summed[part]
            at = head * groups + g
            marks = jnp.where(lane == at, peak[part], marks)
            marks = jnp.where(lane == heads + at, total[part], marks)
    stats[...] = marks


def attend(ids, ranks, ring, me, queries, tables, near, passages):
    pieces = len(passages[0])
    key_pieces, value_pieces = passages
    owned, kv_local, length, head_dim = key_pieces[0].shape
    tokens, features = queries.shape
    holders = ids.shape[0]
    smem = pl.BlockSpec(memory_space=pltpu.SMEM)
    vmem = pl.BlockSpec(memory_space=pltpu.VMEM)
    seen = pieces * length
    scores = tokens * (features // head_dim) * (seen + (length if near else 0))
    return pl.pallas_call(
        functools.partial(attend_kernel, pieces, owned),
        out_shape=[
            jax.ShapeDtypeStruct((tokens, features), jnp.float32),
            jax.ShapeDtypeStruct((tokens, LANES), jnp.float32),
        ],
        in_specs=[smem] * 4
        + [vmem] * 3
        + [pl.BlockSpec(memory_space=pl.ANY)] * (2 * pieces)
        + [vmem] * len(near),
        out_specs=[vmem] * 2,
        scratch_shapes=[
            pltpu.VMEM((kv_local, seen, head_dim), jnp.bfloat16),
            pltpu.VMEM((kv_local, seen, head_dim), jnp.bfloat16),
            pltpu.SMEM((holders,), jnp.int32),
            pltpu.SMEM((holders,), jnp.int32),
            pltpu.SemaphoreType.DMA((pieces,)),
            pltpu.SemaphoreType.DMA((pieces,)),
        ],
        compiler_params=pltpu.CompilerParams(vmem_limit_bytes=32 * MIB),
        cost_estimate=pl.CostEstimate(
            flops=4 * scores * head_dim, bytes_accessed=4 * MIB, transcendentals=scores
        ),
        name="attend",
    )(ids, ranks, ring, me, queries, *tables, *key_pieces, *value_pieces, *near)


def combine_kernel(head_dim, sums, stats, sums_in, stats_in, attended):
    heads = sums.shape[1] // head_dim
    factor = math.log2(math.e) / math.sqrt(head_dim)
    for head in range(heads):
        columns = slice(head * head_dim, (head + 1) * head_dim)
        peak_a, peak_b = stats[:, head : head + 1], stats_in[:, head : head + 1]
        at = heads + head
        total_a, total_b = stats[:, at : at + 1], stats_in[:, at : at + 1]
        peak = jnp.maximum(peak_a, peak_b)
        part_a = jnp.exp2((peak_a - peak) * factor)
        part_b = jnp.exp2((peak_b - peak) * factor)
        total = total_a * part_a + total_b * part_b
        value = sums[:, columns] * part_a + sums_in[:, columns] * part_b
        attended[:, columns] = (value / total).astype(attended.dtype)


def combine(head_dim, sums, stats, sums_in, stats_in):
    vmem = pl.BlockSpec(memory_space=pltpu.VMEM)
    return pl.pallas_call(
        functools.partial(combine_kernel, head_dim),
        out_shape=jax.ShapeDtypeStruct(sums.shape, jnp.bfloat16),
        in_specs=[vmem] * 4,
        out_specs=vmem,
        compiler_params=pltpu.CompilerParams(vmem_limit_bytes=24 * MIB),
        cost_estimate=pl.CostEstimate(
            flops=4 * sums.size, bytes_accessed=10 * sums.size, transcendentals=0
        ),
        name="combine",
    )(sums, stats, sums_in, stats_in)


def project_kernel(places, based, ring, me, own_rows, other_rows, *refs):
    count = len(places)
    blocks, refs = refs[: 2 * count], refs[2 * count :]
    base = None
    if based:
        base, refs = refs[0], refs[1:]
    results, (held, total, sems) = refs[:-3], refs[-3:]
    planes, span, _ = held.shape[1:]
    copies = [
        pltpu.make_async_copy(block, held.at[at], sems.at[at]) for at, block in enumerate(blocks)
    ]
    for copy in copies:
        copy.start()
    for at, place in enumerate(places):
        home = holder(ring, me, place)
        left, right = [], []
        for part, source in enumerate((home, home + 1 - 2 * lax.rem(home, CORES))):
            copies[2 * at + part].wait()
            first = pl.multiple_of(source * span, span)
            for plane, rows in enumerate((own_rows, other_rows)):
                left.append(rows[:, pl.ds(first, span)])
                right.append(held[2 * at + part, plane])
        value = jnp.dot(
            jnp.concatenate(left, axis=1),
            jnp.concatenate(right, axis=0),
            preferred_element_type=jnp.float32,
        )
        if at:
            value = value + total[...]
        elif base is not None:
            value = value + base[...]
        if at + 1 < count:
            total[...] = value
    tokens = results[0].shape[0]
    for part, result in enumerate(results):
        result[...] = value[part * tokens : (part + 1) * tokens].astype(result.dtype)


def project(ring, me, rows, places, weights, base, shapes):
    blocks = [half[place] for place in places for half in weights]
    tokens = rows[0].shape[0]
    planes, span, width = blocks[0].shape
    smem = pl.BlockSpec(memory_space=pltpu.SMEM)
    vmem = pl.BlockSpec(memory_space=pltpu.VMEM)
    return pl.pallas_call(
        functools.partial(project_kernel, tuple(places), base is not None),
        out_shape=shapes,
        in_specs=[smem] * 2
        + [vmem] * 2
        + [pl.BlockSpec(memory_space=pl.ANY)] * len(blocks)
        + ([vmem] if base is not None else []),
        out_specs=[vmem] * len(shapes),
        scratch_shapes=[
            pltpu.VMEM((len(blocks), planes, span, width), jnp.bfloat16),
            pltpu.VMEM((tokens, width), jnp.float32),
            pltpu.SemaphoreType.DMA((len(blocks),)),
        ],
        compiler_params=pltpu.CompilerParams(vmem_limit_bytes=32 * MIB),
        cost_estimate=pl.CostEstimate(
            flops=2 * len(blocks) * planes * tokens * span * width,
            bytes_accessed=2 * len(blocks) * planes * span * width + 4 * tokens * width,
            transcendentals=0,
        ),
        name="project",
    )(ring, me, *rows, *blocks, *([base] if base is not None else []))


def rotation_tables(ranks, length, head_dim):
    offsets = (jnp.arange(ranks) * length).astype(jnp.float32)
    angles = offsets[:, None] * frequency_table(head_dim)[None, :]
    cosine, sine = jnp.cos(angles), jnp.sin(angles)
    return (
        jnp.concatenate([cosine, cosine], axis=1),
        jnp.concatenate([-sine, sine], axis=1),
    )


def ring_body(
    pool,
    queries,
    request_keys,
    request_values,
    cache_keys,
    cache_values,
    passage_ids,
    passage_order,
    out_weight,
):
    _, _, pass_len, head_dim = cache_keys.shape
    tokens = queries.shape[1]
    chips = pool // CORES
    half = chips // 2
    order = ring_order(chips)
    ring = jnp.asarray(order + [order.index(chip) for chip in range(chips)], jnp.int32)
    index = lax.axis_index("pool")
    me = jnp.reshape(index, (1,))
    core = lax.rem(index, CORES)
    plane = lax.axis_index("head")

    span = out_weight.shape[1] // 2
    width = span // CORES
    leaving = lax.dynamic_slice_in_dim(out_weight, (1 - plane) * span, span, axis=1)
    cache_keys, cache_values, leaving = lax.optimization_barrier(
        (cache_keys, cache_values, leaving)
    )
    across = swap_plane(leaving)

    kept = {0: cache_keys}, {0: cache_values}
    for pieces in kept:
        onward(pieces, 1, order)
    across, kept[1][1], kept[1][chips - 1] = lax.optimization_barrier(
        (across, kept[1][1], kept[1][chips - 1])
    )
    for step in range(2, half):
        for pieces in kept:
            onward(pieces, step, order)

    out_weight, across, queries, picks = after(
        (out_weight, across, queries[0], jnp.concatenate([passage_ids, passage_order], axis=0)),
        *[pieces[at] for pieces in kept for at in (2, chips - 2)],
    )

    def columns(to_core):
        first = to_core * width
        return jnp.stack(
            [
                lax.dynamic_slice_in_dim(out_weight, plane * span + first, width, axis=1),
                lax.dynamic_slice_in_dim(across, first, width, axis=1),
            ]
        )

    near, far = heavy = {0: columns(core)}, {0: swap_core(columns(1 - core), pool)}
    for step in range(1, half):
        for pieces in heavy:
            onward(pieces, step, order)

    kept[0][half] = shift(kept[0][half - 1], order, 1)
    kept[1][half] = shift(kept[1][half + 1], order, -1)
    passages = [[pieces[at] for at in range(chips)] for pieces in kept]

    picks_in = swap_core(picks, pool)
    other_queries = after(
        swap_core(queries, pool), *[pieces[at] for pieces in heavy for at in (1, chips - 1)]
    )
    tables = rotation_tables(passage_ids.shape[1], pass_len, head_dim)
    other = attend(picks_in[0], picks_in[1], ring, me, other_queries, tables, (), passages)
    own_block = (request_keys[0], request_values[0])
    own = attend(picks[0], picks[1], ring, me, queries, tables, own_block, passages)
    other, own = after(
        (other, own), *[pieces[at] for pieces in heavy for at in (2, chips - 2)]
    )
    other_in = [swap_core(value, pool) for value in other]

    attended = combine(head_dim, *own, *other_in)
    turned = after(
        swap_plane(attended), *[pieces[at] for pieces in heavy for at in (3, chips - 3)]
    )
    rows = []
    for value in (attended, turned):
        rows.append(jnp.concatenate([value, swap_core(value, pool)], axis=0))

    near[half] = shift(near[half - 1], order, 1)
    far[half] = shift(far[half + 1], order, -1)
    sums = [jax.ShapeDtypeStruct((CORES * tokens, width), jnp.float32)]
    weights = (near, far)
    early = [0] + [at for step in range(1, half - 1) for at in (step, chips - step)]
    total = project(ring, me, rows, early, weights, None, sums)[0]
    total = project(ring, me, rows, [half - 1, half + 1], weights, total, sums)[0]
    own_out, other_out = project(
        ring, me, rows, [half], weights, total, [jax.ShapeDtypeStruct((tokens, width), jnp.bfloat16)] * 2
    )
    beside = swap_core(other_out, pool)
    result = jnp.where(
        core == 0,
        jnp.concatenate([own_out, beside], axis=1),
        jnp.concatenate([beside, own_out], axis=1),
    )
    return result[None]


def solution(mesh):
    pool, heads_axis = mesh.shape["pool"], mesh.shape["head"]

    def body(*args):
        weight = args[-1]
        tiled = weight.shape[0] % LANES == 0 and weight.shape[1] % (2 * CORES * LANES) == 0
        if tiled and heads_axis == 2 and pool % (2 * ROWS * CORES) == 0:
            return ring_body(pool, *args)
        return plain_body(*args)

    placed = (
        P("pool", None, "head"),
        P("pool", None, "head"),
        P("pool", None, "head"),
        P("pool", "head", None, None),
        P("pool", "head", None, None),
        P("pool", None),
        P("pool", None),
        P(("head", "pool"), None),
    )
    return jax.shard_map(
        body, mesh=mesh, in_specs=placed, out_specs=P("pool", None, "head"), check_vma=False
    )
```

```python
import functools
import math

import jax
import jax.numpy as jnp
from jax import lax
from jax.experimental import pallas as pl
from jax.experimental.pallas import tpu as pltpu
from jax.sharding import PartitionSpec as P

CORES = 2
ROWS = 4
LANES = 128
MIB = 1024 * 1024


def frequency_table(head_dim):
    pair_index = jnp.arange(head_dim // 2, dtype=jnp.float32)
    return jnp.exp(pair_index * (-2.0 / head_dim) * jnp.log(jnp.float32(500000.0)))


def reposition(vectors, offset, head_dim):
    angles = offset.astype(jnp.float32) * frequency_table(head_dim)
    cosine = jnp.cos(angles)
    sine_term = jnp.sin(angles)
    front_half = vectors[..., : head_dim // 2]
    back_half = vectors[..., head_dim // 2 :]
    return jnp.concatenate(
        [front_half * cosine - back_half * sine_term, back_half * cosine + front_half * sine_term],
        axis=-1,
    )


def absorb(state, query_rows, keys_block, values_block, allowed):
    running_peak, running_total, running_sum = state
    scores = jnp.einsum(
        "hrd,hnd->hrn", query_rows, keys_block, preferred_element_type=jnp.float32
    ) * query_rows.shape[2] ** (-0.5)
    if allowed is not None:
        scores = jnp.where(allowed[None], scores, -jnp.inf)
    new_peak = jnp.maximum(running_peak, jnp.max(scores, axis=-1))
    factor = jnp.exp(running_peak - new_peak)
    exponent = jnp.exp(scores - new_peak[..., None])
    weights = exponent.astype(jnp.bfloat16)
    new_total = running_total * factor + jnp.sum(exponent, axis=-1)
    new_sum = running_sum * factor[..., None] + jnp.einsum(
        "hrn,hnd->hrd", weights, values_block, preferred_element_type=jnp.float32
    )
    return (new_peak, new_total, new_sum)


def plain_body(
    queries,
    request_keys,
    request_values,
    cache_keys,
    cache_values,
    passage_ids,
    passage_order,
    out_weight,
):
    owned, kv_local, pass_len, head_dim = cache_keys.shape
    query_len = queries.shape[1]
    groups = queries.shape[2] // (kv_local * head_dim)
    row_count = query_len * groups
    query_rows = (
        queries[0]
        .reshape(query_len, kv_local, groups, head_dim)
        .transpose(1, 0, 2, 3)
        .reshape(kv_local, row_count, head_dim)
    )
    own_keys = request_keys[0].reshape(query_len, kv_local, head_dim).transpose(1, 0, 2)
    own_values = request_values[0].reshape(query_len, kv_local, head_dim).transpose(1, 0, 2)
    query_token = jnp.arange(row_count) // groups
    causal = jnp.arange(query_len)[None, :] <= query_token[:, None]
    state = (
        jnp.full((kv_local, row_count), -jnp.inf, jnp.float32),
        jnp.zeros((kv_local, row_count), jnp.float32),
        jnp.zeros((kv_local, row_count, head_dim), jnp.float32),
    )
    state = absorb(state, query_rows, own_keys, own_values, causal)
    slots = passage_ids[0]
    offsets = passage_order[0] * pass_len
    piece_keys = lax.all_gather(cache_keys, "pool", axis=0, tiled=True)
    piece_values = lax.all_gather(cache_values, "pool", axis=0, tiled=True)

    def visit_one(position, current):
        matches = slots == position
        offset = jnp.sum(jnp.where(matches, offsets, 0))

        def absorb_one(inner):
            placed = reposition(piece_keys[position].astype(jnp.float32), offset, head_dim).astype(
                jnp.bfloat16
            )
            return absorb(inner, query_rows, placed, piece_values[position], None)

        return lax.cond(jnp.any(matches), absorb_one, lambda inner: inner, current)

    state = lax.fori_loop(0, piece_keys.shape[0], visit_one, state)
    running_peak, running_total, running_sum = state
    attended = (running_sum / running_total[..., None]).astype(jnp.bfloat16)
    attended = (
        attended.reshape(kv_local, query_len, groups, head_dim)
        .transpose(1, 0, 2, 3)
        .reshape(query_len, kv_local * groups * head_dim)
    )
    partial_value = jnp.dot(
        attended,
        lax.all_gather(out_weight, "pool", axis=0, tiled=True),
        preferred_element_type=jnp.float32,
    )
    summed = lax.psum_scatter(
        partial_value.astype(jnp.bfloat16), "head", scatter_dimension=1, tiled=True
    )
    return summed[None]


def ring_order(chips):
    columns = chips // ROWS
    cells = []
    for row in range(ROWS):
        across = range(1, columns) if row % 2 == 0 else range(columns - 1, 0, -1)
        cells += [row * columns + column for column in across]
    return cells + [row * columns for row in reversed(range(ROWS))]


def shift(value, order, step):
    chips = len(order)
    pairs = [
        (order[at] * CORES + core, order[(at + step) % chips] * CORES + core)
        for at in range(chips)
        for core in range(CORES)
    ]
    return lax.ppermute(value, "pool", pairs)


def onward(pieces, step, order):
    chips = len(order)
    pieces[step] = shift(pieces[step - 1], order, 1)
    pieces[chips - step] = shift(pieces[(chips - step + 1) % chips], order, -1)


def after(value, *earlier):
    return lax.optimization_barrier((value, earlier))[0]


def swap_core(value, pool):
    return lax.ppermute(value, "pool", [(at, at ^ 1) for at in range(pool)])


def swap_plane(value):
    return lax.ppermute(value, "head", [(0, 1), (1, 0)])


def holder(ring, me, back):
    chips = ring.shape[0] // 2
    chip = lax.div(me[0], CORES)
    place = lax.rem(ring[chips + chip] + chips - back, chips)
    return ring[place] * CORES + lax.rem(me[0], CORES)


def attend_kernel(pieces, owned, ids, ranks, ring, me, queries, cosine, sine, *refs):
    key_pieces, value_pieces, refs = refs[:pieces], refs[pieces : 2 * pieces], refs[2 * pieces :]
    near = refs[:-8]
    sums, stats, keys, values, within, rank_of, key_sem, value_sem = refs[-8:]
    slots = ids.shape[0]
    kv_local, _, head_dim = keys.shape
    length = key_pieces[0].shape[2]
    tokens = queries.shape[0]
    groups = queries.shape[1] // (kv_local * head_dim)
    heads = kv_local * groups
    factor = math.log2(math.e) / math.sqrt(head_dim)
    across = (((1,), (1,)), ((), ()))

    for slot in range(slots):
        passage = ids[slot]
        home = lax.div(passage, owned)
        within[home] = passage - home * owned
        rank_of[home] = ranks[slot]
    homes = [holder(ring, me, piece) for piece in range(pieces)]

    def copy(source, target, sem, piece):
        rows = pl.ds(piece * length, length)
        return pltpu.make_async_copy(
            source[piece].at[within[homes[piece]]], target.at[:, rows], sem.at[piece]
        )

    key_copies = [copy(key_pieces, keys, key_sem, piece) for piece in range(pieces)]
    value_copies = [copy(value_pieces, values, value_sem, piece) for piece in range(pieces)]
    for each in key_copies + value_copies:
        each.start()
    for piece in range(pieces):
        key_copies[piece].wait()
        rank = rank_of[homes[piece]]
        cos = cosine[pl.ds(rank, 1), :]
        sin = sine[pl.ds(rank, 1), :]
        rows = pl.ds(piece * length, length)
        for head in range(kv_local):
            block = keys[head, rows, :].astype(jnp.float32)
            turned = block * cos + pltpu.roll(block, head_dim // 2, 1) * sin
            keys[head, rows, :] = turned.astype(jnp.bfloat16)
    for each in value_copies:
        each.wait()

    lane = lax.broadcasted_iota(jnp.int32, (tokens, LANES), 1)
    marks = jnp.zeros((tokens, LANES), jnp.float32)
    for head in range(kv_local):
        spans = [
            slice((head * groups + g) * head_dim, (head * groups + g + 1) * head_dim)
            for g in range(groups)
        ]
        rows = jnp.concatenate([queries[:, span] for span in spans], axis=0)
        scores = lax.dot_general(rows, keys[head], across, preferred_element_type=jnp.float32)
        peak = jnp.max(scores, axis=1, keepdims=True)
        if near:
            own = slice(head * head_dim, (head + 1) * head_dim)
            close = lax.dot_general(
                rows, near[0][:, own], across, preferred_element_type=jnp.float32
            )
            token = lax.rem(lax.broadcasted_iota(jnp.int32, close.shape, 0), tokens)
            column = lax.broadcasted_iota(jnp.int32, close.shape, 1)
            close = jnp.where(column <= token, close, -jnp.inf)
            peak = jnp.maximum(peak, jnp.max(close, axis=1, keepdims=True))
        exponent = jnp.exp2((scores - peak) * factor)
        total = jnp.sum(exponent, axis=1, keepdims=True)
        summed = jnp.dot(
            exponent.astype(jnp.bfloat16), values[head], preferred_element_type=jnp.float32
        )
        if near:
            exponent = jnp.exp2((close - peak) * factor)
            total = total + jnp.sum(exponent, axis=1, keepdims=True)
            summed = summed + jnp.dot(
                exponent.astype(jnp.bfloat16), near[1][:, own], preferred_element_type=jnp.float32
            )
        for g in range(groups):
            part = slice(g * tokens, (g + 1) * tokens)
            sums[:, spans[g]] = summed[part]
            at = head * groups + g
            marks = jnp.where(lane == at, peak[part], marks)
            marks = jnp.where(lane == heads + at, total[part], marks)
    stats[...] = marks


def attend(ids, ranks, ring, me, queries, tables, near, passages):
    pieces = len(passages[0])
    key_pieces, value_pieces = passages
    owned, kv_local, length, head_dim = key_pieces[0].shape
    tokens, features = queries.shape
    holders = ids.shape[0]
    smem = pl.BlockSpec(memory_space=pltpu.SMEM)
    vmem = pl.BlockSpec(memory_space=pltpu.VMEM)
    seen = pieces * length
    scores = tokens * (features // head_dim) * (seen + (length if near else 0))
    return pl.pallas_call(
        functools.partial(attend_kernel, pieces, owned),
        out_shape=[
            jax.ShapeDtypeStruct((tokens, features), jnp.float32),
            jax.ShapeDtypeStruct((tokens, LANES), jnp.float32),
        ],
        in_specs=[smem] * 4
        + [vmem] * 3
        + [pl.BlockSpec(memory_space=pl.ANY)] * (2 * pieces)
        + [vmem] * len(near),
        out_specs=[vmem] * 2,
        scratch_shapes=[
            pltpu.VMEM((kv_local, seen, head_dim), jnp.bfloat16),
            pltpu.VMEM((kv_local, seen, head_dim), jnp.bfloat16),
            pltpu.SMEM((holders,), jnp.int32),
            pltpu.SMEM((holders,), jnp.int32),
            pltpu.SemaphoreType.DMA((pieces,)),
            pltpu.SemaphoreType.DMA((pieces,)),
        ],
        compiler_params=pltpu.CompilerParams(vmem_limit_bytes=32 * MIB),
        cost_estimate=pl.CostEstimate(
            flops=4 * scores * head_dim, bytes_accessed=4 * MIB, transcendentals=scores
        ),
        name="attend",
    )(ids, ranks, ring, me, queries, *tables, *key_pieces, *value_pieces, *near)


def combine_kernel(head_dim, sums, stats, sums_in, stats_in, attended):
    heads = sums.shape[1] // head_dim
    factor = math.log2(math.e) / math.sqrt(head_dim)
    for head in range(heads):
        columns = slice(head * head_dim, (head + 1) * head_dim)
        peak_a, peak_b = stats[:, head : head + 1], stats_in[:, head : head + 1]
        at = heads + head
        total_a, total_b = stats[:, at : at + 1], stats_in[:, at : at + 1]
        peak = jnp.maximum(peak_a, peak_b)
        part_a = jnp.exp2((peak_a - peak) * factor)
        part_b = jnp.exp2((peak_b - peak) * factor)
        total = total_a * part_a + total_b * part_b
        value = sums[:, columns] * part_a + sums_in[:, columns] * part_b
        attended[:, columns] = (value / total).astype(attended.dtype)


def combine(head_dim, sums, stats, sums_in, stats_in):
    vmem = pl.BlockSpec(memory_space=pltpu.VMEM)
    return pl.pallas_call(
        functools.partial(combine_kernel, head_dim),
        out_shape=jax.ShapeDtypeStruct(sums.shape, jnp.bfloat16),
        in_specs=[vmem] * 4,
        out_specs=vmem,
        compiler_params=pltpu.CompilerParams(vmem_limit_bytes=24 * MIB),
        cost_estimate=pl.CostEstimate(
            flops=4 * sums.size, bytes_accessed=10 * sums.size, transcendentals=0
        ),
        name="combine",
    )(sums, stats, sums_in, stats_in)


def project_kernel(places, based, ring, me, own_rows, other_rows, *refs):
    count = len(places)
    blocks, refs = refs[: 2 * count], refs[2 * count :]
    base = None
    if based:
        base, refs = refs[0], refs[1:]
    results, (held, total, sems) = refs[:-3], refs[-3:]
    planes, span, _ = held.shape[1:]
    copies = [
        pltpu.make_async_copy(block, held.at[at], sems.at[at]) for at, block in enumerate(blocks)
    ]
    for copy in copies:
        copy.start()
    for at, place in enumerate(places):
        home = holder(ring, me, place)
        left, right = [], []
        for part, source in enumerate((home, home + 1 - 2 * lax.rem(home, CORES))):
            copies[2 * at + part].wait()
            first = pl.multiple_of(source * span, span)
            for plane, rows in enumerate((own_rows, other_rows)):
                left.append(rows[:, pl.ds(first, span)])
                right.append(held[2 * at + part, plane])
        value = jnp.dot(
            jnp.concatenate(left, axis=1),
            jnp.concatenate(right, axis=0),
            preferred_element_type=jnp.float32,
        )
        if at:
            value = value + total[...]
        elif base is not None:
            value = value + base[...]
        if at + 1 < count:
            total[...] = value
    tokens = results[0].shape[0]
    for part, result in enumerate(results):
        result[...] = value[part * tokens : (part + 1) * tokens].astype(result.dtype)


def project(ring, me, rows, places, weights, base, shapes):
    blocks = [half[place] for place in places for half in weights]
    tokens = rows[0].shape[0]
    planes, span, width = blocks[0].shape
    smem = pl.BlockSpec(memory_space=pltpu.SMEM)
    vmem = pl.BlockSpec(memory_space=pltpu.VMEM)
    return pl.pallas_call(
        functools.partial(project_kernel, tuple(places), base is not None),
        out_shape=shapes,
        in_specs=[smem] * 2
        + [vmem] * 2
        + [pl.BlockSpec(memory_space=pl.ANY)] * len(blocks)
        + ([vmem] if base is not None else []),
        out_specs=[vmem] * len(shapes),
        scratch_shapes=[
            pltpu.VMEM((len(blocks), planes, span, width), jnp.bfloat16),
            pltpu.VMEM((tokens, width), jnp.float32),
            pltpu.SemaphoreType.DMA((len(blocks),)),
        ],
        compiler_params=pltpu.CompilerParams(vmem_limit_bytes=32 * MIB),
        cost_estimate=pl.CostEstimate(
            flops=2 * len(blocks) * planes * tokens * span * width,
            bytes_accessed=2 * len(blocks) * planes * span * width + 4 * tokens * width,
            transcendentals=0,
        ),
        name="project",
    )(ring, me, *rows, *blocks, *([base] if base is not None else []))


def rotation_tables(ranks, length, head_dim):
    offsets = (jnp.arange(ranks) * length).astype(jnp.float32)
    angles = offsets[:, None] * frequency_table(head_dim)[None, :]
    cosine, sine = jnp.cos(angles), jnp.sin(angles)
    return (
        jnp.concatenate([cosine, cosine], axis=1),
        jnp.concatenate([-sine, sine], axis=1),
    )


def ring_body(
    pool,
    queries,
    request_keys,
    request_values,
    cache_keys,
    cache_values,
    passage_ids,
    passage_order,
    out_weight,
):
    _, _, pass_len, head_dim = cache_keys.shape
    tokens = queries.shape[1]
    chips = pool // CORES
    half = chips // 2
    order = ring_order(chips)
    ring = jnp.asarray(order + [order.index(chip) for chip in range(chips)], jnp.int32)
    index = lax.axis_index("pool")
    me = jnp.reshape(index, (1,))
    core = lax.rem(index, CORES)
    plane = lax.axis_index("head")

    span = out_weight.shape[1] // 2
    width = span // CORES
    leaving = lax.dynamic_slice_in_dim(out_weight, (1 - plane) * span, span, axis=1)
    cache_keys, cache_values, leaving = lax.optimization_barrier(
        (cache_keys, cache_values, leaving)
    )
    across = swap_plane(leaving)

    kept = {0: cache_keys}, {0: cache_values}
    for pieces in kept:
        onward(pieces, 1, order)
    across, kept[1][1], kept[1][chips - 1] = lax.optimization_barrier(
        (across, kept[1][1], kept[1][chips - 1])
    )
    for step in range(2, half):
        for pieces in kept:
            onward(pieces, step, order)

    out_weight, across = after(
        (out_weight, across),
        *[kept[1][at] for at in (1, chips - 1)],
    )

    def columns(to_core):
        first = to_core * width
        return jnp.stack(
            [
                lax.dynamic_slice_in_dim(out_weight, plane * span + first, width, axis=1),
                lax.dynamic_slice_in_dim(across, first, width, axis=1),
            ]
        )

    near, far = heavy = {0: columns(core)}, {0: swap_core(columns(1 - core), pool)}
    near[0] = after(near[0], *[kept[1][at] for at in (2, chips - 2)])
    far[0] = after(far[0], *[kept[0][at] for at in (half - 1, half + 1)])
    for step in range(1, half):
        for pieces in heavy:
            onward(pieces, step, order)

    queries, picks, last_keys, last_values = after(
        (
            queries[0],
            jnp.concatenate([passage_ids, passage_order], axis=0),
            kept[0][half - 1],
            kept[1][half + 1],
        ),
        near[1],
        near[chips - 1],
        kept[1][half - 1],
        kept[0][half + 1],
    )
    kept[0][half] = shift(last_keys, order, 1)
    kept[1][half] = shift(last_values, order, -1)
    passages = [[pieces[at] for at in range(chips)] for pieces in kept]

    picks_in = swap_core(picks, pool)
    other_queries = after(
        swap_core(queries, pool), far[1], far[chips - 1]
    )
    tables = rotation_tables(passage_ids.shape[1], pass_len, head_dim)
    other = attend(picks_in[0], picks_in[1], ring, me, other_queries, tables, (), passages)
    own_block = (request_keys[0], request_values[0])
    own = attend(picks[0], picks[1], ring, me, queries, tables, own_block, passages)
    other_in = [swap_core(value, pool) for value in other]
    own = after(own, far[2], far[chips - 2], near[3], near[chips - 3])

    attended = combine(head_dim, *own, *other_in)
    turned = after(
        swap_plane(attended), far[3], far[chips - 3]
    )
    rows = []
    for value in (attended, turned):
        rows.append(jnp.concatenate([value, swap_core(value, pool)], axis=0))

    near[half] = shift(near[half - 1], order, 1)
    far[half] = shift(far[half + 1], order, -1)
    sums = [jax.ShapeDtypeStruct((CORES * tokens, width), jnp.float32)]
    weights = (near, far)
    early = [0] + [at for step in range(1, half - 1) for at in (step, chips - step)]
    total = project(ring, me, rows, early, weights, None, sums)[0]
    total = project(ring, me, rows, [half - 1, half + 1], weights, total, sums)[0]
    own_out, other_out = project(
        ring, me, rows, [half], weights, total, [jax.ShapeDtypeStruct((tokens, width), jnp.bfloat16)] * 2
    )
    beside = swap_core(other_out, pool)
    result = jnp.where(
        core == 0,
        jnp.concatenate([own_out, beside], axis=1),
        jnp.concatenate([beside, own_out], axis=1),
    )
    return result[None]


def solution(mesh):
    pool, heads_axis = mesh.shape["pool"], mesh.shape["head"]

    def body(*args):
        weight = args[-1]
        tiled = weight.shape[0] % LANES == 0 and weight.shape[1] % (2 * CORES * LANES) == 0
        if tiled and heads_axis == 2 and pool % (2 * ROWS * CORES) == 0:
            return ring_body(pool, *args)
        return plain_body(*args)

    placed = (
        P("pool", None, "head"),
        P("pool", None, "head"),
        P("pool", None, "head"),
        P("pool", "head", None, None),
        P("pool", "head", None, None),
        P("pool", None),
        P("pool", None),
        P(("head", "pool"), None),
    )
    return jax.shard_map(
        body, mesh=mesh, in_specs=placed, out_specs=P("pool", None, "head"), check_vma=False
    )
```

```python
import functools
import math

import jax
import jax.numpy as jnp
from jax import lax
from jax.experimental import pallas as pl
from jax.experimental.pallas import tpu as pltpu
from jax.sharding import PartitionSpec as P

CORES = 2
ROWS = 4
LANES = 128
MIB = 1024 * 1024


def frequency_table(head_dim):
    pair_index = jnp.arange(head_dim // 2, dtype=jnp.float32)
    return jnp.exp(pair_index * (-2.0 / head_dim) * jnp.log(jnp.float32(500000.0)))


def reposition(vectors, offset, head_dim):
    angles = offset.astype(jnp.float32) * frequency_table(head_dim)
    cosine = jnp.cos(angles)
    sine_term = jnp.sin(angles)
    front_half = vectors[..., : head_dim // 2]
    back_half = vectors[..., head_dim // 2 :]
    return jnp.concatenate(
        [front_half * cosine - back_half * sine_term, back_half * cosine + front_half * sine_term],
        axis=-1,
    )


def absorb(state, query_rows, keys_block, values_block, allowed):
    running_peak, running_total, running_sum = state
    scores = jnp.einsum(
        "hrd,hnd->hrn", query_rows, keys_block, preferred_element_type=jnp.float32
    ) * query_rows.shape[2] ** (-0.5)
    if allowed is not None:
        scores = jnp.where(allowed[None], scores, -jnp.inf)
    new_peak = jnp.maximum(running_peak, jnp.max(scores, axis=-1))
    factor = jnp.exp(running_peak - new_peak)
    exponent = jnp.exp(scores - new_peak[..., None])
    weights = exponent.astype(jnp.bfloat16)
    new_total = running_total * factor + jnp.sum(exponent, axis=-1)
    new_sum = running_sum * factor[..., None] + jnp.einsum(
        "hrn,hnd->hrd", weights, values_block, preferred_element_type=jnp.float32
    )
    return (new_peak, new_total, new_sum)


def plain_body(
    queries,
    request_keys,
    request_values,
    cache_keys,
    cache_values,
    passage_ids,
    passage_order,
    out_weight,
):
    owned, kv_local, pass_len, head_dim = cache_keys.shape
    query_len = queries.shape[1]
    groups = queries.shape[2] // (kv_local * head_dim)
    row_count = query_len * groups
    query_rows = (
        queries[0]
        .reshape(query_len, kv_local, groups, head_dim)
        .transpose(1, 0, 2, 3)
        .reshape(kv_local, row_count, head_dim)
    )
    own_keys = request_keys[0].reshape(query_len, kv_local, head_dim).transpose(1, 0, 2)
    own_values = request_values[0].reshape(query_len, kv_local, head_dim).transpose(1, 0, 2)
    query_token = jnp.arange(row_count) // groups
    causal = jnp.arange(query_len)[None, :] <= query_token[:, None]
    state = (
        jnp.full((kv_local, row_count), -jnp.inf, jnp.float32),
        jnp.zeros((kv_local, row_count), jnp.float32),
        jnp.zeros((kv_local, row_count, head_dim), jnp.float32),
    )
    state = absorb(state, query_rows, own_keys, own_values, causal)
    slots = passage_ids[0]
    offsets = passage_order[0] * pass_len
    piece_keys = lax.all_gather(cache_keys, "pool", axis=0, tiled=True)
    piece_values = lax.all_gather(cache_values, "pool", axis=0, tiled=True)

    def visit_one(position, current):
        matches = slots == position
        offset = jnp.sum(jnp.where(matches, offsets, 0))

        def absorb_one(inner):
            placed = reposition(piece_keys[position].astype(jnp.float32), offset, head_dim).astype(
                jnp.bfloat16
            )
            return absorb(inner, query_rows, placed, piece_values[position], None)

        return lax.cond(jnp.any(matches), absorb_one, lambda inner: inner, current)

    state = lax.fori_loop(0, piece_keys.shape[0], visit_one, state)
    running_peak, running_total, running_sum = state
    attended = (running_sum / running_total[..., None]).astype(jnp.bfloat16)
    attended = (
        attended.reshape(kv_local, query_len, groups, head_dim)
        .transpose(1, 0, 2, 3)
        .reshape(query_len, kv_local * groups * head_dim)
    )
    partial_value = jnp.dot(
        attended,
        lax.all_gather(out_weight, "pool", axis=0, tiled=True),
        preferred_element_type=jnp.float32,
    )
    summed = lax.psum_scatter(
        partial_value.astype(jnp.bfloat16), "head", scatter_dimension=1, tiled=True
    )
    return summed[None]


def ring_order(chips):
    columns = chips // ROWS
    cells = []
    for row in range(ROWS):
        across = range(1, columns) if row % 2 == 0 else range(columns - 1, 0, -1)
        cells += [row * columns + column for column in across]
    return cells + [row * columns for row in reversed(range(ROWS))]


def shift(value, order, step):
    chips = len(order)
    pairs = [
        (order[at] * CORES + core, order[(at + step) % chips] * CORES + core)
        for at in range(chips)
        for core in range(CORES)
    ]
    return lax.ppermute(value, "pool", pairs)


def onward(pieces, step, order):
    chips = len(order)
    pieces[step] = shift(pieces[step - 1], order, 1)
    pieces[chips - step] = shift(pieces[(chips - step + 1) % chips], order, -1)


def after(value, *earlier):
    return lax.optimization_barrier((value, earlier))[0]


def swap_core(value, pool):
    return lax.ppermute(value, "pool", [(at, at ^ 1) for at in range(pool)])


def swap_plane(value):
    return lax.ppermute(value, "head", [(0, 1), (1, 0)])


def holder(ring, me, back):
    chips = ring.shape[0] // 2
    chip = lax.div(me[0], CORES)
    place = lax.rem(ring[chips + chip] + chips - back, chips)
    return ring[place] * CORES + lax.rem(me[0], CORES)


def attend_kernel(pieces, owned, ids, ranks, ring, me, queries, cosine, sine, *refs):
    key_pieces, value_pieces, refs = refs[:pieces], refs[pieces : 2 * pieces], refs[2 * pieces :]
    stats, keys, values, within, rank_of, key_sem, value_sem = refs[-7:]
    slots = ids.shape[0]
    kv_local, _, head_dim = keys.shape
    near, sums = refs[: -7 - kv_local], refs[-7 - kv_local : -7]
    length = key_pieces[0].shape[2]
    tokens = queries.shape[0]
    groups = queries.shape[1] // (kv_local * head_dim)
    heads = kv_local * groups
    factor = math.log2(math.e) / math.sqrt(head_dim)
    across = (((1,), (1,)), ((), ()))

    for slot in range(slots):
        passage = ids[slot]
        home = lax.div(passage, owned)
        within[home] = passage - home * owned
        rank_of[home] = ranks[slot]
    homes = [holder(ring, me, piece) for piece in range(pieces)]

    def copy(source, target, sem, piece):
        rows = pl.ds(piece * length, length)
        return pltpu.make_async_copy(
            source[piece].at[within[homes[piece]]], target.at[:, rows], sem.at[piece]
        )

    key_copies = [copy(key_pieces, keys, key_sem, piece) for piece in range(pieces)]
    value_copies = [copy(value_pieces, values, value_sem, piece) for piece in range(pieces)]
    for each in key_copies + value_copies:
        each.start()
    for piece in range(pieces):
        key_copies[piece].wait()
        rank = rank_of[homes[piece]]
        cos = cosine[pl.ds(rank, 1), :]
        sin = sine[pl.ds(rank, 1), :]
        rows = pl.ds(piece * length, length)
        for head in range(kv_local):
            block = keys[head, rows, :].astype(jnp.float32)
            turned = block * cos + pltpu.roll(block, head_dim // 2, 1) * sin
            keys[head, rows, :] = turned.astype(jnp.bfloat16)
    for each in value_copies:
        each.wait()

    lane = lax.broadcasted_iota(jnp.int32, (tokens, LANES), 1)
    marks = jnp.zeros((tokens, LANES), jnp.float32)
    for head in range(kv_local):
        spans = [
            slice((head * groups + g) * head_dim, (head * groups + g + 1) * head_dim)
            for g in range(groups)
        ]
        rows = jnp.concatenate([queries[:, span] for span in spans], axis=0)
        scores = lax.dot_general(rows, keys[head], across, preferred_element_type=jnp.float32)
        peak = jnp.max(scores, axis=1, keepdims=True)
        if near:
            own = slice(head * head_dim, (head + 1) * head_dim)
            close = lax.dot_general(
                rows, near[0][:, own], across, preferred_element_type=jnp.float32
            )
            token = lax.rem(lax.broadcasted_iota(jnp.int32, close.shape, 0), tokens)
            column = lax.broadcasted_iota(jnp.int32, close.shape, 1)
            close = jnp.where(column <= token, close, -jnp.inf)
            peak = jnp.maximum(peak, jnp.max(close, axis=1, keepdims=True))
        exponent = jnp.exp2((scores - peak) * factor)
        total = jnp.sum(exponent, axis=1, keepdims=True)
        summed = jnp.dot(
            exponent.astype(jnp.bfloat16), values[head], preferred_element_type=jnp.float32
        )
        if near:
            exponent = jnp.exp2((close - peak) * factor)
            total = total + jnp.sum(exponent, axis=1, keepdims=True)
            summed = summed + jnp.dot(
                exponent.astype(jnp.bfloat16), near[1][:, own], preferred_element_type=jnp.float32
            )
        for g in range(groups):
            part = slice(g * tokens, (g + 1) * tokens)
            sums[head][:, g * head_dim : (g + 1) * head_dim] = summed[part]
            at = head * groups + g
            marks = jnp.where(lane == at, peak[part], marks)
            marks = jnp.where(lane == heads + at, total[part], marks)
    stats[...] = marks


def attend(ids, ranks, ring, me, queries, tables, near, passages):
    pieces = len(passages[0])
    key_pieces, value_pieces = passages
    owned, kv_local, length, head_dim = key_pieces[0].shape
    tokens, features = queries.shape
    holders = ids.shape[0]
    smem = pl.BlockSpec(memory_space=pltpu.SMEM)
    vmem = pl.BlockSpec(memory_space=pltpu.VMEM)
    seen = pieces * length
    scores = tokens * (features // head_dim) * (seen + (length if near else 0))
    return pl.pallas_call(
        functools.partial(attend_kernel, pieces, owned),
        out_shape=[jax.ShapeDtypeStruct((tokens, features // kv_local), jnp.float32)] * kv_local
        + [jax.ShapeDtypeStruct((tokens, LANES), jnp.float32)],
        in_specs=[smem] * 4
        + [vmem] * 3
        + [pl.BlockSpec(memory_space=pl.ANY)] * (2 * pieces)
        + [vmem] * len(near),
        out_specs=[vmem] * (kv_local + 1),
        scratch_shapes=[
            pltpu.VMEM((kv_local, seen, head_dim), jnp.bfloat16),
            pltpu.VMEM((kv_local, seen, head_dim), jnp.bfloat16),
            pltpu.SMEM((holders,), jnp.int32),
            pltpu.SMEM((holders,), jnp.int32),
            pltpu.SemaphoreType.DMA((pieces,)),
            pltpu.SemaphoreType.DMA((pieces,)),
        ],
        compiler_params=pltpu.CompilerParams(vmem_limit_bytes=32 * MIB),
        cost_estimate=pl.CostEstimate(
            flops=24 * scores * head_dim, bytes_accessed=4 * MIB, transcendentals=scores
        ),
        name="attend",
    )(ids, ranks, ring, me, queries, *tables, *key_pieces, *value_pieces, *near)


def combine_kernel(head_dim, *refs):
    attended, refs = refs[-1], refs[:-1]
    count = len(refs) // 2
    sums, stats = refs[: count - 1], refs[count - 1]
    sums_in, stats_in = refs[count:-1], refs[-1]
    groups = sums[0].shape[1] // head_dim
    heads = groups * len(sums)
    factor = math.log2(math.e) / math.sqrt(head_dim)
    for head in range(heads):
        block, at = divmod(head, groups)
        columns = slice(at * head_dim, (at + 1) * head_dim)
        peak_a, peak_b = stats[:, head : head + 1], stats_in[:, head : head + 1]
        at = heads + head
        total_a, total_b = stats[:, at : at + 1], stats_in[:, at : at + 1]
        peak = jnp.maximum(peak_a, peak_b)
        part_a = jnp.exp2((peak_a - peak) * factor)
        part_b = jnp.exp2((peak_b - peak) * factor)
        total = total_a * part_a + total_b * part_b
        value = sums[block][:, columns] * part_a + sums_in[block][:, columns] * part_b
        columns = slice(head * head_dim, (head + 1) * head_dim)
        attended[:, columns] = (value / total).astype(attended.dtype)


def combine(head_dim, state, state_in):
    tokens, width = state[0].shape
    size = tokens * width * (len(state) - 1)
    vmem = pl.BlockSpec(memory_space=pltpu.VMEM)
    return pl.pallas_call(
        functools.partial(combine_kernel, head_dim),
        out_shape=jax.ShapeDtypeStruct((tokens, size // tokens), jnp.bfloat16),
        in_specs=[vmem] * (2 * len(state)),
        out_specs=vmem,
        compiler_params=pltpu.CompilerParams(vmem_limit_bytes=24 * MIB),
        cost_estimate=pl.CostEstimate(flops=4 * size, bytes_accessed=10 * size, transcendentals=0),
        name="combine",
    )(*state, *state_in)


def project_kernel(places, based, ring, me, own_rows, other_rows, *refs):
    count = len(places)
    blocks, refs = refs[: 2 * count], refs[2 * count :]
    base = None
    if based:
        base, refs = refs[0], refs[1:]
    results, (held, total, sems) = refs[:-3], refs[-3:]
    planes, span, _ = held.shape[1:]
    copies = [
        pltpu.make_async_copy(block, held.at[at], sems.at[at]) for at, block in enumerate(blocks)
    ]
    for copy in copies:
        copy.start()
    for at, place in enumerate(places):
        home = holder(ring, me, place)
        left, right = [], []
        for part, source in enumerate((home, home + 1 - 2 * lax.rem(home, CORES))):
            copies[2 * at + part].wait()
            first = pl.multiple_of(source * span, span)
            for plane, rows in enumerate((own_rows, other_rows)):
                left.append(rows[:, pl.ds(first, span)])
                right.append(held[2 * at + part, plane])
        value = jnp.dot(
            jnp.concatenate(left, axis=1),
            jnp.concatenate(right, axis=0),
            preferred_element_type=jnp.float32,
        )
        if at:
            value = value + total[...]
        elif base is not None:
            value = value + base[...]
        if at + 1 < count:
            total[...] = value
    tokens = results[0].shape[0]
    for part, result in enumerate(results):
        result[...] = value[part * tokens : (part + 1) * tokens].astype(result.dtype)


def project(ring, me, rows, places, weights, base, shapes):
    blocks = [half[place] for place in places for half in weights]
    tokens = rows[0].shape[0]
    planes, span, width = blocks[0].shape
    smem = pl.BlockSpec(memory_space=pltpu.SMEM)
    vmem = pl.BlockSpec(memory_space=pltpu.VMEM)
    return pl.pallas_call(
        functools.partial(project_kernel, tuple(places), base is not None),
        out_shape=shapes,
        in_specs=[smem] * 2
        + [vmem] * 2
        + [pl.BlockSpec(memory_space=pl.ANY)] * len(blocks)
        + ([vmem] if base is not None else []),
        out_specs=[vmem] * len(shapes),
        scratch_shapes=[
            pltpu.VMEM((len(blocks), planes, span, width), jnp.bfloat16),
            pltpu.VMEM((tokens, width), jnp.float32),
            pltpu.SemaphoreType.DMA((len(blocks),)),
        ],
        compiler_params=pltpu.CompilerParams(vmem_limit_bytes=32 * MIB),
        cost_estimate=pl.CostEstimate(
            flops=2 * len(blocks) * planes * tokens * span * width,
            bytes_accessed=2 * len(blocks) * planes * span * width + 4 * tokens * width,
            transcendentals=0,
        ),
        name="project",
    )(ring, me, *rows, *blocks, *([base] if base is not None else []))


def rotation_tables(ranks, length, head_dim):
    offsets = (jnp.arange(ranks) * length).astype(jnp.float32)
    angles = offsets[:, None] * frequency_table(head_dim)[None, :]
    cosine, sine = jnp.cos(angles), jnp.sin(angles)
    return (
        jnp.concatenate([cosine, cosine], axis=1),
        jnp.concatenate([-sine, sine], axis=1),
    )


def ring_body(
    pool,
    queries,
    request_keys,
    request_values,
    cache_keys,
    cache_values,
    passage_ids,
    passage_order,
    out_weight,
):
    _, _, pass_len, head_dim = cache_keys.shape
    tokens = queries.shape[1]
    chips = pool // CORES
    half = chips // 2
    order = ring_order(chips)
    ring = jnp.asarray(order + [order.index(chip) for chip in range(chips)], jnp.int32)
    index = lax.axis_index("pool")
    me = jnp.reshape(index, (1,))
    core = lax.rem(index, CORES)
    plane = lax.axis_index("head")

    span = out_weight.shape[1] // 2
    width = span // CORES
    leaving = lax.dynamic_slice_in_dim(out_weight, (1 - plane) * span, span, axis=1)
    cache_keys, cache_values, leaving = lax.optimization_barrier(
        (cache_keys, cache_values, leaving)
    )
    across = swap_plane(leaving)

    kept = {0: cache_keys}, {0: cache_values}
    for pieces in kept:
        onward(pieces, 1, order)
    across, kept[1][1], kept[1][chips - 1] = lax.optimization_barrier(
        (across, kept[1][1], kept[1][chips - 1])
    )
    for step in range(2, half):
        for pieces in kept:
            onward(pieces, step, order)

    out_weight, across = after(
        (out_weight, across),
        *[kept[1][at] for at in (1, chips - 1)],
    )

    def columns(to_core):
        first = to_core * width
        return jnp.stack(
            [
                lax.dynamic_slice_in_dim(out_weight, plane * span + first, width, axis=1),
                lax.dynamic_slice_in_dim(across, first, width, axis=1),
            ]
        )

    near, far = heavy = {0: columns(core)}, {0: swap_core(columns(1 - core), pool)}
    near[0] = after(near[0], *[kept[1][at] for at in (2, chips - 2)])
    far[0] = after(far[0], *[kept[0][at] for at in (half - 1, half + 1)])
    for step in range(1, half):
        for pieces in heavy:
            onward(pieces, step, order)

    queries, picks, last_keys, last_values = after(
        (
            queries[0],
            jnp.concatenate([passage_ids, passage_order], axis=0),
            kept[0][half - 1],
            kept[1][half + 1],
        ),
        near[1],
        near[chips - 1],
    )
    kept[0][half] = shift(last_keys, order, 1)
    kept[1][half] = shift(last_values, order, -1)
    passages = [[pieces[at] for at in range(chips)] for pieces in kept]

    picks_in = swap_core(picks, pool)
    other_queries = after(
        swap_core(queries, pool), far[1], far[chips - 1]
    )
    tables = rotation_tables(passage_ids.shape[1], pass_len, head_dim)
    other = attend(picks_in[0], picks_in[1], ring, me, other_queries, tables, (), passages)
    own_block = (request_keys[0], request_values[0])
    other_in = [swap_core(value, pool) for value in other]
    queries, other_in = after((queries, other_in), near[2], near[chips - 2])
    own = attend(picks[0], picks[1], ring, me, queries, tables, own_block, passages)
    own = after(own, far[2], far[chips - 2], near[3], near[chips - 3])

    attended = combine(head_dim, own, other_in)
    turned = after(
        swap_plane(attended), far[3], far[chips - 3]
    )
    rows = []
    for value in (attended, turned):
        rows.append(jnp.concatenate([value, swap_core(value, pool)], axis=0))

    near[half] = shift(near[half - 1], order, 1)
    far[half] = shift(far[half + 1], order, -1)
    sums = [jax.ShapeDtypeStruct((CORES * tokens, width), jnp.float32)]
    weights = (near, far)
    early = [0] + [at for step in range(1, half - 1) for at in (step, chips - step)]
    total = project(ring, me, rows, early, weights, None, sums)[0]
    total = project(ring, me, rows, [half - 1, half + 1], weights, total, sums)[0]
    own_out, other_out = project(
        ring, me, rows, [half], weights, total, [jax.ShapeDtypeStruct((tokens, width), jnp.bfloat16)] * 2
    )
    beside = swap_core(other_out, pool)
    result = jnp.where(
        core == 0,
        jnp.concatenate([own_out, beside], axis=1),
        jnp.concatenate([beside, own_out], axis=1),
    )
    return result[None]


def solution(mesh):
    pool, heads_axis = mesh.shape["pool"], mesh.shape["head"]

    def body(*args):
        weight = args[-1]
        tiled = weight.shape[0] % LANES == 0 and weight.shape[1] % (2 * CORES * LANES) == 0
        if tiled and heads_axis == 2 and pool % (2 * ROWS * CORES) == 0:
            return ring_body(pool, *args)
        return plain_body(*args)

    placed = (
        P("pool", None, "head"),
        P("pool", None, "head"),
        P("pool", None, "head"),
        P("pool", "head", None, None),
        P("pool", "head", None, None),
        P("pool", None),
        P("pool", None),
        P(("head", "pool"), None),
    )
    return jax.shard_map(
        body, mesh=mesh, in_specs=placed, out_specs=P("pool", None, "head"), check_vma=False
    )
```

```python
import functools
import math

import jax
import jax.numpy as jnp
from jax import lax
from jax.experimental import pallas as pl
from jax.experimental.pallas import tpu as pltpu
from jax.sharding import PartitionSpec as P

CORES = 2
ROWS = 4
LANES = 128
MIB = 1024 * 1024


def frequency_table(head_dim):
    pair_index = jnp.arange(head_dim // 2, dtype=jnp.float32)
    return jnp.exp(pair_index * (-2.0 / head_dim) * jnp.log(jnp.float32(500000.0)))


def reposition(vectors, offset, head_dim):
    angles = offset.astype(jnp.float32) * frequency_table(head_dim)
    cosine = jnp.cos(angles)
    sine_term = jnp.sin(angles)
    front_half = vectors[..., : head_dim // 2]
    back_half = vectors[..., head_dim // 2 :]
    return jnp.concatenate(
        [front_half * cosine - back_half * sine_term, back_half * cosine + front_half * sine_term],
        axis=-1,
    )


def absorb(state, query_rows, keys_block, values_block, allowed):
    running_peak, running_total, running_sum = state
    scores = jnp.einsum(
        "hrd,hnd->hrn", query_rows, keys_block, preferred_element_type=jnp.float32
    ) * query_rows.shape[2] ** (-0.5)
    if allowed is not None:
        scores = jnp.where(allowed[None], scores, -jnp.inf)
    new_peak = jnp.maximum(running_peak, jnp.max(scores, axis=-1))
    factor = jnp.exp(running_peak - new_peak)
    exponent = jnp.exp(scores - new_peak[..., None])
    weights = exponent.astype(jnp.bfloat16)
    new_total = running_total * factor + jnp.sum(exponent, axis=-1)
    new_sum = running_sum * factor[..., None] + jnp.einsum(
        "hrn,hnd->hrd", weights, values_block, preferred_element_type=jnp.float32
    )
    return (new_peak, new_total, new_sum)


def plain_body(
    queries,
    request_keys,
    request_values,
    cache_keys,
    cache_values,
    passage_ids,
    passage_order,
    out_weight,
):
    owned, kv_local, pass_len, head_dim = cache_keys.shape
    query_len = queries.shape[1]
    groups = queries.shape[2] // (kv_local * head_dim)
    row_count = query_len * groups
    query_rows = (
        queries[0]
        .reshape(query_len, kv_local, groups, head_dim)
        .transpose(1, 0, 2, 3)
        .reshape(kv_local, row_count, head_dim)
    )
    own_keys = request_keys[0].reshape(query_len, kv_local, head_dim).transpose(1, 0, 2)
    own_values = request_values[0].reshape(query_len, kv_local, head_dim).transpose(1, 0, 2)
    query_token = jnp.arange(row_count) // groups
    causal = jnp.arange(query_len)[None, :] <= query_token[:, None]
    state = (
        jnp.full((kv_local, row_count), -jnp.inf, jnp.float32),
        jnp.zeros((kv_local, row_count), jnp.float32),
        jnp.zeros((kv_local, row_count, head_dim), jnp.float32),
    )
    state = absorb(state, query_rows, own_keys, own_values, causal)
    slots = passage_ids[0]
    offsets = passage_order[0] * pass_len
    piece_keys = lax.all_gather(cache_keys, "pool", axis=0, tiled=True)
    piece_values = lax.all_gather(cache_values, "pool", axis=0, tiled=True)

    def visit_one(position, current):
        matches = slots == position
        offset = jnp.sum(jnp.where(matches, offsets, 0))

        def absorb_one(inner):
            placed = reposition(piece_keys[position].astype(jnp.float32), offset, head_dim).astype(
                jnp.bfloat16
            )
            return absorb(inner, query_rows, placed, piece_values[position], None)

        return lax.cond(jnp.any(matches), absorb_one, lambda inner: inner, current)

    state = lax.fori_loop(0, piece_keys.shape[0], visit_one, state)
    running_peak, running_total, running_sum = state
    attended = (running_sum / running_total[..., None]).astype(jnp.bfloat16)
    attended = (
        attended.reshape(kv_local, query_len, groups, head_dim)
        .transpose(1, 0, 2, 3)
        .reshape(query_len, kv_local * groups * head_dim)
    )
    partial_value = jnp.dot(
        attended,
        lax.all_gather(out_weight, "pool", axis=0, tiled=True),
        preferred_element_type=jnp.float32,
    )
    summed = lax.psum_scatter(
        partial_value.astype(jnp.bfloat16), "head", scatter_dimension=1, tiled=True
    )
    return summed[None]


def ring_order(chips):
    columns = chips // ROWS
    cells = []
    for row in range(ROWS):
        across = range(1, columns) if row % 2 == 0 else range(columns - 1, 0, -1)
        cells += [row * columns + column for column in across]
    return cells + [row * columns for row in reversed(range(ROWS))]


def shift(value, order, step):
    chips = len(order)
    pairs = [
        (order[at] * CORES + core, order[(at + step) % chips] * CORES + core)
        for at in range(chips)
        for core in range(CORES)
    ]
    return lax.ppermute(value, "pool", pairs)


def onward(pieces, step, order):
    chips = len(order)
    pieces[step] = shift(pieces[step - 1], order, 1)
    pieces[chips - step] = shift(pieces[(chips - step + 1) % chips], order, -1)


def after(value, *earlier):
    return lax.optimization_barrier((value, earlier))[0]


def swap_core(value, pool):
    return lax.ppermute(value, "pool", [(at, at ^ 1) for at in range(pool)])


def swap_plane(value):
    return lax.ppermute(value, "head", [(0, 1), (1, 0)])


def holder(ring, me, back):
    chips = ring.shape[0] // 2
    chip = lax.div(me[0], CORES)
    place = lax.rem(ring[chips + chip] + chips - back, chips)
    return ring[place] * CORES + lax.rem(me[0], CORES)


def attend_kernel(pieces, owned, ids, ranks, ring, me, queries, cosine, sine, *refs):
    key_pieces, value_pieces, refs = refs[:pieces], refs[pieces : 2 * pieces], refs[2 * pieces :]
    stats, keys, values, within, rank_of, key_sem, value_sem = refs[-7:]
    slots = ids.shape[0]
    kv_local, _, head_dim = keys.shape
    near, sums = refs[: -7 - kv_local], refs[-7 - kv_local : -7]
    length = key_pieces[0].shape[2]
    tokens = queries.shape[0]
    groups = queries.shape[1] // (kv_local * head_dim)
    heads = kv_local * groups
    factor = math.log2(math.e) / math.sqrt(head_dim)
    across = (((1,), (1,)), ((), ()))

    for slot in range(slots):
        passage = ids[slot]
        home = lax.div(passage, owned)
        within[home] = passage - home * owned
        rank_of[home] = ranks[slot]
    homes = [holder(ring, me, piece) for piece in range(pieces)]

    def copy(source, target, sem, piece):
        rows = pl.ds(piece * length, length)
        return pltpu.make_async_copy(
            source[piece].at[within[homes[piece]]], target.at[:, rows], sem.at[piece]
        )

    key_copies = [copy(key_pieces, keys, key_sem, piece) for piece in range(pieces)]
    value_copies = [copy(value_pieces, values, value_sem, piece) for piece in range(pieces)]
    for each in key_copies + value_copies:
        each.start()
    for piece in range(pieces):
        key_copies[piece].wait()
        rank = rank_of[homes[piece]]
        cos = cosine[pl.ds(rank, 1), :]
        sin = sine[pl.ds(rank, 1), :]
        rows = pl.ds(piece * length, length)
        for head in range(kv_local):
            block = keys[head, rows, :].astype(jnp.float32)
            turned = block * cos + pltpu.roll(block, head_dim // 2, 1) * sin
            keys[head, rows, :] = turned.astype(jnp.bfloat16)
    for each in value_copies:
        each.wait()

    lane = lax.broadcasted_iota(jnp.int32, (tokens, LANES), 1)
    marks = jnp.zeros((tokens, LANES), jnp.float32)
    for head in range(kv_local):
        spans = [
            slice((head * groups + g) * head_dim, (head * groups + g + 1) * head_dim)
            for g in range(groups)
        ]
        rows = jnp.concatenate([queries[:, span] for span in spans], axis=0)
        scores = lax.dot_general(rows, keys[head], across, preferred_element_type=jnp.float32)
        peak = jnp.max(scores, axis=1, keepdims=True)
        if near:
            own = slice(head * head_dim, (head + 1) * head_dim)
            close = lax.dot_general(
                rows, near[0][:, own], across, preferred_element_type=jnp.float32
            )
            token = lax.rem(lax.broadcasted_iota(jnp.int32, close.shape, 0), tokens)
            column = lax.broadcasted_iota(jnp.int32, close.shape, 1)
            close = jnp.where(column <= token, close, -jnp.inf)
            peak = jnp.maximum(peak, jnp.max(close, axis=1, keepdims=True))
        exponent = jnp.exp2((scores - peak) * factor)
        total = jnp.sum(exponent, axis=1, keepdims=True)
        summed = jnp.dot(
            exponent.astype(jnp.bfloat16), values[head], preferred_element_type=jnp.float32
        )
        if near:
            exponent = jnp.exp2((close - peak) * factor)
            total = total + jnp.sum(exponent, axis=1, keepdims=True)
            summed = summed + jnp.dot(
                exponent.astype(jnp.bfloat16), near[1][:, own], preferred_element_type=jnp.float32
            )
        for g in range(groups):
            part = slice(g * tokens, (g + 1) * tokens)
            sums[head][:, g * head_dim : (g + 1) * head_dim] = summed[part]
            at = head * groups + g
            marks = jnp.where(lane == at, peak[part], marks)
            marks = jnp.where(lane == heads + at, total[part], marks)
    stats[...] = marks


def attend(ids, ranks, ring, me, queries, tables, near, passages):
    pieces = len(passages[0])
    key_pieces, value_pieces = passages
    owned, kv_local, length, head_dim = key_pieces[0].shape
    tokens, features = queries.shape
    holders = ids.shape[0]
    smem = pl.BlockSpec(memory_space=pltpu.SMEM)
    vmem = pl.BlockSpec(memory_space=pltpu.VMEM)
    seen = pieces * length
    scores = tokens * (features // head_dim) * (seen + (length if near else 0))
    return pl.pallas_call(
        functools.partial(attend_kernel, pieces, owned),
        out_shape=[jax.ShapeDtypeStruct((tokens, features // kv_local), jnp.float32)] * kv_local
        + [jax.ShapeDtypeStruct((tokens, LANES), jnp.float32)],
        in_specs=[smem] * 4
        + [vmem] * 3
        + [pl.BlockSpec(memory_space=pl.ANY)] * (2 * pieces)
        + [vmem] * len(near),
        out_specs=[vmem] * (kv_local + 1),
        scratch_shapes=[
            pltpu.VMEM((kv_local, seen, head_dim), jnp.bfloat16),
            pltpu.VMEM((kv_local, seen, head_dim), jnp.bfloat16),
            pltpu.SMEM((holders,), jnp.int32),
            pltpu.SMEM((holders,), jnp.int32),
            pltpu.SemaphoreType.DMA((pieces,)),
            pltpu.SemaphoreType.DMA((pieces,)),
        ],
        compiler_params=pltpu.CompilerParams(vmem_limit_bytes=32 * MIB),
        cost_estimate=pl.CostEstimate(
            flops=24 * scores * head_dim, bytes_accessed=4 * MIB, transcendentals=scores
        ),
        name="attend",
    )(ids, ranks, ring, me, queries, *tables, *key_pieces, *value_pieces, *near)


def combine_kernel(head_dim, *refs):
    attended, refs = refs[-1], refs[:-1]
    count = len(refs) // 2
    sums, stats = refs[: count - 1], refs[count - 1]
    sums_in, stats_in = refs[count:-1], refs[-1]
    groups = sums[0].shape[1] // head_dim
    heads = groups * len(sums)
    factor = math.log2(math.e) / math.sqrt(head_dim)
    for head in range(heads):
        block, at = divmod(head, groups)
        columns = slice(at * head_dim, (at + 1) * head_dim)
        peak_a, peak_b = stats[:, head : head + 1], stats_in[:, head : head + 1]
        at = heads + head
        total_a, total_b = stats[:, at : at + 1], stats_in[:, at : at + 1]
        peak = jnp.maximum(peak_a, peak_b)
        part_a = jnp.exp2((peak_a - peak) * factor)
        part_b = jnp.exp2((peak_b - peak) * factor)
        total = total_a * part_a + total_b * part_b
        value = sums[block][:, columns] * part_a + sums_in[block][:, columns] * part_b
        columns = slice(head * head_dim, (head + 1) * head_dim)
        attended[:, columns] = (value / total).astype(attended.dtype)


def combine(head_dim, state, state_in):
    tokens, width = state[0].shape
    size = tokens * width * (len(state) - 1)
    vmem = pl.BlockSpec(memory_space=pltpu.VMEM)
    return pl.pallas_call(
        functools.partial(combine_kernel, head_dim),
        out_shape=jax.ShapeDtypeStruct((tokens, size // tokens), jnp.bfloat16),
        in_specs=[vmem] * (2 * len(state)),
        out_specs=vmem,
        compiler_params=pltpu.CompilerParams(vmem_limit_bytes=24 * MIB),
        cost_estimate=pl.CostEstimate(flops=4 * size, bytes_accessed=10 * size, transcendentals=0),
        name="combine",
    )(*state, *state_in)


def project_kernel(items, based, ring, me, own_rows, other_rows, *refs):
    count = sum(number for _, _, number in items)
    blocks, refs = refs[:count], refs[count:]
    base = None
    if based:
        base, refs = refs[0], refs[1:]
    results, (held, total, sems) = refs[:-3], refs[-3:]
    span = held.shape[2]
    copies, at = [], 0
    for item, (_, _, number) in enumerate(items):
        targets = [held.at[item]] if number == 1 else [held.at[item, pl.ds(i, 1)] for i in range(number)]
        copies.append(
            [
                pltpu.make_async_copy(blocks[at + i], target, sems.at[at + i])
                for i, target in enumerate(targets)
            ]
        )
        at += number
    for group in copies:
        for copy in group:
            copy.start()
    for item, (place, crossed, _) in enumerate(items):
        for copy in copies[item]:
            copy.wait()
        home = holder(ring, me, place)
        if crossed:
            home = home + 1 - 2 * lax.rem(home, CORES)
        columns = pl.ds(pl.multiple_of(home * span, span), span)
        value = jnp.dot(
            jnp.concatenate([rows[:, columns] for rows in (own_rows, other_rows)], axis=1),
            jnp.concatenate([held[item, plane] for plane in range(2)], axis=0),
            preferred_element_type=jnp.float32,
        )
        if item:
            value = value + total[...]
        elif base is not None:
            value = value + base[...]
        if item + 1 < len(items):
            total[...] = value
    tokens = results[0].shape[0]
    for part, result in enumerate(results):
        result[...] = value[part * tokens : (part + 1) * tokens].astype(result.dtype)


def project(ring, me, rows, blocks, base, shapes):
    items = tuple((place, crossed, len(parts)) for (place, crossed), parts in blocks.items())
    flat = [part for parts in blocks.values() for part in parts]
    tokens = rows[0].shape[0]
    span, width = flat[0].shape[1:]
    size = len(items) * 2 * span * width
    smem = pl.BlockSpec(memory_space=pltpu.SMEM)
    vmem = pl.BlockSpec(memory_space=pltpu.VMEM)
    return pl.pallas_call(
        functools.partial(project_kernel, items, base is not None),
        out_shape=shapes,
        in_specs=[smem] * 2
        + [vmem] * 2
        + [pl.BlockSpec(memory_space=pl.ANY)] * len(flat)
        + ([vmem] if base is not None else []),
        out_specs=[vmem] * len(shapes),
        scratch_shapes=[
            pltpu.VMEM((len(items), 2, span, width), jnp.bfloat16),
            pltpu.VMEM((tokens, width), jnp.float32),
            pltpu.SemaphoreType.DMA((len(flat),)),
        ],
        compiler_params=pltpu.CompilerParams(vmem_limit_bytes=32 * MIB),
        cost_estimate=pl.CostEstimate(
            flops=2 * tokens * size, bytes_accessed=2 * size + 4 * tokens * width, transcendentals=0
        ),
        name="project",
    )(ring, me, *rows, *flat, *([base] if base is not None else []))


def rotation_tables(ranks, length, head_dim):
    offsets = (jnp.arange(ranks) * length).astype(jnp.float32)
    angles = offsets[:, None] * frequency_table(head_dim)[None, :]
    cosine, sine = jnp.cos(angles), jnp.sin(angles)
    return (
        jnp.concatenate([cosine, cosine], axis=1),
        jnp.concatenate([-sine, sine], axis=1),
    )


def ring_body(
    pool,
    queries,
    request_keys,
    request_values,
    cache_keys,
    cache_values,
    passage_ids,
    passage_order,
    out_weight,
):
    _, _, pass_len, head_dim = cache_keys.shape
    tokens = queries.shape[1]
    chips = pool // CORES
    half = chips // 2
    order = ring_order(chips)
    ring = jnp.asarray(order + [order.index(chip) for chip in range(chips)], jnp.int32)
    index = lax.axis_index("pool")
    me = jnp.reshape(index, (1,))
    core = lax.rem(index, CORES)
    plane = lax.axis_index("head")

    span = out_weight.shape[1] // 2
    width = span // CORES
    leaving = lax.dynamic_slice_in_dim(out_weight, (1 - plane) * span, span, axis=1)
    cache_keys, cache_values, leaving = lax.optimization_barrier(
        (cache_keys, cache_values, leaving)
    )
    across = swap_plane(leaving)

    kept = {0: cache_keys}, {0: cache_values}
    for pieces in kept:
        onward(pieces, 1, order)
    across, kept[1][1], kept[1][chips - 1] = lax.optimization_barrier(
        (across, kept[1][1], kept[1][chips - 1])
    )
    for step in range(2, half):
        for pieces in kept:
            onward(pieces, step, order)

    out_weight, across = after(
        (out_weight, across),
        *[kept[1][at] for at in (1, chips - 1)],
    )

    def columns(to_core):
        first = to_core * width
        return jnp.stack(
            [
                lax.dynamic_slice_in_dim(out_weight, plane * span + first, width, axis=1),
                lax.dynamic_slice_in_dim(across, first, width, axis=1),
            ]
        )

    near, far = heavy = {0: columns(core)}, {0: swap_core(columns(1 - core), pool)}
    near[0] = after(near[0], *[kept[1][at] for at in (2, chips - 2)])
    far[0] = after(far[0], *[kept[0][at] for at in (half - 1, half + 1)])
    for step in range(1, half):
        for pieces in heavy:
            onward(pieces, step, order)

    queries, picks, last_keys, last_values = after(
        (
            queries[0],
            jnp.concatenate([passage_ids, passage_order], axis=0),
            kept[0][half - 1],
            kept[1][half + 1],
        ),
        near[1],
        near[chips - 1],
    )
    kept[0][half] = shift(last_keys, order, 1)
    kept[1][half] = shift(last_values, order, -1)
    passages = [[pieces[at] for at in range(chips)] for pieces in kept]

    picks_in = swap_core(picks, pool)
    other_queries = after(
        swap_core(queries, pool), far[1], far[chips - 1]
    )
    tables = rotation_tables(passage_ids.shape[1], pass_len, head_dim)
    other = attend(picks_in[0], picks_in[1], ring, me, other_queries, tables, (), passages)
    own_block = (request_keys[0], request_values[0])
    other_in = [swap_core(value, pool) for value in other]
    queries, other_in = after((queries, other_in), near[2], near[chips - 2], far[2], far[chips - 2])
    own = attend(picks[0], picks[1], ring, me, queries, tables, own_block, passages)
    own = after(own, far[2], far[chips - 2])

    attended = combine(head_dim, own, other_in)
    turned = after(swap_plane(attended), near[3], near[chips - 3])
    quarters = {}

    def last(crossed):
        part = heavy[crossed]
        quarters[(half, crossed)] = (
            shift(part[half - 1][:1], order, 1),
            shift(part[half + 1][1:], order, -1),
        )

    last(0)
    last(1)
    crossed_rows = swap_core(turned, pool)
    crossed_rows = after(crossed_rows, far[3], far[chips - 3])
    rows = [
        jnp.concatenate([attended, swap_core(attended, pool)], axis=0),
        jnp.concatenate([turned, crossed_rows], axis=0),
    ]

    def blocks(places):
        return {(at, part): (heavy[part][at],) for at in places for part in range(2)}

    sums = [jax.ShapeDtypeStruct((CORES * tokens, width), jnp.float32)]
    early = [0] + [at for step in range(1, half - 1) for at in (step, chips - step)]
    total = project(ring, me, rows, blocks(early), None, sums)[0]
    middle = blocks([half - 1, half + 1]) | {(half, 0): quarters[half, 0]}
    total = project(ring, me, rows, middle, total, sums)[0]
    own_out, other_out = project(
        ring,
        me,
        rows,
        {(half, 1): quarters[half, 1]},
        total,
        [jax.ShapeDtypeStruct((tokens, width), jnp.bfloat16)] * 2,
    )
    beside = swap_core(other_out, pool)
    result = jnp.where(
        core == 0,
        jnp.concatenate([own_out, beside], axis=1),
        jnp.concatenate([beside, own_out], axis=1),
    )
    return result[None]


def solution(mesh):
    pool, heads_axis = mesh.shape["pool"], mesh.shape["head"]

    def body(*args):
        weight = args[-1]
        tiled = weight.shape[0] % LANES == 0 and weight.shape[1] % (2 * CORES * LANES) == 0
        if tiled and heads_axis == 2 and pool % (2 * ROWS * CORES) == 0:
            return ring_body(pool, *args)
        return plain_body(*args)

    placed = (
        P("pool", None, "head"),
        P("pool", None, "head"),
        P("pool", None, "head"),
        P("pool", "head", None, None),
        P("pool", "head", None, None),
        P("pool", None),
        P("pool", None),
        P(("head", "pool"), None),
    )
    return jax.shard_map(
        body, mesh=mesh, in_specs=placed, out_specs=P("pool", None, "head"), check_vma=False
    )
```

```python
import functools
import math

import jax
import jax.numpy as jnp
from jax import lax
from jax.experimental import pallas as pl
from jax.experimental.pallas import tpu as pltpu
from jax.sharding import PartitionSpec as P

CORES = 2
ROWS = 4
LANES = 128
MIB = 1024 * 1024


def frequency_table(head_dim):
    pair_index = jnp.arange(head_dim // 2, dtype=jnp.float32)
    return jnp.exp(pair_index * (-2.0 / head_dim) * jnp.log(jnp.float32(500000.0)))


def reposition(vectors, offset, head_dim):
    angles = offset.astype(jnp.float32) * frequency_table(head_dim)
    cosine = jnp.cos(angles)
    sine_term = jnp.sin(angles)
    front_half = vectors[..., : head_dim // 2]
    back_half = vectors[..., head_dim // 2 :]
    return jnp.concatenate(
        [front_half * cosine - back_half * sine_term, back_half * cosine + front_half * sine_term],
        axis=-1,
    )


def absorb(state, query_rows, keys_block, values_block, allowed):
    running_peak, running_total, running_sum = state
    scores = jnp.einsum(
        "hrd,hnd->hrn", query_rows, keys_block, preferred_element_type=jnp.float32
    ) * query_rows.shape[2] ** (-0.5)
    if allowed is not None:
        scores = jnp.where(allowed[None], scores, -jnp.inf)
    new_peak = jnp.maximum(running_peak, jnp.max(scores, axis=-1))
    factor = jnp.exp(running_peak - new_peak)
    exponent = jnp.exp(scores - new_peak[..., None])
    weights = exponent.astype(jnp.bfloat16)
    new_total = running_total * factor + jnp.sum(exponent, axis=-1)
    new_sum = running_sum * factor[..., None] + jnp.einsum(
        "hrn,hnd->hrd", weights, values_block, preferred_element_type=jnp.float32
    )
    return (new_peak, new_total, new_sum)


def plain_body(
    queries,
    request_keys,
    request_values,
    cache_keys,
    cache_values,
    passage_ids,
    passage_order,
    out_weight,
):
    owned, kv_local, pass_len, head_dim = cache_keys.shape
    query_len = queries.shape[1]
    groups = queries.shape[2] // (kv_local * head_dim)
    row_count = query_len * groups
    query_rows = (
        queries[0]
        .reshape(query_len, kv_local, groups, head_dim)
        .transpose(1, 0, 2, 3)
        .reshape(kv_local, row_count, head_dim)
    )
    own_keys = request_keys[0].reshape(query_len, kv_local, head_dim).transpose(1, 0, 2)
    own_values = request_values[0].reshape(query_len, kv_local, head_dim).transpose(1, 0, 2)
    query_token = jnp.arange(row_count) // groups
    causal = jnp.arange(query_len)[None, :] <= query_token[:, None]
    state = (
        jnp.full((kv_local, row_count), -jnp.inf, jnp.float32),
        jnp.zeros((kv_local, row_count), jnp.float32),
        jnp.zeros((kv_local, row_count, head_dim), jnp.float32),
    )
    state = absorb(state, query_rows, own_keys, own_values, causal)
    slots = passage_ids[0]
    offsets = passage_order[0] * pass_len
    piece_keys = lax.all_gather(cache_keys, "pool", axis=0, tiled=True)
    piece_values = lax.all_gather(cache_values, "pool", axis=0, tiled=True)

    def visit_one(position, current):
        matches = slots == position
        offset = jnp.sum(jnp.where(matches, offsets, 0))

        def absorb_one(inner):
            placed = reposition(piece_keys[position].astype(jnp.float32), offset, head_dim).astype(
                jnp.bfloat16
            )
            return absorb(inner, query_rows, placed, piece_values[position], None)

        return lax.cond(jnp.any(matches), absorb_one, lambda inner: inner, current)

    state = lax.fori_loop(0, piece_keys.shape[0], visit_one, state)
    running_peak, running_total, running_sum = state
    attended = (running_sum / running_total[..., None]).astype(jnp.bfloat16)
    attended = (
        attended.reshape(kv_local, query_len, groups, head_dim)
        .transpose(1, 0, 2, 3)
        .reshape(query_len, kv_local * groups * head_dim)
    )
    partial_value = jnp.dot(
        attended,
        lax.all_gather(out_weight, "pool", axis=0, tiled=True),
        preferred_element_type=jnp.float32,
    )
    summed = lax.psum_scatter(
        partial_value.astype(jnp.bfloat16), "head", scatter_dimension=1, tiled=True
    )
    return summed[None]


def ring_order(chips):
    columns = chips // ROWS
    cells = []
    for row in range(ROWS):
        across = range(1, columns) if row % 2 == 0 else range(columns - 1, 0, -1)
        cells += [row * columns + column for column in across]
    return cells + [row * columns for row in reversed(range(ROWS))]


def shift(value, order, step):
    chips = len(order)
    pairs = [
        (order[at] * CORES + core, order[(at + step) % chips] * CORES + core)
        for at in range(chips)
        for core in range(CORES)
    ]
    return lax.ppermute(value, "pool", pairs)


def onward(pieces, step, order):
    chips = len(order)
    pieces[step] = shift(pieces[step - 1], order, 1)
    pieces[chips - step] = shift(pieces[(chips - step + 1) % chips], order, -1)


def after(value, *earlier):
    return lax.optimization_barrier((value, earlier))[0]


def swap_core(value, pool):
    return lax.ppermute(value, "pool", [(at, at ^ 1) for at in range(pool)])


def swap_plane(value):
    return lax.ppermute(value, "head", [(0, 1), (1, 0)])


def holder(ring, me, back):
    chips = ring.shape[0] // 2
    chip = lax.div(me[0], CORES)
    place = lax.rem(ring[chips + chip] + chips - back, chips)
    return ring[place] * CORES + lax.rem(me[0], CORES)


def attend_kernel(pieces, owned, ids, ranks, ring, me, queries, cosine, sine, *refs):
    key_pieces, value_pieces, refs = refs[:pieces], refs[pieces : 2 * pieces], refs[2 * pieces :]
    stats, keys, values, within, rank_of, key_sem, value_sem = refs[-7:]
    slots = ids.shape[0]
    kv_local, _, head_dim = keys.shape
    near, sums = refs[: -7 - kv_local], refs[-7 - kv_local : -7]
    length = key_pieces[0].shape[2]
    tokens = queries.shape[0]
    groups = queries.shape[1] // (kv_local * head_dim)
    heads = kv_local * groups
    factor = math.log2(math.e) / math.sqrt(head_dim)
    across = (((1,), (1,)), ((), ()))

    for slot in range(slots):
        passage = ids[slot]
        home = lax.div(passage, owned)
        within[home] = passage - home * owned
        rank_of[home] = ranks[slot]
    homes = [holder(ring, me, piece) for piece in range(pieces)]

    def copy(source, target, sem, piece):
        rows = pl.ds(piece * length, length)
        return pltpu.make_async_copy(
            source[piece].at[within[homes[piece]]], target.at[:, rows], sem.at[piece]
        )

    key_copies = [copy(key_pieces, keys, key_sem, piece) for piece in range(pieces)]
    value_copies = [copy(value_pieces, values, value_sem, piece) for piece in range(pieces)]
    for each in key_copies + value_copies:
        each.start()
    for piece in range(pieces):
        key_copies[piece].wait()
        rank = rank_of[homes[piece]]
        cos = cosine[pl.ds(rank, 1), :]
        sin = sine[pl.ds(rank, 1), :]
        rows = pl.ds(piece * length, length)
        for head in range(kv_local):
            block = keys[head, rows, :].astype(jnp.float32)
            turned = block * cos + pltpu.roll(block, head_dim // 2, 1) * sin
            keys[head, rows, :] = turned.astype(jnp.bfloat16)
    for each in value_copies:
        each.wait()

    lane = lax.broadcasted_iota(jnp.int32, (tokens, LANES), 1)
    marks = jnp.zeros((tokens, LANES), jnp.float32)
    for head in range(kv_local):
        spans = [
            slice((head * groups + g) * head_dim, (head * groups + g + 1) * head_dim)
            for g in range(groups)
        ]
        rows = jnp.concatenate([queries[:, span] for span in spans], axis=0)
        scores = lax.dot_general(rows, keys[head], across, preferred_element_type=jnp.float32)
        peak = jnp.max(scores, axis=1, keepdims=True)
        if near:
            own = slice(head * head_dim, (head + 1) * head_dim)
            close = lax.dot_general(
                rows, near[0][:, own], across, preferred_element_type=jnp.float32
            )
            token = lax.rem(lax.broadcasted_iota(jnp.int32, close.shape, 0), tokens)
            column = lax.broadcasted_iota(jnp.int32, close.shape, 1)
            close = jnp.where(column <= token, close, -jnp.inf)
            peak = jnp.maximum(peak, jnp.max(close, axis=1, keepdims=True))
        exponent = jnp.exp2((scores - peak) * factor)
        total = jnp.sum(exponent, axis=1, keepdims=True)
        summed = jnp.dot(
            exponent.astype(jnp.bfloat16), values[head], preferred_element_type=jnp.float32
        )
        if near:
            exponent = jnp.exp2((close - peak) * factor)
            total = total + jnp.sum(exponent, axis=1, keepdims=True)
            summed = summed + jnp.dot(
                exponent.astype(jnp.bfloat16), near[1][:, own], preferred_element_type=jnp.float32
            )
        for g in range(groups):
            part = slice(g * tokens, (g + 1) * tokens)
            sums[head][:, g * head_dim : (g + 1) * head_dim] = summed[part]
            at = head * groups + g
            marks = jnp.where(lane == at, peak[part], marks)
            marks = jnp.where(lane == heads + at, total[part], marks)
    stats[...] = marks


def attend(ids, ranks, ring, me, queries, tables, near, passages, effort=24):
    pieces = len(passages[0])
    key_pieces, value_pieces = passages
    owned, kv_local, length, head_dim = key_pieces[0].shape
    tokens, features = queries.shape
    holders = ids.shape[0]
    smem = pl.BlockSpec(memory_space=pltpu.SMEM)
    vmem = pl.BlockSpec(memory_space=pltpu.VMEM)
    seen = pieces * length
    scores = tokens * (features // head_dim) * (seen + (length if near else 0))
    return pl.pallas_call(
        functools.partial(attend_kernel, pieces, owned),
        out_shape=[jax.ShapeDtypeStruct((tokens, features // kv_local), jnp.float32)] * kv_local
        + [jax.ShapeDtypeStruct((tokens, LANES), jnp.float32)],
        in_specs=[smem] * 4
        + [vmem] * 3
        + [pl.BlockSpec(memory_space=pl.ANY)] * (2 * pieces)
        + [vmem] * len(near),
        out_specs=[vmem] * (kv_local + 1),
        scratch_shapes=[
            pltpu.VMEM((kv_local, seen, head_dim), jnp.bfloat16),
            pltpu.VMEM((kv_local, seen, head_dim), jnp.bfloat16),
            pltpu.SMEM((holders,), jnp.int32),
            pltpu.SMEM((holders,), jnp.int32),
            pltpu.SemaphoreType.DMA((pieces,)),
            pltpu.SemaphoreType.DMA((pieces,)),
        ],
        compiler_params=pltpu.CompilerParams(vmem_limit_bytes=32 * MIB),
        cost_estimate=pl.CostEstimate(
            flops=effort * scores * head_dim, bytes_accessed=4 * MIB, transcendentals=scores
        ),
        name="attend",
    )(ids, ranks, ring, me, queries, *tables, *key_pieces, *value_pieces, *near)


def combine_kernel(head_dim, *refs):
    attended, refs = refs[-1], refs[:-1]
    count = len(refs) // 2
    sums, stats = refs[: count - 1], refs[count - 1]
    sums_in, stats_in = refs[count:-1], refs[-1]
    groups = sums[0].shape[1] // head_dim
    heads = groups * len(sums)
    factor = math.log2(math.e) / math.sqrt(head_dim)
    for head in range(heads):
        block, at = divmod(head, groups)
        columns = slice(at * head_dim, (at + 1) * head_dim)
        peak_a, peak_b = stats[:, head : head + 1], stats_in[:, head : head + 1]
        at = heads + head
        total_a, total_b = stats[:, at : at + 1], stats_in[:, at : at + 1]
        peak = jnp.maximum(peak_a, peak_b)
        part_a = jnp.exp2((peak_a - peak) * factor)
        part_b = jnp.exp2((peak_b - peak) * factor)
        total = total_a * part_a + total_b * part_b
        value = sums[block][:, columns] * part_a + sums_in[block][:, columns] * part_b
        columns = slice(head * head_dim, (head + 1) * head_dim)
        attended[:, columns] = (value / total).astype(attended.dtype)


def combine(head_dim, state, state_in):
    tokens, width = state[0].shape
    size = tokens * width * (len(state) - 1)
    vmem = pl.BlockSpec(memory_space=pltpu.VMEM)
    return pl.pallas_call(
        functools.partial(combine_kernel, head_dim),
        out_shape=jax.ShapeDtypeStruct((tokens, size // tokens), jnp.bfloat16),
        in_specs=[vmem] * (2 * len(state)),
        out_specs=vmem,
        compiler_params=pltpu.CompilerParams(vmem_limit_bytes=24 * MIB),
        cost_estimate=pl.CostEstimate(flops=4 * size, bytes_accessed=10 * size, transcendentals=0),
        name="combine",
    )(*state, *state_in)


def project_kernel(items, based, ring, me, own_rows, other_rows, *refs):
    count = sum(number for _, _, number in items)
    blocks, refs = refs[:count], refs[count:]
    base = None
    if based:
        base, refs = refs[0], refs[1:]
    results, (held, total, sems) = refs[:-3], refs[-3:]
    span = held.shape[2]
    copies, at = [], 0
    for item, (_, _, number) in enumerate(items):
        targets = [held.at[item]] if number == 1 else [held.at[item, pl.ds(i, 1)] for i in range(number)]
        copies.append(
            [
                pltpu.make_async_copy(blocks[at + i], target, sems.at[at + i])
                for i, target in enumerate(targets)
            ]
        )
        at += number
    for group in copies:
        for copy in group:
            copy.start()
    for item, (place, crossed, _) in enumerate(items):
        for copy in copies[item]:
            copy.wait()
        home = holder(ring, me, place)
        if crossed:
            home = home + 1 - 2 * lax.rem(home, CORES)
        columns = pl.ds(pl.multiple_of(home * span, span), span)
        value = jnp.dot(
            jnp.concatenate([rows[:, columns] for rows in (own_rows, other_rows)], axis=1),
            jnp.concatenate([held[item, plane] for plane in range(2)], axis=0),
            preferred_element_type=jnp.float32,
        )
        if item:
            value = value + total[...]
        elif base is not None:
            value = value + base[...]
        if item + 1 < len(items):
            total[...] = value
    tokens = results[0].shape[0]
    for part, result in enumerate(results):
        result[...] = value[part * tokens : (part + 1) * tokens].astype(result.dtype)


def project(ring, me, rows, blocks, base, shapes):
    items = tuple((place, crossed, len(parts)) for (place, crossed), parts in blocks.items())
    flat = [part for parts in blocks.values() for part in parts]
    tokens = rows[0].shape[0]
    span, width = flat[0].shape[1:]
    size = len(items) * 2 * span * width
    smem = pl.BlockSpec(memory_space=pltpu.SMEM)
    vmem = pl.BlockSpec(memory_space=pltpu.VMEM)
    return pl.pallas_call(
        functools.partial(project_kernel, items, base is not None),
        out_shape=shapes,
        in_specs=[smem] * 2
        + [vmem] * 2
        + [pl.BlockSpec(memory_space=pl.ANY)] * len(flat)
        + ([vmem] if base is not None else []),
        out_specs=[vmem] * len(shapes),
        scratch_shapes=[
            pltpu.VMEM((len(items), 2, span, width), jnp.bfloat16),
            pltpu.VMEM((tokens, width), jnp.float32),
            pltpu.SemaphoreType.DMA((len(flat),)),
        ],
        compiler_params=pltpu.CompilerParams(vmem_limit_bytes=32 * MIB),
        cost_estimate=pl.CostEstimate(
            flops=2 * tokens * size, bytes_accessed=2 * size + 4 * tokens * width, transcendentals=0
        ),
        name="project",
    )(ring, me, *rows, *flat, *([base] if base is not None else []))


def rotation_tables(ranks, length, head_dim):
    offsets = (jnp.arange(ranks) * length).astype(jnp.float32)
    angles = offsets[:, None] * frequency_table(head_dim)[None, :]
    cosine, sine = jnp.cos(angles), jnp.sin(angles)
    return (
        jnp.concatenate([cosine, cosine], axis=1),
        jnp.concatenate([-sine, sine], axis=1),
    )


def ring_body(
    pool,
    queries,
    request_keys,
    request_values,
    cache_keys,
    cache_values,
    passage_ids,
    passage_order,
    out_weight,
):
    _, _, pass_len, head_dim = cache_keys.shape
    tokens = queries.shape[1]
    chips = pool // CORES
    half = chips // 2
    order = ring_order(chips)
    ring = jnp.asarray(order + [order.index(chip) for chip in range(chips)], jnp.int32)
    index = lax.axis_index("pool")
    me = jnp.reshape(index, (1,))
    core = lax.rem(index, CORES)
    plane = lax.axis_index("head")

    span = out_weight.shape[1] // 2
    width = span // CORES
    leaving = lax.dynamic_slice_in_dim(out_weight, (1 - plane) * span, span, axis=1)
    cache_keys, cache_values, leaving = lax.optimization_barrier(
        (cache_keys, cache_values, leaving)
    )
    across = swap_plane(leaving)

    kept = {0: cache_keys}, {0: cache_values}
    for pieces in kept:
        onward(pieces, 1, order)
    across, kept[1][1], kept[1][chips - 1] = lax.optimization_barrier(
        (across, kept[1][1], kept[1][chips - 1])
    )
    for step in range(2, half):
        for pieces in kept:
            onward(pieces, step, order)

    out_weight, across = after(
        (out_weight, across),
        *[kept[1][at] for at in (1, chips - 1)],
    )

    def columns(to_core):
        first = to_core * width
        return jnp.stack(
            [
                lax.dynamic_slice_in_dim(out_weight, plane * span + first, width, axis=1),
                lax.dynamic_slice_in_dim(across, first, width, axis=1),
            ]
        )

    near, far = heavy = {0: columns(core)}, {0: swap_core(columns(1 - core), pool)}
    near[0] = after(near[0], *[kept[1][at] for at in (2, chips - 2)])
    far[0] = after(far[0], *[kept[0][at] for at in (half - 1, half + 1)])
    for step in range(1, half):
        for pieces in heavy:
            onward(pieces, step, order)

    queries, picks, last_keys, last_values = after(
        (
            queries[0],
            jnp.concatenate([passage_ids, passage_order], axis=0),
            kept[0][half - 1],
            kept[1][half + 1],
        ),
        near[1],
        near[chips - 1],
    )
    kept[0][half] = shift(last_keys, order, 1)
    kept[1][half] = shift(last_values, order, -1)
    passages = [[pieces[at] for at in range(chips)] for pieces in kept]

    picks_in = swap_core(picks, pool)
    other_queries = after(
        swap_core(queries, pool), far[1], far[chips - 1]
    )
    tables = rotation_tables(passage_ids.shape[1], pass_len, head_dim)
    other = attend(picks_in[0], picks_in[1], ring, me, other_queries, tables, (), passages)
    own_block = (request_keys[0], request_values[0])
    other_in = [swap_core(value, pool) for value in other]
    queries, other_in = after((queries, other_in), near[2], near[chips - 2])
    own = attend(picks[0], picks[1], ring, me, queries, tables, own_block, passages, 1)
    own = after(own, far[2], far[chips - 2])

    attended = combine(head_dim, own, other_in)
    turned = after(swap_plane(attended), near[3], near[chips - 3])
    quarters = {}

    def last(crossed):
        part = heavy[crossed]
        quarters[(half, crossed)] = (
            shift(part[half - 1][:1], order, 1),
            shift(part[half + 1][1:], order, -1),
        )

    last(0)
    last(1)
    crossed_rows = swap_core(turned, pool)
    crossed_rows = after(crossed_rows, far[3], far[chips - 3])
    rows = [
        jnp.concatenate([attended, swap_core(attended, pool)], axis=0),
        jnp.concatenate([turned, crossed_rows], axis=0),
    ]

    def blocks(places):
        return {(at, part): (heavy[part][at],) for at in places for part in range(2)}

    sums = [jax.ShapeDtypeStruct((CORES * tokens, width), jnp.float32)]
    early = [0] + [at for step in range(1, half - 1) for at in (step, chips - step)]
    total = project(ring, me, rows, blocks(early), None, sums)[0]
    middle = blocks([half - 1, half + 1]) | {(half, 0): quarters[half, 0]}
    total = project(ring, me, rows, middle, total, sums)[0]
    own_out, other_out = project(
        ring,
        me,
        rows,
        {(half, 1): quarters[half, 1]},
        total,
        [jax.ShapeDtypeStruct((tokens, width), jnp.bfloat16)] * 2,
    )
    beside = swap_core(other_out, pool)
    result = jnp.where(
        core == 0,
        jnp.concatenate([own_out, beside], axis=1),
        jnp.concatenate([beside, own_out], axis=1),
    )
    return result[None]


def solution(mesh):
    pool, heads_axis = mesh.shape["pool"], mesh.shape["head"]

    def body(*args):
        weight = args[-1]
        tiled = weight.shape[0] % LANES == 0 and weight.shape[1] % (2 * CORES * LANES) == 0
        if tiled and heads_axis == 2 and pool % (2 * ROWS * CORES) == 0:
            return ring_body(pool, *args)
        return plain_body(*args)

    placed = (
        P("pool", None, "head"),
        P("pool", None, "head"),
        P("pool", None, "head"),
        P("pool", "head", None, None),
        P("pool", "head", None, None),
        P("pool", None),
        P("pool", None),
        P(("head", "pool"), None),
    )
    return jax.shard_map(
        body, mesh=mesh, in_specs=placed, out_specs=P("pool", None, "head"), check_vma=False
    )
```

```python
import functools
import math

import jax
import jax.numpy as jnp
from jax import lax
from jax.experimental import pallas as pl
from jax.experimental.pallas import tpu as pltpu
from jax.sharding import PartitionSpec as P

CORES = 2
ROWS = 4
LANES = 128
MIB = 1024 * 1024


def frequency_table(head_dim):
    pair_index = jnp.arange(head_dim // 2, dtype=jnp.float32)
    return jnp.exp(pair_index * (-2.0 / head_dim) * jnp.log(jnp.float32(500000.0)))


def reposition(vectors, offset, head_dim):
    angles = offset.astype(jnp.float32) * frequency_table(head_dim)
    cosine = jnp.cos(angles)
    sine_term = jnp.sin(angles)
    front_half = vectors[..., : head_dim // 2]
    back_half = vectors[..., head_dim // 2 :]
    return jnp.concatenate(
        [front_half * cosine - back_half * sine_term, back_half * cosine + front_half * sine_term],
        axis=-1,
    )


def absorb(state, query_rows, keys_block, values_block, allowed):
    running_peak, running_total, running_sum = state
    scores = jnp.einsum(
        "hrd,hnd->hrn", query_rows, keys_block, preferred_element_type=jnp.float32
    ) * query_rows.shape[2] ** (-0.5)
    if allowed is not None:
        scores = jnp.where(allowed[None], scores, -jnp.inf)
    new_peak = jnp.maximum(running_peak, jnp.max(scores, axis=-1))
    factor = jnp.exp(running_peak - new_peak)
    exponent = jnp.exp(scores - new_peak[..., None])
    weights = exponent.astype(jnp.bfloat16)
    new_total = running_total * factor + jnp.sum(exponent, axis=-1)
    new_sum = running_sum * factor[..., None] + jnp.einsum(
        "hrn,hnd->hrd", weights, values_block, preferred_element_type=jnp.float32
    )
    return (new_peak, new_total, new_sum)


def plain_body(
    queries,
    request_keys,
    request_values,
    cache_keys,
    cache_values,
    passage_ids,
    passage_order,
    out_weight,
):
    owned, kv_local, pass_len, head_dim = cache_keys.shape
    query_len = queries.shape[1]
    groups = queries.shape[2] // (kv_local * head_dim)
    row_count = query_len * groups
    query_rows = (
        queries[0]
        .reshape(query_len, kv_local, groups, head_dim)
        .transpose(1, 0, 2, 3)
        .reshape(kv_local, row_count, head_dim)
    )
    own_keys = request_keys[0].reshape(query_len, kv_local, head_dim).transpose(1, 0, 2)
    own_values = request_values[0].reshape(query_len, kv_local, head_dim).transpose(1, 0, 2)
    query_token = jnp.arange(row_count) // groups
    causal = jnp.arange(query_len)[None, :] <= query_token[:, None]
    state = (
        jnp.full((kv_local, row_count), -jnp.inf, jnp.float32),
        jnp.zeros((kv_local, row_count), jnp.float32),
        jnp.zeros((kv_local, row_count, head_dim), jnp.float32),
    )
    state = absorb(state, query_rows, own_keys, own_values, causal)
    slots = passage_ids[0]
    offsets = passage_order[0] * pass_len
    piece_keys = lax.all_gather(cache_keys, "pool", axis=0, tiled=True)
    piece_values = lax.all_gather(cache_values, "pool", axis=0, tiled=True)

    def visit_one(position, current):
        matches = slots == position
        offset = jnp.sum(jnp.where(matches, offsets, 0))

        def absorb_one(inner):
            placed = reposition(piece_keys[position].astype(jnp.float32), offset, head_dim).astype(
                jnp.bfloat16
            )
            return absorb(inner, query_rows, placed, piece_values[position], None)

        return lax.cond(jnp.any(matches), absorb_one, lambda inner: inner, current)

    state = lax.fori_loop(0, piece_keys.shape[0], visit_one, state)
    running_peak, running_total, running_sum = state
    attended = (running_sum / running_total[..., None]).astype(jnp.bfloat16)
    attended = (
        attended.reshape(kv_local, query_len, groups, head_dim)
        .transpose(1, 0, 2, 3)
        .reshape(query_len, kv_local * groups * head_dim)
    )
    partial_value = jnp.dot(
        attended,
        lax.all_gather(out_weight, "pool", axis=0, tiled=True),
        preferred_element_type=jnp.float32,
    )
    summed = lax.psum_scatter(
        partial_value.astype(jnp.bfloat16), "head", scatter_dimension=1, tiled=True
    )
    return summed[None]


def ring_order(chips):
    columns = chips // ROWS
    cells = []
    for row in range(ROWS):
        across = range(1, columns) if row % 2 == 0 else range(columns - 1, 0, -1)
        cells += [row * columns + column for column in across]
    return cells + [row * columns for row in reversed(range(ROWS))]


def shift(value, order, step):
    chips = len(order)
    pairs = [
        (order[at] * CORES + core, order[(at + step) % chips] * CORES + core)
        for at in range(chips)
        for core in range(CORES)
    ]
    return lax.ppermute(value, "pool", pairs)


def onward(pieces, step, order):
    chips = len(order)
    pieces[step] = shift(pieces[step - 1], order, 1)
    pieces[chips - step] = shift(pieces[(chips - step + 1) % chips], order, -1)


def after(value, *earlier):
    return lax.optimization_barrier((value, earlier))[0]


def swap_core(value, pool):
    return lax.ppermute(value, "pool", [(at, at ^ 1) for at in range(pool)])


def swap_plane(value):
    return lax.ppermute(value, "head", [(0, 1), (1, 0)])


def holder(ring, me, back):
    chips = ring.shape[0] // 2
    chip = lax.div(me[0], CORES)
    place = lax.rem(ring[chips + chip] + chips - back, chips)
    return ring[place] * CORES + lax.rem(me[0], CORES)


def attend_kernel(pieces, owned, ids, ranks, ring, me, queries, cosine, sine, *refs):
    key_pieces, value_pieces, refs = refs[:pieces], refs[pieces : 2 * pieces], refs[2 * pieces :]
    stats, keys, values, within, rank_of, key_sem, value_sem = refs[-7:]
    slots = ids.shape[0]
    kv_local, _, head_dim = keys.shape
    near, sums = refs[: -7 - kv_local], refs[-7 - kv_local : -7]
    length = key_pieces[0].shape[2]
    tokens = queries.shape[0]
    groups = queries.shape[1] // (kv_local * head_dim)
    heads = kv_local * groups
    factor = math.log2(math.e) / math.sqrt(head_dim)
    across = (((1,), (1,)), ((), ()))

    for slot in range(slots):
        passage = ids[slot]
        home = lax.div(passage, owned)
        within[home] = passage - home * owned
        rank_of[home] = ranks[slot]
    homes = [holder(ring, me, piece) for piece in range(pieces)]

    def copy(source, target, sem, piece):
        rows = pl.ds(piece * length, length)
        return pltpu.make_async_copy(
            source[piece].at[within[homes[piece]]], target.at[:, rows], sem.at[piece]
        )

    key_copies = [copy(key_pieces, keys, key_sem, piece) for piece in range(pieces)]
    value_copies = [copy(value_pieces, values, value_sem, piece) for piece in range(pieces)]
    for each in key_copies + value_copies:
        each.start()
    for piece in range(pieces):
        key_copies[piece].wait()
        rank = rank_of[homes[piece]]
        cos = cosine[pl.ds(rank, 1), :]
        sin = sine[pl.ds(rank, 1), :]
        rows = pl.ds(piece * length, length)
        for head in range(kv_local):
            block = keys[head, rows, :].astype(jnp.float32)
            turned = block * cos + pltpu.roll(block, head_dim // 2, 1) * sin
            keys[head, rows, :] = turned.astype(jnp.bfloat16)
    for each in value_copies:
        each.wait()

    lane = lax.broadcasted_iota(jnp.int32, (tokens, LANES), 1)
    marks = jnp.zeros((tokens, LANES), jnp.float32)
    for head in range(kv_local):
        spans = [
            slice((head * groups + g) * head_dim, (head * groups + g + 1) * head_dim)
            for g in range(groups)
        ]
        rows = jnp.concatenate([queries[:, span] for span in spans], axis=0)
        scores = lax.dot_general(rows, keys[head], across, preferred_element_type=jnp.float32)
        peak = jnp.max(scores, axis=1, keepdims=True)
        if near:
            own = slice(head * head_dim, (head + 1) * head_dim)
            close = lax.dot_general(
                rows, near[0][:, own], across, preferred_element_type=jnp.float32
            )
            token = lax.rem(lax.broadcasted_iota(jnp.int32, close.shape, 0), tokens)
            column = lax.broadcasted_iota(jnp.int32, close.shape, 1)
            close = jnp.where(column <= token, close, -jnp.inf)
            peak = jnp.maximum(peak, jnp.max(close, axis=1, keepdims=True))
        exponent = jnp.exp2((scores - peak) * factor)
        total = jnp.sum(exponent, axis=1, keepdims=True)
        summed = jnp.dot(
            exponent.astype(jnp.bfloat16), values[head], preferred_element_type=jnp.float32
        )
        if near:
            exponent = jnp.exp2((close - peak) * factor)
            total = total + jnp.sum(exponent, axis=1, keepdims=True)
            summed = summed + jnp.dot(
                exponent.astype(jnp.bfloat16), near[1][:, own], preferred_element_type=jnp.float32
            )
        for g in range(groups):
            part = slice(g * tokens, (g + 1) * tokens)
            sums[head][:, g * head_dim : (g + 1) * head_dim] = summed[part]
            at = head * groups + g
            marks = jnp.where(lane == at, peak[part], marks)
            marks = jnp.where(lane == heads + at, total[part], marks)
    stats[...] = marks


def attend(ids, ranks, ring, me, queries, tables, near, passages, effort=24):
    pieces = len(passages[0])
    key_pieces, value_pieces = passages
    owned, kv_local, length, head_dim = key_pieces[0].shape
    tokens, features = queries.shape
    holders = ids.shape[0]
    smem = pl.BlockSpec(memory_space=pltpu.SMEM)
    vmem = pl.BlockSpec(memory_space=pltpu.VMEM)
    seen = pieces * length
    scores = tokens * (features // head_dim) * (seen + (length if near else 0))
    return pl.pallas_call(
        functools.partial(attend_kernel, pieces, owned),
        out_shape=[jax.ShapeDtypeStruct((tokens, features // kv_local), jnp.float32)] * kv_local
        + [jax.ShapeDtypeStruct((tokens, LANES), jnp.float32)],
        in_specs=[smem] * 4
        + [vmem] * 3
        + [pl.BlockSpec(memory_space=pl.ANY)] * (2 * pieces)
        + [vmem] * len(near),
        out_specs=[vmem] * (kv_local + 1),
        scratch_shapes=[
            pltpu.VMEM((kv_local, seen, head_dim), jnp.bfloat16),
            pltpu.VMEM((kv_local, seen, head_dim), jnp.bfloat16),
            pltpu.SMEM((holders,), jnp.int32),
            pltpu.SMEM((holders,), jnp.int32),
            pltpu.SemaphoreType.DMA((pieces,)),
            pltpu.SemaphoreType.DMA((pieces,)),
        ],
        compiler_params=pltpu.CompilerParams(vmem_limit_bytes=32 * MIB),
        cost_estimate=pl.CostEstimate(
            flops=effort * scores * head_dim, bytes_accessed=4 * MIB, transcendentals=scores
        ),
        name="attend",
    )(ids, ranks, ring, me, queries, *tables, *key_pieces, *value_pieces, *near)


def combine_kernel(head_dim, *refs):
    attended, refs = refs[-1], refs[:-1]
    count = len(refs) // 2
    sums, stats = refs[: count - 1], refs[count - 1]
    sums_in, stats_in = refs[count:-1], refs[-1]
    groups = sums[0].shape[1] // head_dim
    heads = groups * len(sums)
    factor = math.log2(math.e) / math.sqrt(head_dim)
    for head in range(heads):
        block, at = divmod(head, groups)
        columns = slice(at * head_dim, (at + 1) * head_dim)
        peak_a, peak_b = stats[:, head : head + 1], stats_in[:, head : head + 1]
        at = heads + head
        total_a, total_b = stats[:, at : at + 1], stats_in[:, at : at + 1]
        peak = jnp.maximum(peak_a, peak_b)
        part_a = jnp.exp2((peak_a - peak) * factor)
        part_b = jnp.exp2((peak_b - peak) * factor)
        total = total_a * part_a + total_b * part_b
        value = sums[block][:, columns] * part_a + sums_in[block][:, columns] * part_b
        columns = slice(head * head_dim, (head + 1) * head_dim)
        attended[:, columns] = (value / total).astype(attended.dtype)


def combine(head_dim, state, state_in):
    tokens, width = state[0].shape
    size = tokens * width * (len(state) - 1)
    vmem = pl.BlockSpec(memory_space=pltpu.VMEM)
    return pl.pallas_call(
        functools.partial(combine_kernel, head_dim),
        out_shape=jax.ShapeDtypeStruct((tokens, size // tokens), jnp.bfloat16),
        in_specs=[vmem] * (2 * len(state)),
        out_specs=vmem,
        compiler_params=pltpu.CompilerParams(vmem_limit_bytes=24 * MIB),
        cost_estimate=pl.CostEstimate(flops=4 * size, bytes_accessed=10 * size, transcendentals=0),
        name="combine",
    )(*state, *state_in)


def project_kernel(items, based, ring, me, own_rows, other_rows, *refs):
    count = sum(number for _, _, number in items)
    blocks, refs = refs[:count], refs[count:]
    base = None
    if based:
        base, refs = refs[0], refs[1:]
    results, (held, total, sems) = refs[:-3], refs[-3:]
    span = held.shape[2]
    copies, at = [], 0
    for item, (_, _, number) in enumerate(items):
        targets = [held.at[item]] if number == 1 else [held.at[item, pl.ds(i, 1)] for i in range(number)]
        copies.append(
            [
                pltpu.make_async_copy(blocks[at + i], target, sems.at[at + i])
                for i, target in enumerate(targets)
            ]
        )
        at += number
    for group in copies:
        for copy in group:
            copy.start()
    for item, (place, crossed, _) in enumerate(items):
        for copy in copies[item]:
            copy.wait()
        home = holder(ring, me, place)
        if crossed:
            home = home + 1 - 2 * lax.rem(home, CORES)
        columns = pl.ds(pl.multiple_of(home * span, span), span)
        value = jnp.dot(
            jnp.concatenate([rows[:, columns] for rows in (own_rows, other_rows)], axis=1),
            jnp.concatenate([held[item, plane] for plane in range(2)], axis=0),
            preferred_element_type=jnp.float32,
        )
        if item:
            value = value + total[...]
        elif base is not None:
            value = value + base[...]
        if item + 1 < len(items):
            total[...] = value
    tokens = results[0].shape[0]
    for part, result in enumerate(results):
        result[...] = value[part * tokens : (part + 1) * tokens].astype(result.dtype)


def project(ring, me, rows, blocks, base, shapes):
    items = tuple((place, crossed, len(parts)) for (place, crossed), parts in blocks.items())
    flat = [part for parts in blocks.values() for part in parts]
    tokens = rows[0].shape[0]
    span, width = flat[0].shape[1:]
    size = len(items) * 2 * span * width
    smem = pl.BlockSpec(memory_space=pltpu.SMEM)
    vmem = pl.BlockSpec(memory_space=pltpu.VMEM)
    return pl.pallas_call(
        functools.partial(project_kernel, items, base is not None),
        out_shape=shapes,
        in_specs=[smem] * 2
        + [vmem] * 2
        + [pl.BlockSpec(memory_space=pl.ANY)] * len(flat)
        + ([vmem] if base is not None else []),
        out_specs=[vmem] * len(shapes),
        scratch_shapes=[
            pltpu.VMEM((len(items), 2, span, width), jnp.bfloat16),
            pltpu.VMEM((tokens, width), jnp.float32),
            pltpu.SemaphoreType.DMA((len(flat),)),
        ],
        compiler_params=pltpu.CompilerParams(vmem_limit_bytes=32 * MIB),
        cost_estimate=pl.CostEstimate(
            flops=2 * tokens * size, bytes_accessed=2 * size + 4 * tokens * width, transcendentals=0
        ),
        name="project",
    )(ring, me, *rows, *flat, *([base] if base is not None else []))


def rotation_tables(ranks, length, head_dim):
    offsets = (jnp.arange(ranks) * length).astype(jnp.float32)
    angles = offsets[:, None] * frequency_table(head_dim)[None, :]
    cosine, sine = jnp.cos(angles), jnp.sin(angles)
    return (
        jnp.concatenate([cosine, cosine], axis=1),
        jnp.concatenate([-sine, sine], axis=1),
    )


def ring_body(
    pool,
    queries,
    request_keys,
    request_values,
    cache_keys,
    cache_values,
    passage_ids,
    passage_order,
    out_weight,
):
    _, _, pass_len, head_dim = cache_keys.shape
    tokens = queries.shape[1]
    chips = pool // CORES
    half = chips // 2
    order = ring_order(chips)
    ring = jnp.asarray(order + [order.index(chip) for chip in range(chips)], jnp.int32)
    index = lax.axis_index("pool")
    me = jnp.reshape(index, (1,))
    core = lax.rem(index, CORES)
    plane = lax.axis_index("head")

    span = out_weight.shape[1] // 2
    width = span // CORES
    leaving = lax.dynamic_slice_in_dim(out_weight, (1 - plane) * span, span, axis=1)
    cache_keys, cache_values, leaving = lax.optimization_barrier(
        (cache_keys, cache_values, leaving)
    )
    across = swap_plane(leaving)

    kept = {0: cache_keys}, {0: cache_values}
    for pieces in kept:
        onward(pieces, 1, order)
    across, kept[1][1], kept[1][chips - 1] = lax.optimization_barrier(
        (across, kept[1][1], kept[1][chips - 1])
    )
    for step in range(2, half):
        for pieces in kept:
            onward(pieces, step, order)

    out_weight, across = after(
        (out_weight, across),
        kept[1][1], kept[1][chips - 1],
    )

    def columns(to_core):
        first = to_core * width
        return jnp.stack(
            [
                lax.dynamic_slice_in_dim(out_weight, plane * span + first, width, axis=1),
                lax.dynamic_slice_in_dim(across, first, width, axis=1),
            ]
        )

    near, far = heavy = {0: columns(core)}, {0: swap_core(columns(1 - core), pool)}
    near[0] = after(near[0], kept[0][2], kept[0][chips - 2], kept[1][2], kept[1][chips - 2])
    far[0] = after(far[0], *[kept[0][at] for at in (half - 1, half + 1)])
    for step in range(1, half):
        for pieces in heavy:
            onward(pieces, step, order)

    queries, picks, last_keys, last_values = after(
        (
            queries[0],
            jnp.concatenate([passage_ids, passage_order], axis=0),
            kept[0][half - 1],
            kept[1][half + 1],
        ),
        near[1],
        near[chips - 1],
    )
    kept[0][half] = shift(last_keys, order, 1)
    kept[1][half] = shift(last_values, order, -1)
    passages = [[pieces[at] for at in range(chips)] for pieces in kept]

    picks_in = swap_core(picks, pool)
    other_queries = after(
        swap_core(queries, pool), far[1], far[chips - 1], near[1], near[chips - 1]
    )
    tables = rotation_tables(passage_ids.shape[1], pass_len, head_dim)
    other = attend(picks_in[0], picks_in[1], ring, me, other_queries, tables, (), passages)
    own_block = (request_keys[0], request_values[0])
    other_in = [swap_core(value, pool) for value in other]
    queries, other_in = after((queries, other_in), near[2], near[chips - 2])
    own = attend(picks[0], picks[1], ring, me, queries, tables, own_block, passages, 1)
    own = after(own, far[2], far[chips - 2])

    attended = combine(head_dim, own, other_in)
    turned = after(swap_plane(attended), near[3], near[chips - 3])
    quarters = {}

    def last(crossed):
        part = heavy[crossed]
        quarters[(half, crossed)] = (
            shift(part[half - 1][:1], order, 1),
            shift(part[half + 1][1:], order, -1),
        )

    last(0)
    last(1)
    crossed_rows = swap_core(turned, pool)
    crossed_rows = after(crossed_rows, far[3], far[chips - 3])
    rows = [
        jnp.concatenate([attended, swap_core(attended, pool)], axis=0),
        jnp.concatenate([turned, crossed_rows], axis=0),
    ]

    def blocks(places):
        return {(at, part): (heavy[part][at],) for at in places for part in range(2)}

    sums = [jax.ShapeDtypeStruct((CORES * tokens, width), jnp.float32)]
    early = [0] + [at for step in range(1, half - 1) for at in (step, chips - step)]
    total = project(ring, me, rows, blocks(early), None, sums)[0]
    middle = blocks([half - 1, half + 1]) | {(half, 0): quarters[half, 0]}
    total = project(ring, me, rows, middle, total, sums)[0]
    own_out, other_out = project(
        ring,
        me,
        rows,
        {(half, 1): quarters[half, 1]},
        total,
        [jax.ShapeDtypeStruct((tokens, width), jnp.bfloat16)] * 2,
    )
    beside = swap_core(other_out, pool)
    result = jnp.where(
        core == 0,
        jnp.concatenate([own_out, beside], axis=1),
        jnp.concatenate([beside, own_out], axis=1),
    )
    return result[None]


def solution(mesh):
    pool, heads_axis = mesh.shape["pool"], mesh.shape["head"]

    def body(*args):
        weight = args[-1]
        tiled = weight.shape[0] % LANES == 0 and weight.shape[1] % (2 * CORES * LANES) == 0
        if tiled and heads_axis == 2 and pool % (2 * ROWS * CORES) == 0:
            return ring_body(pool, *args)
        return plain_body(*args)

    placed = (
        P("pool", None, "head"),
        P("pool", None, "head"),
        P("pool", None, "head"),
        P("pool", "head", None, None),
        P("pool", "head", None, None),
        P("pool", None),
        P("pool", None),
        P(("head", "pool"), None),
    )
    return jax.shard_map(
        body, mesh=mesh, in_specs=placed, out_specs=P("pool", None, "head"), check_vma=False
    )
```

```python
import functools
import math

import jax
import jax.numpy as jnp
from jax import lax
from jax.experimental import pallas as pl
from jax.experimental.pallas import tpu as pltpu
from jax.sharding import PartitionSpec as P

CORES = 2
ROWS = 4
LANES = 128
MIB = 1024 * 1024


def frequency_table(head_dim):
    pair_index = jnp.arange(head_dim // 2, dtype=jnp.float32)
    return jnp.exp(pair_index * (-2.0 / head_dim) * jnp.log(jnp.float32(500000.0)))


def reposition(vectors, offset, head_dim):
    angles = offset.astype(jnp.float32) * frequency_table(head_dim)
    cosine = jnp.cos(angles)
    sine_term = jnp.sin(angles)
    front_half = vectors[..., : head_dim // 2]
    back_half = vectors[..., head_dim // 2 :]
    return jnp.concatenate(
        [front_half * cosine - back_half * sine_term, back_half * cosine + front_half * sine_term],
        axis=-1,
    )


def absorb(state, query_rows, keys_block, values_block, allowed):
    running_peak, running_total, running_sum = state
    scores = jnp.einsum(
        "hrd,hnd->hrn", query_rows, keys_block, preferred_element_type=jnp.float32
    ) * query_rows.shape[2] ** (-0.5)
    if allowed is not None:
        scores = jnp.where(allowed[None], scores, -jnp.inf)
    new_peak = jnp.maximum(running_peak, jnp.max(scores, axis=-1))
    factor = jnp.exp(running_peak - new_peak)
    exponent = jnp.exp(scores - new_peak[..., None])
    weights = exponent.astype(jnp.bfloat16)
    new_total = running_total * factor + jnp.sum(exponent, axis=-1)
    new_sum = running_sum * factor[..., None] + jnp.einsum(
        "hrn,hnd->hrd", weights, values_block, preferred_element_type=jnp.float32
    )
    return (new_peak, new_total, new_sum)


def plain_body(
    queries,
    request_keys,
    request_values,
    cache_keys,
    cache_values,
    passage_ids,
    passage_order,
    out_weight,
):
    owned, kv_local, pass_len, head_dim = cache_keys.shape
    query_len = queries.shape[1]
    groups = queries.shape[2] // (kv_local * head_dim)
    row_count = query_len * groups
    query_rows = (
        queries[0]
        .reshape(query_len, kv_local, groups, head_dim)
        .transpose(1, 0, 2, 3)
        .reshape(kv_local, row_count, head_dim)
    )
    own_keys = request_keys[0].reshape(query_len, kv_local, head_dim).transpose(1, 0, 2)
    own_values = request_values[0].reshape(query_len, kv_local, head_dim).transpose(1, 0, 2)
    query_token = jnp.arange(row_count) // groups
    causal = jnp.arange(query_len)[None, :] <= query_token[:, None]
    state = (
        jnp.full((kv_local, row_count), -jnp.inf, jnp.float32),
        jnp.zeros((kv_local, row_count), jnp.float32),
        jnp.zeros((kv_local, row_count, head_dim), jnp.float32),
    )
    state = absorb(state, query_rows, own_keys, own_values, causal)
    slots = passage_ids[0]
    offsets = passage_order[0] * pass_len
    piece_keys = lax.all_gather(cache_keys, "pool", axis=0, tiled=True)
    piece_values = lax.all_gather(cache_values, "pool", axis=0, tiled=True)

    def visit_one(position, current):
        matches = slots == position
        offset = jnp.sum(jnp.where(matches, offsets, 0))

        def absorb_one(inner):
            placed = reposition(piece_keys[position].astype(jnp.float32), offset, head_dim).astype(
                jnp.bfloat16
            )
            return absorb(inner, query_rows, placed, piece_values[position], None)

        return lax.cond(jnp.any(matches), absorb_one, lambda inner: inner, current)

    state = lax.fori_loop(0, piece_keys.shape[0], visit_one, state)
    running_peak, running_total, running_sum = state
    attended = (running_sum / running_total[..., None]).astype(jnp.bfloat16)
    attended = (
        attended.reshape(kv_local, query_len, groups, head_dim)
        .transpose(1, 0, 2, 3)
        .reshape(query_len, kv_local * groups * head_dim)
    )
    partial_value = jnp.dot(
        attended,
        lax.all_gather(out_weight, "pool", axis=0, tiled=True),
        preferred_element_type=jnp.float32,
    )
    summed = lax.psum_scatter(
        partial_value.astype(jnp.bfloat16), "head", scatter_dimension=1, tiled=True
    )
    return summed[None]


def ring_order(chips):
    columns = chips // ROWS
    cells = []
    for row in range(ROWS):
        across = range(1, columns) if row % 2 == 0 else range(columns - 1, 0, -1)
        cells += [row * columns + column for column in across]
    return cells + [row * columns for row in reversed(range(ROWS))]


def shift(value, order, step):
    chips = len(order)
    pairs = [
        (order[at] * CORES + core, order[(at + step) % chips] * CORES + core)
        for at in range(chips)
        for core in range(CORES)
    ]
    return lax.ppermute(value, "pool", pairs)


def onward(pieces, step, order):
    chips = len(order)
    pieces[step] = shift(pieces[step - 1], order, 1)
    pieces[chips - step] = shift(pieces[(chips - step + 1) % chips], order, -1)


def after(value, *earlier):
    return lax.optimization_barrier((value, earlier))[0]


def swap_core(value, pool):
    return lax.ppermute(value, "pool", [(at, at ^ 1) for at in range(pool)])


def swap_plane(value):
    return lax.ppermute(value, "head", [(0, 1), (1, 0)])


def holder(ring, me, back):
    chips = ring.shape[0] // 2
    chip = lax.div(me[0], CORES)
    place = lax.rem(ring[chips + chip] + chips - back, chips)
    return ring[place] * CORES + lax.rem(me[0], CORES)


def attend_kernel(pieces, owned, ids, ranks, ring, me, queries, cosine, sine, *refs):
    key_pieces, value_pieces, refs = refs[:pieces], refs[pieces : 2 * pieces], refs[2 * pieces :]
    stats, keys, values, within, rank_of, key_sem, value_sem = refs[-7:]
    slots = ids.shape[0]
    kv_local, _, head_dim = keys.shape
    near, sums = refs[: -7 - kv_local], refs[-7 - kv_local : -7]
    length = key_pieces[0].shape[2]
    tokens = queries.shape[0]
    groups = queries.shape[1] // (kv_local * head_dim)
    heads = kv_local * groups
    factor = math.log2(math.e) / math.sqrt(head_dim)
    across = (((1,), (1,)), ((), ()))

    for slot in range(slots):
        passage = ids[slot]
        home = lax.div(passage, owned)
        within[home] = passage - home * owned
        rank_of[home] = ranks[slot]
    homes = [holder(ring, me, piece) for piece in range(pieces)]

    def copy(source, target, sem, piece):
        rows = pl.ds(piece * length, length)
        return pltpu.make_async_copy(
            source[piece].at[within[homes[piece]]], target.at[:, rows], sem.at[piece]
        )

    key_copies = [copy(key_pieces, keys, key_sem, piece) for piece in range(pieces)]
    value_copies = [copy(value_pieces, values, value_sem, piece) for piece in range(pieces)]
    for each in key_copies + value_copies:
        each.start()
    for piece in range(pieces):
        key_copies[piece].wait()
        rank = rank_of[homes[piece]]
        cos = cosine[pl.ds(rank, 1), :]
        sin = sine[pl.ds(rank, 1), :]
        rows = pl.ds(piece * length, length)
        for head in range(kv_local):
            block = keys[head, rows, :].astype(jnp.float32)
            turned = block * cos + pltpu.roll(block, head_dim // 2, 1) * sin
            keys[head, rows, :] = turned.astype(jnp.bfloat16)
    for each in value_copies:
        each.wait()

    lane = lax.broadcasted_iota(jnp.int32, (tokens, LANES), 1)
    marks = jnp.zeros((tokens, LANES), jnp.float32)
    for head in range(kv_local):
        spans = [
            slice((head * groups + g) * head_dim, (head * groups + g + 1) * head_dim)
            for g in range(groups)
        ]
        rows = jnp.concatenate([queries[:, span] for span in spans], axis=0)
        scores = lax.dot_general(rows, keys[head], across, preferred_element_type=jnp.float32)
        peak = jnp.max(scores, axis=1, keepdims=True)
        if near:
            own = slice(head * head_dim, (head + 1) * head_dim)
            close = lax.dot_general(
                rows, near[0][:, own], across, preferred_element_type=jnp.float32
            )
            token = lax.rem(lax.broadcasted_iota(jnp.int32, close.shape, 0), tokens)
            column = lax.broadcasted_iota(jnp.int32, close.shape, 1)
            close = jnp.where(column <= token, close, -jnp.inf)
            peak = jnp.maximum(peak, jnp.max(close, axis=1, keepdims=True))
        exponent = jnp.exp2((scores - peak) * factor)
        total = jnp.sum(exponent, axis=1, keepdims=True)
        summed = jnp.dot(
            exponent.astype(jnp.bfloat16), values[head], preferred_element_type=jnp.float32
        )
        if near:
            exponent = jnp.exp2((close - peak) * factor)
            total = total + jnp.sum(exponent, axis=1, keepdims=True)
            summed = summed + jnp.dot(
                exponent.astype(jnp.bfloat16), near[1][:, own], preferred_element_type=jnp.float32
            )
        for g in range(groups):
            part = slice(g * tokens, (g + 1) * tokens)
            sums[head][:, g * head_dim : (g + 1) * head_dim] = summed[part]
            at = head * groups + g
            marks = jnp.where(lane == at, peak[part], marks)
            marks = jnp.where(lane == heads + at, total[part], marks)
    stats[...] = marks


def attend(ids, ranks, ring, me, queries, tables, near, passages, effort=24):
    pieces = len(passages[0])
    key_pieces, value_pieces = passages
    owned, kv_local, length, head_dim = key_pieces[0].shape
    tokens, features = queries.shape
    holders = ids.shape[0]
    smem = pl.BlockSpec(memory_space=pltpu.SMEM)
    vmem = pl.BlockSpec(memory_space=pltpu.VMEM)
    seen = pieces * length
    scores = tokens * (features // head_dim) * (seen + (length if near else 0))
    return pl.pallas_call(
        functools.partial(attend_kernel, pieces, owned),
        out_shape=[jax.ShapeDtypeStruct((tokens, features // kv_local), jnp.float32)] * kv_local
        + [jax.ShapeDtypeStruct((tokens, LANES), jnp.float32)],
        in_specs=[smem] * 4
        + [vmem] * 3
        + [pl.BlockSpec(memory_space=pl.ANY)] * (2 * pieces)
        + [vmem] * len(near),
        out_specs=[vmem] * (kv_local + 1),
        scratch_shapes=[
            pltpu.VMEM((kv_local, seen, head_dim), jnp.bfloat16),
            pltpu.VMEM((kv_local, seen, head_dim), jnp.bfloat16),
            pltpu.SMEM((holders,), jnp.int32),
            pltpu.SMEM((holders,), jnp.int32),
            pltpu.SemaphoreType.DMA((pieces,)),
            pltpu.SemaphoreType.DMA((pieces,)),
        ],
        compiler_params=pltpu.CompilerParams(vmem_limit_bytes=32 * MIB),
        cost_estimate=pl.CostEstimate(
            flops=effort * scores * head_dim, bytes_accessed=4 * MIB, transcendentals=scores
        ),
        name="attend",
    )(ids, ranks, ring, me, queries, *tables, *key_pieces, *value_pieces, *near)


def combine_kernel(head_dim, *refs):
    attended, refs = refs[-1], refs[:-1]
    count = len(refs) // 2
    sums, stats = refs[: count - 1], refs[count - 1]
    sums_in, stats_in = refs[count:-1], refs[-1]
    groups = sums[0].shape[1] // head_dim
    heads = groups * len(sums)
    factor = math.log2(math.e) / math.sqrt(head_dim)
    for head in range(heads):
        block, at = divmod(head, groups)
        columns = slice(at * head_dim, (at + 1) * head_dim)
        peak_a, peak_b = stats[:, head : head + 1], stats_in[:, head : head + 1]
        at = heads + head
        total_a, total_b = stats[:, at : at + 1], stats_in[:, at : at + 1]
        peak = jnp.maximum(peak_a, peak_b)
        part_a = jnp.exp2((peak_a - peak) * factor)
        part_b = jnp.exp2((peak_b - peak) * factor)
        total = total_a * part_a + total_b * part_b
        value = sums[block][:, columns] * part_a + sums_in[block][:, columns] * part_b
        columns = slice(head * head_dim, (head + 1) * head_dim)
        attended[:, columns] = (value / total).astype(attended.dtype)


def combine(head_dim, state, state_in):
    tokens, width = state[0].shape
    size = tokens * width * (len(state) - 1)
    vmem = pl.BlockSpec(memory_space=pltpu.VMEM)
    return pl.pallas_call(
        functools.partial(combine_kernel, head_dim),
        out_shape=jax.ShapeDtypeStruct((tokens, size // tokens), jnp.bfloat16),
        in_specs=[vmem] * (2 * len(state)),
        out_specs=vmem,
        compiler_params=pltpu.CompilerParams(vmem_limit_bytes=24 * MIB),
        cost_estimate=pl.CostEstimate(flops=4 * size, bytes_accessed=10 * size, transcendentals=0),
        name="combine",
    )(*state, *state_in)


def project_kernel(items, based, ring, me, own_rows, other_rows, *refs):
    count = sum(number for _, _, number in items)
    blocks, refs = refs[:count], refs[count:]
    base = None
    if based:
        base, refs = refs[0], refs[1:]
    results, (held, total, sems) = refs[:-3], refs[-3:]
    span = held.shape[2]
    copies, at = [], 0
    for item, (_, _, number) in enumerate(items):
        targets = [held.at[item]] if number == 1 else [held.at[item, pl.ds(i, 1)] for i in range(number)]
        copies.append(
            [
                pltpu.make_async_copy(blocks[at + i], target, sems.at[at + i])
                for i, target in enumerate(targets)
            ]
        )
        at += number
    for group in copies:
        for copy in group:
            copy.start()
    for item, (place, crossed, _) in enumerate(items):
        for copy in copies[item]:
            copy.wait()
        home = holder(ring, me, place)
        if crossed:
            home = home + 1 - 2 * lax.rem(home, CORES)
        columns = pl.ds(pl.multiple_of(home * span, span), span)
        value = jnp.dot(
            jnp.concatenate([rows[:, columns] for rows in (own_rows, other_rows)], axis=1),
            jnp.concatenate([held[item, plane] for plane in range(2)], axis=0),
            preferred_element_type=jnp.float32,
        )
        if item:
            value = value + total[...]
        elif base is not None:
            value = value + base[...]
        if item + 1 < len(items):
            total[...] = value
    tokens = results[0].shape[0]
    for part, result in enumerate(results):
        result[...] = value[part * tokens : (part + 1) * tokens].astype(result.dtype)


def project(ring, me, rows, blocks, base, shapes):
    items = tuple((place, crossed, len(parts)) for (place, crossed), parts in blocks.items())
    flat = [part for parts in blocks.values() for part in parts]
    tokens = rows[0].shape[0]
    span, width = flat[0].shape[1:]
    size = len(items) * 2 * span * width
    smem = pl.BlockSpec(memory_space=pltpu.SMEM)
    vmem = pl.BlockSpec(memory_space=pltpu.VMEM)
    return pl.pallas_call(
        functools.partial(project_kernel, items, base is not None),
        out_shape=shapes,
        in_specs=[smem] * 2
        + [vmem] * 2
        + [pl.BlockSpec(memory_space=pl.ANY)] * len(flat)
        + ([vmem] if base is not None else []),
        out_specs=[vmem] * len(shapes),
        scratch_shapes=[
            pltpu.VMEM((len(items), 2, span, width), jnp.bfloat16),
            pltpu.VMEM((tokens, width), jnp.float32),
            pltpu.SemaphoreType.DMA((len(flat),)),
        ],
        compiler_params=pltpu.CompilerParams(vmem_limit_bytes=32 * MIB),
        cost_estimate=pl.CostEstimate(
            flops=2 * tokens * size, bytes_accessed=2 * size + 4 * tokens * width, transcendentals=0
        ),
        name="project",
    )(ring, me, *rows, *flat, *([base] if base is not None else []))


def rotation_tables(ranks, length, head_dim):
    offsets = (jnp.arange(ranks) * length).astype(jnp.float32)
    angles = offsets[:, None] * frequency_table(head_dim)[None, :]
    cosine, sine = jnp.cos(angles), jnp.sin(angles)
    return (
        jnp.concatenate([cosine, cosine], axis=1),
        jnp.concatenate([-sine, sine], axis=1),
    )


def ring_body(
    pool,
    queries,
    request_keys,
    request_values,
    cache_keys,
    cache_values,
    passage_ids,
    passage_order,
    out_weight,
):
    _, _, pass_len, head_dim = cache_keys.shape
    tokens = queries.shape[1]
    chips = pool // CORES
    half = chips // 2
    order = ring_order(chips)
    ring = jnp.asarray(order + [order.index(chip) for chip in range(chips)], jnp.int32)
    index = lax.axis_index("pool")
    me = jnp.reshape(index, (1,))
    core = lax.rem(index, CORES)
    plane = lax.axis_index("head")

    span = out_weight.shape[1] // 2
    width = span // CORES
    other_queries = swap_core(queries[0], pool)
    weight, other_queries = lax.optimization_barrier((out_weight, other_queries))
    across = swap_plane(
        lax.dynamic_slice_in_dim(weight, (1 - plane) * span, span, axis=1)
    )

    kept = {0: cache_keys}, {0: cache_values}
    for pieces in kept:
        onward(pieces, 1, order)
    for step in range(2, half):
        for pieces in kept:
            onward(pieces, step, order)

    out_weight, across = after(
        (out_weight, across),
        kept[0][2], kept[0][chips - 2],
    )

    def columns(to_core):
        first = to_core * width
        return jnp.stack(
            [
                lax.dynamic_slice_in_dim(out_weight, plane * span + first, width, axis=1),
                lax.dynamic_slice_in_dim(across, first, width, axis=1),
            ]
        )

    near, far = heavy = {0: columns(core)}, {0: swap_core(columns(1 - core), pool)}
    near[0] = after(near[0], *[kept[1][at] for at in (2, chips - 2)])
    far[0] = after(far[0], *[kept[0][at] for at in (half - 1, half + 1)])
    for step in range(1, half):
        for pieces in heavy:
            onward(pieces, step, order)

    queries, picks, last_keys, last_values = after(
        (
            queries[0],
            jnp.concatenate([passage_ids, passage_order], axis=0),
            kept[0][half - 1],
            kept[1][half + 1],
        ),
        near[1],
        near[chips - 1],
    )
    kept[0][half] = shift(last_keys, order, 1)
    kept[1][half] = shift(last_values, order, -1)
    passages = [[pieces[at] for at in range(chips)] for pieces in kept]

    picks_in = swap_core(picks, pool)
    other_queries = after(
        other_queries, far[1], far[chips - 1]
    )
    tables = rotation_tables(passage_ids.shape[1], pass_len, head_dim)
    other = attend(picks_in[0], picks_in[1], ring, me, other_queries, tables, (), passages)
    own_block = (request_keys[0], request_values[0])
    other_in = [swap_core(value, pool) for value in other]
    queries, other_in = after((queries, other_in), near[2], near[chips - 2])
    own = attend(picks[0], picks[1], ring, me, queries, tables, own_block, passages, 1)
    own = after(own, far[2], far[chips - 2])

    attended = combine(head_dim, own, other_in)
    turned = after(swap_plane(attended), near[3], near[chips - 3])
    quarters = {}

    def last(crossed):
        part = heavy[crossed]
        quarters[(half, crossed)] = (
            shift(part[half - 1][:1], order, 1),
            shift(part[half + 1][1:], order, -1),
        )

    last(0)
    last(1)
    crossed_rows = swap_core(turned, pool)
    crossed_rows = after(crossed_rows, far[3], far[chips - 3])
    rows = [
        jnp.concatenate([attended, swap_core(attended, pool)], axis=0),
        jnp.concatenate([turned, crossed_rows], axis=0),
    ]

    def blocks(places):
        return {(at, part): (heavy[part][at],) for at in places for part in range(2)}

    sums = [jax.ShapeDtypeStruct((CORES * tokens, width), jnp.float32)]
    early = [0] + [at for step in range(1, half - 1) for at in (step, chips - step)]
    total = project(ring, me, rows, blocks(early), None, sums)[0]
    middle = blocks([half - 1, half + 1]) | {(half, 0): quarters[half, 0]}
    total = project(ring, me, rows, middle, total, sums)[0]
    own_out, other_out = project(
        ring,
        me,
        rows,
        {(half, 1): quarters[half, 1]},
        total,
        [jax.ShapeDtypeStruct((tokens, width), jnp.bfloat16)] * 2,
    )
    beside = swap_core(other_out, pool)
    result = jnp.where(
        core == 0,
        jnp.concatenate([own_out, beside], axis=1),
        jnp.concatenate([beside, own_out], axis=1),
    )
    return result[None]


def solution(mesh):
    pool, heads_axis = mesh.shape["pool"], mesh.shape["head"]

    def body(*args):
        weight = args[-1]
        tiled = weight.shape[0] % LANES == 0 and weight.shape[1] % (2 * CORES * LANES) == 0
        if tiled and heads_axis == 2 and pool % (2 * ROWS * CORES) == 0:
            return ring_body(pool, *args)
        return plain_body(*args)

    placed = (
        P("pool", None, "head"),
        P("pool", None, "head"),
        P("pool", None, "head"),
        P("pool", "head", None, None),
        P("pool", "head", None, None),
        P("pool", None),
        P("pool", None),
        P(("head", "pool"), None),
    )
    return jax.shard_map(
        body, mesh=mesh, in_specs=placed, out_specs=P("pool", None, "head"), check_vma=False
    )
```

```python
import functools
import math

import jax
import jax.numpy as jnp
from jax import lax
from jax.experimental import pallas as pl
from jax.experimental.pallas import tpu as pltpu
from jax.sharding import PartitionSpec as P

CORES = 2
ROWS = 4
LANES = 128
MIB = 1024 * 1024


def frequency_table(head_dim):
    pair_index = jnp.arange(head_dim // 2, dtype=jnp.float32)
    return jnp.exp(pair_index * (-2.0 / head_dim) * jnp.log(jnp.float32(500000.0)))


def reposition(vectors, offset, head_dim):
    angles = offset.astype(jnp.float32) * frequency_table(head_dim)
    cosine = jnp.cos(angles)
    sine_term = jnp.sin(angles)
    front_half = vectors[..., : head_dim // 2]
    back_half = vectors[..., head_dim // 2 :]
    return jnp.concatenate(
        [front_half * cosine - back_half * sine_term, back_half * cosine + front_half * sine_term],
        axis=-1,
    )


def absorb(state, query_rows, keys_block, values_block, allowed):
    running_peak, running_total, running_sum = state
    scores = jnp.einsum(
        "hrd,hnd->hrn", query_rows, keys_block, preferred_element_type=jnp.float32
    ) * query_rows.shape[2] ** (-0.5)
    if allowed is not None:
        scores = jnp.where(allowed[None], scores, -jnp.inf)
    new_peak = jnp.maximum(running_peak, jnp.max(scores, axis=-1))
    factor = jnp.exp(running_peak - new_peak)
    exponent = jnp.exp(scores - new_peak[..., None])
    weights = exponent.astype(jnp.bfloat16)
    new_total = running_total * factor + jnp.sum(exponent, axis=-1)
    new_sum = running_sum * factor[..., None] + jnp.einsum(
        "hrn,hnd->hrd", weights, values_block, preferred_element_type=jnp.float32
    )
    return (new_peak, new_total, new_sum)


def plain_body(
    queries,
    request_keys,
    request_values,
    cache_keys,
    cache_values,
    passage_ids,
    passage_order,
    out_weight,
):
    owned, kv_local, pass_len, head_dim = cache_keys.shape
    query_len = queries.shape[1]
    groups = queries.shape[2] // (kv_local * head_dim)
    row_count = query_len * groups
    query_rows = (
        queries[0]
        .reshape(query_len, kv_local, groups, head_dim)
        .transpose(1, 0, 2, 3)
        .reshape(kv_local, row_count, head_dim)
    )
    own_keys = request_keys[0].reshape(query_len, kv_local, head_dim).transpose(1, 0, 2)
    own_values = request_values[0].reshape(query_len, kv_local, head_dim).transpose(1, 0, 2)
    query_token = jnp.arange(row_count) // groups
    causal = jnp.arange(query_len)[None, :] <= query_token[:, None]
    state = (
        jnp.full((kv_local, row_count), -jnp.inf, jnp.float32),
        jnp.zeros((kv_local, row_count), jnp.float32),
        jnp.zeros((kv_local, row_count, head_dim), jnp.float32),
    )
    state = absorb(state, query_rows, own_keys, own_values, causal)
    slots = passage_ids[0]
    offsets = passage_order[0] * pass_len
    piece_keys = lax.all_gather(cache_keys, "pool", axis=0, tiled=True)
    piece_values = lax.all_gather(cache_values, "pool", axis=0, tiled=True)

    def visit_one(position, current):
        matches = slots == position
        offset = jnp.sum(jnp.where(matches, offsets, 0))

        def absorb_one(inner):
            placed = reposition(piece_keys[position].astype(jnp.float32), offset, head_dim).astype(
                jnp.bfloat16
            )
            return absorb(inner, query_rows, placed, piece_values[position], None)

        return lax.cond(jnp.any(matches), absorb_one, lambda inner: inner, current)

    state = lax.fori_loop(0, piece_keys.shape[0], visit_one, state)
    running_peak, running_total, running_sum = state
    attended = (running_sum / running_total[..., None]).astype(jnp.bfloat16)
    attended = (
        attended.reshape(kv_local, query_len, groups, head_dim)
        .transpose(1, 0, 2, 3)
        .reshape(query_len, kv_local * groups * head_dim)
    )
    partial_value = jnp.dot(
        attended,
        lax.all_gather(out_weight, "pool", axis=0, tiled=True),
        preferred_element_type=jnp.float32,
    )
    summed = lax.psum_scatter(
        partial_value.astype(jnp.bfloat16), "head", scatter_dimension=1, tiled=True
    )
    return summed[None]


def ring_order(chips):
    columns = chips // ROWS
    cells = []
    for row in range(ROWS):
        across = range(1, columns) if row % 2 == 0 else range(columns - 1, 0, -1)
        cells += [row * columns + column for column in across]
    return cells + [row * columns for row in reversed(range(ROWS))]


def shift(value, order, step):
    chips = len(order)
    pairs = [
        (order[at] * CORES + core, order[(at + step) % chips] * CORES + core)
        for at in range(chips)
        for core in range(CORES)
    ]
    return lax.ppermute(value, "pool", pairs)


def onward(pieces, step, order):
    chips = len(order)
    pieces[step] = shift(pieces[step - 1], order, 1)
    pieces[chips - step] = shift(pieces[(chips - step + 1) % chips], order, -1)


def after(value, *earlier):
    return lax.optimization_barrier((value, earlier))[0]


def swap_core(value, pool):
    return lax.ppermute(value, "pool", [(at, at ^ 1) for at in range(pool)])


def swap_plane(value):
    return lax.ppermute(value, "head", [(0, 1), (1, 0)])


def holder(ring, me, back):
    chips = ring.shape[0] // 2
    chip = lax.div(me[0], CORES)
    place = lax.rem(ring[chips + chip] + chips - back, chips)
    return ring[place] * CORES + lax.rem(me[0], CORES)


def attend_kernel(pieces, owned, ids, ranks, ring, me, queries, cosine, sine, *refs):
    key_pieces, value_pieces, refs = refs[:pieces], refs[pieces : 2 * pieces], refs[2 * pieces :]
    stats, keys, values, within, rank_of, key_sem, value_sem = refs[-7:]
    slots = ids.shape[0]
    kv_local, _, head_dim = keys.shape
    near, sums = refs[: -7 - kv_local], refs[-7 - kv_local : -7]
    length = key_pieces[0].shape[2]
    tokens = queries.shape[0]
    groups = queries.shape[1] // (kv_local * head_dim)
    heads = kv_local * groups
    factor = math.log2(math.e) / math.sqrt(head_dim)
    across = (((1,), (1,)), ((), ()))

    for slot in range(slots):
        passage = ids[slot]
        home = lax.div(passage, owned)
        within[home] = passage - home * owned
        rank_of[home] = ranks[slot]
    homes = [holder(ring, me, piece) for piece in range(pieces)]

    def copy(source, target, sem, piece):
        rows = pl.ds(piece * length, length)
        return pltpu.make_async_copy(
            source[piece].at[within[homes[piece]]], target.at[:, rows], sem.at[piece]
        )

    key_copies = [copy(key_pieces, keys, key_sem, piece) for piece in range(pieces)]
    value_copies = [copy(value_pieces, values, value_sem, piece) for piece in range(pieces)]
    for each in key_copies + value_copies:
        each.start()
    for piece in range(pieces):
        key_copies[piece].wait()
        rank = rank_of[homes[piece]]
        cos = cosine[pl.ds(rank, 1), :]
        sin = sine[pl.ds(rank, 1), :]
        rows = pl.ds(piece * length, length)
        for head in range(kv_local):
            block = keys[head, rows, :].astype(jnp.float32)
            turned = block * cos + pltpu.roll(block, head_dim // 2, 1) * sin
            keys[head, rows, :] = turned.astype(jnp.bfloat16)
    for each in value_copies:
        each.wait()

    lane = lax.broadcasted_iota(jnp.int32, (tokens, LANES), 1)
    marks = jnp.zeros((tokens, LANES), jnp.float32)
    for head in range(kv_local):
        spans = [
            slice((head * groups + g) * head_dim, (head * groups + g + 1) * head_dim)
            for g in range(groups)
        ]
        rows = jnp.concatenate([queries[:, span] for span in spans], axis=0)
        scores = lax.dot_general(rows, keys[head], across, preferred_element_type=jnp.float32)
        peak = jnp.max(scores, axis=1, keepdims=True)
        if near:
            own = slice(head * head_dim, (head + 1) * head_dim)
            close = lax.dot_general(
                rows, near[0][:, own], across, preferred_element_type=jnp.float32
            )
            token = lax.rem(lax.broadcasted_iota(jnp.int32, close.shape, 0), tokens)
            column = lax.broadcasted_iota(jnp.int32, close.shape, 1)
            close = jnp.where(column <= token, close, -jnp.inf)
            peak = jnp.maximum(peak, jnp.max(close, axis=1, keepdims=True))
        exponent = jnp.exp2((scores - peak) * factor)
        total = jnp.sum(exponent, axis=1, keepdims=True)
        summed = jnp.dot(
            exponent.astype(jnp.bfloat16), values[head], preferred_element_type=jnp.float32
        )
        if near:
            exponent = jnp.exp2((close - peak) * factor)
            total = total + jnp.sum(exponent, axis=1, keepdims=True)
            summed = summed + jnp.dot(
                exponent.astype(jnp.bfloat16), near[1][:, own], preferred_element_type=jnp.float32
            )
        for g in range(groups):
            part = slice(g * tokens, (g + 1) * tokens)
            sums[head][:, g * head_dim : (g + 1) * head_dim] = summed[part]
            at = head * groups + g
            marks = jnp.where(lane == at, peak[part], marks)
            marks = jnp.where(lane == heads + at, total[part], marks)
    stats[...] = marks


def attend(ids, ranks, ring, me, queries, tables, near, passages, effort=24):
    pieces = len(passages[0])
    key_pieces, value_pieces = passages
    owned, kv_local, length, head_dim = key_pieces[0].shape
    tokens, features = queries.shape
    holders = ids.shape[0]
    smem = pl.BlockSpec(memory_space=pltpu.SMEM)
    vmem = pl.BlockSpec(memory_space=pltpu.VMEM)
    seen = pieces * length
    scores = tokens * (features // head_dim) * (seen + (length if near else 0))
    return pl.pallas_call(
        functools.partial(attend_kernel, pieces, owned),
        out_shape=[jax.ShapeDtypeStruct((tokens, features // kv_local), jnp.float32)] * kv_local
        + [jax.ShapeDtypeStruct((tokens, LANES), jnp.float32)],
        in_specs=[smem] * 4
        + [vmem] * 3
        + [pl.BlockSpec(memory_space=pl.ANY)] * (2 * pieces)
        + [vmem] * len(near),
        out_specs=[vmem] * (kv_local + 1),
        scratch_shapes=[
            pltpu.VMEM((kv_local, seen, head_dim), jnp.bfloat16),
            pltpu.VMEM((kv_local, seen, head_dim), jnp.bfloat16),
            pltpu.SMEM((holders,), jnp.int32),
            pltpu.SMEM((holders,), jnp.int32),
            pltpu.SemaphoreType.DMA((pieces,)),
            pltpu.SemaphoreType.DMA((pieces,)),
        ],
        compiler_params=pltpu.CompilerParams(vmem_limit_bytes=32 * MIB),
        cost_estimate=pl.CostEstimate(
            flops=effort * scores * head_dim, bytes_accessed=4 * MIB, transcendentals=scores
        ),
        name="attend",
    )(ids, ranks, ring, me, queries, *tables, *key_pieces, *value_pieces, *near)


def combine_kernel(head_dim, *refs):
    attended, refs = refs[-1], refs[:-1]
    count = len(refs) // 2
    sums, stats = refs[: count - 1], refs[count - 1]
    sums_in, stats_in = refs[count:-1], refs[-1]
    groups = sums[0].shape[1] // head_dim
    heads = groups * len(sums)
    factor = math.log2(math.e) / math.sqrt(head_dim)
    for head in range(heads):
        block, at = divmod(head, groups)
        columns = slice(at * head_dim, (at + 1) * head_dim)
        peak_a, peak_b = stats[:, head : head + 1], stats_in[:, head : head + 1]
        at = heads + head
        total_a, total_b = stats[:, at : at + 1], stats_in[:, at : at + 1]
        peak = jnp.maximum(peak_a, peak_b)
        part_a = jnp.exp2((peak_a - peak) * factor)
        part_b = jnp.exp2((peak_b - peak) * factor)
        total = total_a * part_a + total_b * part_b
        value = sums[block][:, columns] * part_a + sums_in[block][:, columns] * part_b
        columns = slice(head * head_dim, (head + 1) * head_dim)
        attended[:, columns] = (value / total).astype(attended.dtype)


def combine(head_dim, state, state_in):
    tokens, width = state[0].shape
    size = tokens * width * (len(state) - 1)
    vmem = pl.BlockSpec(memory_space=pltpu.VMEM)
    return pl.pallas_call(
        functools.partial(combine_kernel, head_dim),
        out_shape=jax.ShapeDtypeStruct((tokens, size // tokens), jnp.bfloat16),
        in_specs=[vmem] * (2 * len(state)),
        out_specs=vmem,
        compiler_params=pltpu.CompilerParams(vmem_limit_bytes=24 * MIB),
        cost_estimate=pl.CostEstimate(flops=4 * size, bytes_accessed=10 * size, transcendentals=0),
        name="combine",
    )(*state, *state_in)


def project_kernel(items, based, ring, me, own_rows, other_rows, *refs):
    count = sum(len(heights) for _, _, heights in items)
    blocks, refs = refs[:count], refs[count:]
    base = None
    if based:
        base, refs = refs[0], refs[1:]
    results, (held, total, sems) = refs[:-3], refs[-3:]
    span = held.shape[1] // 2
    copies, at = [], 0
    for item, (_, _, heights) in enumerate(items):
        copies.append([])
        for i, height in enumerate(heights):
            target = held.at[item, pl.ds(sum(heights[:i]), height)]
            copies[-1].append(pltpu.make_async_copy(blocks[at], target, sems.at[at]))
            at += 1
    for group in copies:
        for copy in group:
            copy.start()
    for item, (place, crossed, _) in enumerate(items):
        for copy in copies[item]:
            copy.wait()
        home = holder(ring, me, place)
        if crossed:
            home = home + 1 - 2 * lax.rem(home, CORES)
        columns = pl.ds(pl.multiple_of(home * span, span), span)
        value = jnp.dot(
            jnp.concatenate([rows[:, columns] for rows in (own_rows, other_rows)], axis=1),
            held[item],
            preferred_element_type=jnp.float32,
        )
        if item:
            value = value + total[...]
        elif base is not None:
            value = value + base[...]
        if item + 1 < len(items):
            total[...] = value
    tokens = results[0].shape[0]
    for part, result in enumerate(results):
        result[...] = value[part * tokens : (part + 1) * tokens].astype(result.dtype)


def project(ring, me, rows, blocks, base, shapes):
    flat = [part.reshape(-1, part.shape[-1]) for parts in blocks.values() for part in parts]
    heights = iter([part.shape[0] for part in flat])
    items = tuple(
        (place, crossed, tuple(next(heights) for _ in parts))
        for (place, crossed), parts in blocks.items()
    )
    tokens, width = rows[0].shape[0], flat[0].shape[1]
    height = sum(items[0][2])
    size = len(items) * height * width
    smem = pl.BlockSpec(memory_space=pltpu.SMEM)
    vmem = pl.BlockSpec(memory_space=pltpu.VMEM)
    return pl.pallas_call(
        functools.partial(project_kernel, items, base is not None),
        out_shape=shapes,
        in_specs=[smem] * 2
        + [vmem] * 2
        + [pl.BlockSpec(memory_space=pl.ANY)] * len(flat)
        + ([vmem] if base is not None else []),
        out_specs=[vmem] * len(shapes),
        scratch_shapes=[
            pltpu.VMEM((len(items), height, width), jnp.bfloat16),
            pltpu.VMEM((tokens, width), jnp.float32),
            pltpu.SemaphoreType.DMA((len(flat),)),
        ],
        compiler_params=pltpu.CompilerParams(vmem_limit_bytes=32 * MIB),
        cost_estimate=pl.CostEstimate(
            flops=2 * tokens * size, bytes_accessed=2 * size + 4 * tokens * width, transcendentals=0
        ),
        name="project",
    )(ring, me, *rows, *flat, *([base] if base is not None else []))


def rotation_tables(ranks, length, head_dim):
    offsets = (jnp.arange(ranks) * length).astype(jnp.float32)
    angles = offsets[:, None] * frequency_table(head_dim)[None, :]
    cosine, sine = jnp.cos(angles), jnp.sin(angles)
    return (
        jnp.concatenate([cosine, cosine], axis=1),
        jnp.concatenate([-sine, sine], axis=1),
    )


def ring_body(
    pool,
    queries,
    request_keys,
    request_values,
    cache_keys,
    cache_values,
    passage_ids,
    passage_order,
    out_weight,
):
    _, _, pass_len, head_dim = cache_keys.shape
    tokens = queries.shape[1]
    chips = pool // CORES
    half = chips // 2
    order = ring_order(chips)
    ring = jnp.asarray(order + [order.index(chip) for chip in range(chips)], jnp.int32)
    index = lax.axis_index("pool")
    me = jnp.reshape(index, (1,))
    core = lax.rem(index, CORES)
    plane = lax.axis_index("head")

    span = out_weight.shape[1] // 2
    width = span // CORES
    other_queries = swap_core(queries[0], pool)
    weight, other_queries = lax.optimization_barrier((out_weight, other_queries))
    across = swap_plane(
        lax.dynamic_slice_in_dim(weight, (1 - plane) * span, span, axis=1)
    )

    kept = {0: cache_keys}, {0: cache_values}
    for pieces in kept:
        onward(pieces, 1, order)
    for step in range(2, half):
        for pieces in kept:
            onward(pieces, step, order)

    out_weight, across = after(
        (out_weight, across),
        kept[0][2], kept[0][chips - 2],
    )

    def columns(to_core):
        first = to_core * width
        return jnp.stack(
            [
                lax.dynamic_slice_in_dim(out_weight, plane * span + first, width, axis=1),
                lax.dynamic_slice_in_dim(across, first, width, axis=1),
            ]
        )

    near, far = heavy = {0: columns(core)}, {0: swap_core(columns(1 - core), pool)}
    near[0] = after(near[0], *[kept[1][at] for at in (2, chips - 2)])
    far[0] = after(far[0], *[kept[0][at] for at in (half - 1, half + 1)])
    for step in range(1, half):
        for pieces in heavy:
            onward(pieces, step, order)

    queries, picks, last_keys, last_values = after(
        (
            queries[0],
            jnp.concatenate([passage_ids, passage_order], axis=0),
            kept[0][half - 1],
            kept[1][half + 1],
        ),
        near[1],
        near[chips - 1],
    )
    kept[0][half] = shift(last_keys, order, 1)
    kept[1][half] = shift(last_values, order, -1)
    passages = [[pieces[at] for at in range(chips)] for pieces in kept]

    picks_in = swap_core(picks, pool)
    other_queries = after(
        other_queries, far[1], far[chips - 1]
    )
    tables = rotation_tables(passage_ids.shape[1], pass_len, head_dim)
    other = attend(picks_in[0], picks_in[1], ring, me, other_queries, tables, (), passages)
    own_block = (request_keys[0], request_values[0])
    other_in = [swap_core(value, pool) for value in other]
    queries, other_in = after((queries, other_in), near[2], near[chips - 2])
    own = attend(picks[0], picks[1], ring, me, queries, tables, own_block, passages, 1)
    own = after(own, far[2], far[chips - 2])

    attended = combine(head_dim, own, other_in)
    turned = after(swap_plane(attended), near[3], near[chips - 3])
    quarters = {}

    def last(crossed, cut):
        ahead, back = (
            heavy[crossed][at].reshape(-1, width) for at in (half - 1, half + 1)
        )
        quarters[(half, crossed)] = (shift(ahead[:cut], order, 1), shift(back[cut:], order, -1))

    rows_held = CORES * heavy[0][0].shape[1]
    last(0, rows_held * 9 // 16)
    last(1, rows_held * 8 // 16)
    crossed_rows = swap_core(turned, pool)
    crossed_rows = after(crossed_rows, far[3], far[chips - 3])
    rows = [
        jnp.concatenate([attended, swap_core(attended, pool)], axis=0),
        jnp.concatenate([turned, crossed_rows], axis=0),
    ]

    def blocks(places):
        return {(at, part): (heavy[part][at],) for at in places for part in range(2)}

    sums = [jax.ShapeDtypeStruct((CORES * tokens, width), jnp.float32)]
    early = [0] + [at for step in range(1, half - 1) for at in (step, chips - step)]
    total = project(ring, me, rows, blocks(early), None, sums)[0]
    middle = blocks([half - 1, half + 1]) | {(half, 0): quarters[half, 0]}
    total = project(ring, me, rows, middle, total, sums)[0]
    own_out, other_out = project(
        ring,
        me,
        rows,
        {(half, 1): quarters[half, 1]},
        total,
        [jax.ShapeDtypeStruct((tokens, width), jnp.bfloat16)] * 2,
    )
    beside = swap_core(other_out, pool)
    result = jnp.where(
        core == 0,
        jnp.concatenate([own_out, beside], axis=1),
        jnp.concatenate([beside, own_out], axis=1),
    )
    return result[None]


def solution(mesh):
    pool, heads_axis = mesh.shape["pool"], mesh.shape["head"]

    def body(*args):
        weight = args[-1]
        tiled = weight.shape[0] % LANES == 0 and weight.shape[1] % (2 * CORES * LANES) == 0
        if tiled and heads_axis == 2 and pool % (2 * ROWS * CORES) == 0:
            return ring_body(pool, *args)
        return plain_body(*args)

    placed = (
        P("pool", None, "head"),
        P("pool", None, "head"),
        P("pool", None, "head"),
        P("pool", "head", None, None),
        P("pool", "head", None, None),
        P("pool", None),
        P("pool", None),
        P(("head", "pool"), None),
    )
    return jax.shard_map(
        body, mesh=mesh, in_specs=placed, out_specs=P("pool", None, "head"), check_vma=False
    )
```

```python
import functools
import math

import jax
import jax.numpy as jnp
from jax import lax
from jax.experimental import pallas as pl
from jax.experimental.pallas import tpu as pltpu
from jax.sharding import PartitionSpec as P

CORES = 2
ROWS = 4
LANES = 128
MIB = 1024 * 1024


def frequency_table(head_dim):
    pair_index = jnp.arange(head_dim // 2, dtype=jnp.float32)
    return jnp.exp(pair_index * (-2.0 / head_dim) * jnp.log(jnp.float32(500000.0)))


def reposition(vectors, offset, head_dim):
    angles = offset.astype(jnp.float32) * frequency_table(head_dim)
    cosine = jnp.cos(angles)
    sine_term = jnp.sin(angles)
    front_half = vectors[..., : head_dim // 2]
    back_half = vectors[..., head_dim // 2 :]
    return jnp.concatenate(
        [front_half * cosine - back_half * sine_term, back_half * cosine + front_half * sine_term],
        axis=-1,
    )


def absorb(state, query_rows, keys_block, values_block, allowed):
    running_peak, running_total, running_sum = state
    scores = jnp.einsum(
        "hrd,hnd->hrn", query_rows, keys_block, preferred_element_type=jnp.float32
    ) * query_rows.shape[2] ** (-0.5)
    if allowed is not None:
        scores = jnp.where(allowed[None], scores, -jnp.inf)
    new_peak = jnp.maximum(running_peak, jnp.max(scores, axis=-1))
    factor = jnp.exp(running_peak - new_peak)
    exponent = jnp.exp(scores - new_peak[..., None])
    weights = exponent.astype(jnp.bfloat16)
    new_total = running_total * factor + jnp.sum(exponent, axis=-1)
    new_sum = running_sum * factor[..., None] + jnp.einsum(
        "hrn,hnd->hrd", weights, values_block, preferred_element_type=jnp.float32
    )
    return (new_peak, new_total, new_sum)


def plain_body(
    queries,
    request_keys,
    request_values,
    cache_keys,
    cache_values,
    passage_ids,
    passage_order,
    out_weight,
):
    owned, kv_local, pass_len, head_dim = cache_keys.shape
    query_len = queries.shape[1]
    groups = queries.shape[2] // (kv_local * head_dim)
    row_count = query_len * groups
    query_rows = (
        queries[0]
        .reshape(query_len, kv_local, groups, head_dim)
        .transpose(1, 0, 2, 3)
        .reshape(kv_local, row_count, head_dim)
    )
    own_keys = request_keys[0].reshape(query_len, kv_local, head_dim).transpose(1, 0, 2)
    own_values = request_values[0].reshape(query_len, kv_local, head_dim).transpose(1, 0, 2)
    query_token = jnp.arange(row_count) // groups
    causal = jnp.arange(query_len)[None, :] <= query_token[:, None]
    state = (
        jnp.full((kv_local, row_count), -jnp.inf, jnp.float32),
        jnp.zeros((kv_local, row_count), jnp.float32),
        jnp.zeros((kv_local, row_count, head_dim), jnp.float32),
    )
    state = absorb(state, query_rows, own_keys, own_values, causal)
    slots = passage_ids[0]
    offsets = passage_order[0] * pass_len
    piece_keys = lax.all_gather(cache_keys, "pool", axis=0, tiled=True)
    piece_values = lax.all_gather(cache_values, "pool", axis=0, tiled=True)

    def visit_one(position, current):
        matches = slots == position
        offset = jnp.sum(jnp.where(matches, offsets, 0))

        def absorb_one(inner):
            placed = reposition(piece_keys[position].astype(jnp.float32), offset, head_dim).astype(
                jnp.bfloat16
            )
            return absorb(inner, query_rows, placed, piece_values[position], None)

        return lax.cond(jnp.any(matches), absorb_one, lambda inner: inner, current)

    state = lax.fori_loop(0, piece_keys.shape[0], visit_one, state)
    running_peak, running_total, running_sum = state
    attended = (running_sum / running_total[..., None]).astype(jnp.bfloat16)
    attended = (
        attended.reshape(kv_local, query_len, groups, head_dim)
        .transpose(1, 0, 2, 3)
        .reshape(query_len, kv_local * groups * head_dim)
    )
    partial_value = jnp.dot(
        attended,
        lax.all_gather(out_weight, "pool", axis=0, tiled=True),
        preferred_element_type=jnp.float32,
    )
    summed = lax.psum_scatter(
        partial_value.astype(jnp.bfloat16), "head", scatter_dimension=1, tiled=True
    )
    return summed[None]


def ring_order(chips):
    columns = chips // ROWS
    cells = []
    for row in range(ROWS):
        across = range(1, columns) if row % 2 == 0 else range(columns - 1, 0, -1)
        cells += [row * columns + column for column in across]
    return cells + [row * columns for row in reversed(range(ROWS))]


def shift(value, order, step):
    chips = len(order)
    pairs = [
        (order[at] * CORES + core, order[(at + step) % chips] * CORES + core)
        for at in range(chips)
        for core in range(CORES)
    ]
    return lax.ppermute(value, "pool", pairs)


def onward(pieces, step, order):
    chips = len(order)
    pieces[step] = shift(pieces[step - 1], order, 1)
    pieces[chips - step] = shift(pieces[(chips - step + 1) % chips], order, -1)


def after(value, *earlier):
    return lax.optimization_barrier((value, earlier))[0]


def swap_core(value, pool):
    return lax.ppermute(value, "pool", [(at, at ^ 1) for at in range(pool)])


def swap_plane(value):
    return lax.ppermute(value, "head", [(0, 1), (1, 0)])


def holder(ring, me, back):
    chips = ring.shape[0] // 2
    chip = lax.div(me[0], CORES)
    place = lax.rem(ring[chips + chip] + chips - back, chips)
    return ring[place] * CORES + lax.rem(me[0], CORES)


def attend_kernel(pieces, owned, ids, ranks, ring, me, queries, cosine, sine, *refs):
    key_pieces, value_pieces, refs = refs[:pieces], refs[pieces : 2 * pieces], refs[2 * pieces :]
    stats, keys, values, within, rank_of, key_sem, value_sem = refs[-7:]
    slots = ids.shape[0]
    kv_local, _, head_dim = keys.shape
    near, sums = refs[: -7 - kv_local], refs[-7 - kv_local : -7]
    length = key_pieces[0].shape[2]
    tokens = queries.shape[0]
    groups = queries.shape[1] // (kv_local * head_dim)
    heads = kv_local * groups
    factor = math.log2(math.e) / math.sqrt(head_dim)
    across = (((1,), (1,)), ((), ()))

    for slot in range(slots):
        passage = ids[slot]
        home = lax.div(passage, owned)
        within[home] = passage - home * owned
        rank_of[home] = ranks[slot]
    homes = [holder(ring, me, piece) for piece in range(pieces)]

    def copy(source, target, sem, piece):
        rows = pl.ds(piece * length, length)
        return pltpu.make_async_copy(
            source[piece].at[within[homes[piece]]], target.at[:, rows], sem.at[piece]
        )

    key_copies = [copy(key_pieces, keys, key_sem, piece) for piece in range(pieces)]
    value_copies = [copy(value_pieces, values, value_sem, piece) for piece in range(pieces)]
    for each in key_copies + value_copies:
        each.start()
    for piece in range(pieces):
        key_copies[piece].wait()
        rank = rank_of[homes[piece]]
        cos = cosine[pl.ds(rank, 1), :]
        sin = sine[pl.ds(rank, 1), :]
        rows = pl.ds(piece * length, length)
        for head in range(kv_local):
            block = keys[head, rows, :].astype(jnp.float32)
            turned = block * cos + pltpu.roll(block, head_dim // 2, 1) * sin
            keys[head, rows, :] = turned.astype(jnp.bfloat16)
    for each in value_copies:
        each.wait()

    lane = lax.broadcasted_iota(jnp.int32, (tokens, LANES), 1)
    marks = jnp.zeros((tokens, LANES), jnp.float32)
    for head in range(kv_local):
        spans = [
            slice((head * groups + g) * head_dim, (head * groups + g + 1) * head_dim)
            for g in range(groups)
        ]
        rows = jnp.concatenate([queries[:, span] for span in spans], axis=0)
        scores = lax.dot_general(rows, keys[head], across, preferred_element_type=jnp.float32)
        peak = jnp.max(scores, axis=1, keepdims=True)
        if near:
            own = slice(head * head_dim, (head + 1) * head_dim)
            close = lax.dot_general(
                rows, near[0][:, own], across, preferred_element_type=jnp.float32
            )
            token = lax.rem(lax.broadcasted_iota(jnp.int32, close.shape, 0), tokens)
            column = lax.broadcasted_iota(jnp.int32, close.shape, 1)
            close = jnp.where(column <= token, close, -jnp.inf)
            peak = jnp.maximum(peak, jnp.max(close, axis=1, keepdims=True))
        exponent = jnp.exp2((scores - peak) * factor)
        total = jnp.sum(exponent, axis=1, keepdims=True)
        summed = jnp.dot(
            exponent.astype(jnp.bfloat16), values[head], preferred_element_type=jnp.float32
        )
        if near:
            exponent = jnp.exp2((close - peak) * factor)
            total = total + jnp.sum(exponent, axis=1, keepdims=True)
            summed = summed + jnp.dot(
                exponent.astype(jnp.bfloat16), near[1][:, own], preferred_element_type=jnp.float32
            )
        for g in range(groups):
            part = slice(g * tokens, (g + 1) * tokens)
            sums[head][:, g * head_dim : (g + 1) * head_dim] = summed[part]
            at = head * groups + g
            marks = jnp.where(lane == at, peak[part], marks)
            marks = jnp.where(lane == heads + at, total[part], marks)
    stats[...] = marks


def attend(ids, ranks, ring, me, queries, tables, near, passages, effort=24):
    pieces = len(passages[0])
    key_pieces, value_pieces = passages
    owned, kv_local, length, head_dim = key_pieces[0].shape
    tokens, features = queries.shape
    holders = ids.shape[0]
    smem = pl.BlockSpec(memory_space=pltpu.SMEM)
    vmem = pl.BlockSpec(memory_space=pltpu.VMEM)
    seen = pieces * length
    scores = tokens * (features // head_dim) * (seen + (length if near else 0))
    return pl.pallas_call(
        functools.partial(attend_kernel, pieces, owned),
        out_shape=[jax.ShapeDtypeStruct((tokens, features // kv_local), jnp.float32)] * kv_local
        + [jax.ShapeDtypeStruct((tokens, LANES), jnp.float32)],
        in_specs=[smem] * 4
        + [vmem] * 3
        + [pl.BlockSpec(memory_space=pl.ANY)] * (2 * pieces)
        + [vmem] * len(near),
        out_specs=[vmem] * (kv_local + 1),
        scratch_shapes=[
            pltpu.VMEM((kv_local, seen, head_dim), jnp.bfloat16),
            pltpu.VMEM((kv_local, seen, head_dim), jnp.bfloat16),
            pltpu.SMEM((holders,), jnp.int32),
            pltpu.SMEM((holders,), jnp.int32),
            pltpu.SemaphoreType.DMA((pieces,)),
            pltpu.SemaphoreType.DMA((pieces,)),
        ],
        compiler_params=pltpu.CompilerParams(vmem_limit_bytes=32 * MIB),
        cost_estimate=pl.CostEstimate(
            flops=effort * scores * head_dim, bytes_accessed=4 * MIB, transcendentals=scores
        ),
        name="attend",
    )(ids, ranks, ring, me, queries, *tables, *key_pieces, *value_pieces, *near)


def combine_kernel(head_dim, *refs):
    attended, refs = refs[-1], refs[:-1]
    count = len(refs) // 2
    sums, stats = refs[: count - 1], refs[count - 1]
    sums_in, stats_in = refs[count:-1], refs[-1]
    groups = sums[0].shape[1] // head_dim
    heads = groups * len(sums)
    factor = math.log2(math.e) / math.sqrt(head_dim)
    for head in range(heads):
        block, at = divmod(head, groups)
        columns = slice(at * head_dim, (at + 1) * head_dim)
        peak_a, peak_b = stats[:, head : head + 1], stats_in[:, head : head + 1]
        at = heads + head
        total_a, total_b = stats[:, at : at + 1], stats_in[:, at : at + 1]
        peak = jnp.maximum(peak_a, peak_b)
        part_a = jnp.exp2((peak_a - peak) * factor)
        part_b = jnp.exp2((peak_b - peak) * factor)
        total = total_a * part_a + total_b * part_b
        value = sums[block][:, columns] * part_a + sums_in[block][:, columns] * part_b
        columns = slice(head * head_dim, (head + 1) * head_dim)
        attended[:, columns] = (value / total).astype(attended.dtype)


def combine(head_dim, state, state_in):
    tokens, width = state[0].shape
    size = tokens * width * (len(state) - 1)
    vmem = pl.BlockSpec(memory_space=pltpu.VMEM)
    return pl.pallas_call(
        functools.partial(combine_kernel, head_dim),
        out_shape=jax.ShapeDtypeStruct((tokens, size // tokens), jnp.bfloat16),
        in_specs=[vmem] * (2 * len(state)),
        out_specs=vmem,
        compiler_params=pltpu.CompilerParams(vmem_limit_bytes=24 * MIB),
        cost_estimate=pl.CostEstimate(flops=4 * size, bytes_accessed=10 * size, transcendentals=0),
        name="combine",
    )(*state, *state_in)


def project_kernel(items, based, ring, me, own_rows, other_rows, *refs):
    count = sum(len(heights) for _, _, heights in items)
    blocks, refs = refs[:count], refs[count:]
    base = None
    if based:
        base, refs = refs[0], refs[1:]
    results, (held, total, sems) = refs[:-3], refs[-3:]
    span = held.shape[1] // 2
    copies, at = [], 0
    for item, (_, _, heights) in enumerate(items):
        copies.append([])
        for i, height in enumerate(heights):
            target = held.at[item, pl.ds(sum(heights[:i]), height)]
            copies[-1].append(pltpu.make_async_copy(blocks[at], target, sems.at[at]))
            at += 1
    for group in copies:
        for copy in group:
            copy.start()
    for item, (place, crossed, _) in enumerate(items):
        for copy in copies[item]:
            copy.wait()
        home = holder(ring, me, place)
        if crossed:
            home = home + 1 - 2 * lax.rem(home, CORES)
        columns = pl.ds(pl.multiple_of(home * span, span), span)
        value = jnp.dot(
            jnp.concatenate([rows[:, columns] for rows in (own_rows, other_rows)], axis=1),
            held[item],
            preferred_element_type=jnp.float32,
        )
        if item:
            value = value + total[...]
        elif base is not None:
            value = value + base[...]
        if item + 1 < len(items):
            total[...] = value
    tokens, width = results[0].shape[0], value.shape[1]
    for part, result in enumerate(results):
        block = value[part * tokens : (part + 1) * tokens].astype(result.dtype)
        if result.shape[1] == width:
            result[...] = block
        else:
            first = pl.multiple_of(lax.rem(me[0], CORES) * width, width)
            result[:, pl.ds(first, width)] = block


def project(ring, me, rows, blocks, base, shapes):
    flat = [part.reshape(-1, part.shape[-1]) for parts in blocks.values() for part in parts]
    heights = iter([part.shape[0] for part in flat])
    items = tuple(
        (place, crossed, tuple(next(heights) for _ in parts))
        for (place, crossed), parts in blocks.items()
    )
    tokens, width = rows[0].shape[0], flat[0].shape[1]
    height = sum(items[0][2])
    size = len(items) * height * width
    smem = pl.BlockSpec(memory_space=pltpu.SMEM)
    vmem = pl.BlockSpec(memory_space=pltpu.VMEM)
    return pl.pallas_call(
        functools.partial(project_kernel, items, base is not None),
        out_shape=shapes,
        in_specs=[smem] * 2
        + [vmem] * 2
        + [pl.BlockSpec(memory_space=pl.ANY)] * len(flat)
        + ([vmem] if base is not None else []),
        out_specs=[vmem] * len(shapes),
        scratch_shapes=[
            pltpu.VMEM((len(items), height, width), jnp.bfloat16),
            pltpu.VMEM((tokens, width), jnp.float32),
            pltpu.SemaphoreType.DMA((len(flat),)),
        ],
        compiler_params=pltpu.CompilerParams(vmem_limit_bytes=32 * MIB),
        cost_estimate=pl.CostEstimate(
            flops=2 * tokens * size, bytes_accessed=2 * size + 4 * tokens * width, transcendentals=0
        ),
        name="project",
    )(ring, me, *rows, *flat, *([base] if base is not None else []))


def rotation_tables(ranks, length, head_dim):
    offsets = (jnp.arange(ranks) * length).astype(jnp.float32)
    angles = offsets[:, None] * frequency_table(head_dim)[None, :]
    cosine, sine = jnp.cos(angles), jnp.sin(angles)
    return (
        jnp.concatenate([cosine, cosine], axis=1),
        jnp.concatenate([-sine, sine], axis=1),
    )


def ring_body(
    pool,
    queries,
    request_keys,
    request_values,
    cache_keys,
    cache_values,
    passage_ids,
    passage_order,
    out_weight,
):
    _, _, pass_len, head_dim = cache_keys.shape
    tokens = queries.shape[1]
    chips = pool // CORES
    half = chips // 2
    order = ring_order(chips)
    ring = jnp.asarray(order + [order.index(chip) for chip in range(chips)], jnp.int32)
    index = lax.axis_index("pool")
    me = jnp.reshape(index, (1,))
    core = lax.rem(index, CORES)
    plane = lax.axis_index("head")

    span = out_weight.shape[1] // 2
    width = span // CORES
    other_queries = swap_core(queries[0], pool)
    weight, other_queries = lax.optimization_barrier((out_weight, other_queries))
    across = swap_plane(
        lax.dynamic_slice_in_dim(weight, (1 - plane) * span, span, axis=1)
    )

    kept = {0: cache_keys}, {0: cache_values}
    for pieces in kept:
        onward(pieces, 1, order)
    for step in range(2, half):
        for pieces in kept:
            onward(pieces, step, order)

    out_weight, across = after(
        (out_weight, across),
        kept[0][2], kept[0][chips - 2],
    )

    def columns(to_core):
        first = to_core * width
        return jnp.stack(
            [
                lax.dynamic_slice_in_dim(out_weight, plane * span + first, width, axis=1),
                lax.dynamic_slice_in_dim(across, first, width, axis=1),
            ]
        )

    near, far = heavy = {0: columns(core)}, {0: swap_core(columns(1 - core), pool)}
    near[0] = after(near[0], *[kept[1][at] for at in (2, chips - 2)])
    far[0] = after(far[0], *[kept[0][at] for at in (half - 1, half + 1)])
    for step in range(1, half):
        for pieces in heavy:
            onward(pieces, step, order)

    queries, picks, last_keys, last_values = after(
        (
            queries[0],
            jnp.concatenate([passage_ids, passage_order], axis=0),
            kept[0][half - 1],
            kept[1][half + 1],
        ),
        near[1],
        near[chips - 1],
    )
    kept[0][half] = shift(last_keys, order, 1)
    kept[1][half] = shift(last_values, order, -1)
    passages = [[pieces[at] for at in range(chips)] for pieces in kept]

    picks_in = swap_core(picks, pool)
    other_queries = after(
        other_queries, far[1], far[chips - 1]
    )
    tables = rotation_tables(passage_ids.shape[1], pass_len, head_dim)
    other = attend(picks_in[0], picks_in[1], ring, me, other_queries, tables, (), passages)
    own_block = (request_keys[0], request_values[0])
    other_in = [swap_core(value, pool) for value in other]
    queries, other_in = after((queries, other_in), near[2], near[chips - 2])
    own = attend(picks[0], picks[1], ring, me, queries, tables, own_block, passages, 1)
    own = after(own, far[2], far[chips - 2])

    attended = combine(head_dim, own, other_in)
    turned = after(swap_plane(attended), near[3], near[chips - 3])
    quarters = {}

    def last(crossed, cut):
        ahead, back = (
            heavy[crossed][at].reshape(-1, width) for at in (half - 1, half + 1)
        )
        quarters[(half, crossed)] = (shift(ahead[:cut], order, 1), shift(back[cut:], order, -1))

    rows_held = CORES * heavy[0][0].shape[1]
    last(0, rows_held * 9 // 16)
    last(1, rows_held * 8 // 16)
    crossed_rows = swap_core(turned, pool)
    crossed_rows = after(crossed_rows, far[3], far[chips - 3])
    swapped = swap_core(attended, pool)
    rows = [
        jnp.concatenate([attended, swapped], axis=0),
        jnp.concatenate([turned, crossed_rows], axis=0),
    ]

    def blocks(places):
        return {(at, part): (heavy[part][at],) for at in places for part in range(2)}

    sums = [jax.ShapeDtypeStruct((CORES * tokens, width), jnp.float32)]
    early = [0] + [at for step in range(1, half - 1) for at in (step, chips - step)]
    total = project(ring, me, rows, blocks(early), None, sums)[0]
    middle = blocks([half - 1, half + 1]) | {(half, 0): quarters[half, 0]}
    sums = [jax.ShapeDtypeStruct((tokens, width), jnp.float32)] * CORES
    own_total, other_total = project(ring, me, rows, middle, total, sums)

    block = [jax.ShapeDtypeStruct((tokens, width), jnp.bfloat16)]
    end = {(half, 1): quarters[half, 1]}
    other_rows = [swapped, crossed_rows]
    beside = swap_core(project(ring, me, other_rows, end, other_total, block)[0], pool)
    whole = [jax.ShapeDtypeStruct((tokens, span), jnp.bfloat16)]
    result = project(ring, me, [attended, turned], end, own_total, whole)[0]
    result = lax.dynamic_update_slice_in_dim(result, beside, (1 - core) * width, axis=1)
    return result[None]


def solution(mesh):
    pool, heads_axis = mesh.shape["pool"], mesh.shape["head"]

    def body(*args):
        weight = args[-1]
        tiled = weight.shape[0] % LANES == 0 and weight.shape[1] % (2 * CORES * LANES) == 0
        if tiled and heads_axis == 2 and pool % (2 * ROWS * CORES) == 0:
            return ring_body(pool, *args)
        return plain_body(*args)

    placed = (
        P("pool", None, "head"),
        P("pool", None, "head"),
        P("pool", None, "head"),
        P("pool", "head", None, None),
        P("pool", "head", None, None),
        P("pool", None),
        P("pool", None),
        P(("head", "pool"), None),
    )
    return jax.shard_map(
        body, mesh=mesh, in_specs=placed, out_specs=P("pool", None, "head"), check_vma=False
    )
```

```python
import functools
import math

import jax
import jax.numpy as jnp
from jax import lax
from jax.experimental import pallas as pl
from jax.experimental.pallas import tpu as pltpu
from jax.sharding import PartitionSpec as P

CORES = 2
ROWS = 4
LANES = 128
MIB = 1024 * 1024


def frequency_table(head_dim):
    pair_index = jnp.arange(head_dim // 2, dtype=jnp.float32)
    return jnp.exp(pair_index * (-2.0 / head_dim) * jnp.log(jnp.float32(500000.0)))


def reposition(vectors, offset, head_dim):
    angles = offset.astype(jnp.float32) * frequency_table(head_dim)
    cosine = jnp.cos(angles)
    sine_term = jnp.sin(angles)
    front_half = vectors[..., : head_dim // 2]
    back_half = vectors[..., head_dim // 2 :]
    return jnp.concatenate(
        [front_half * cosine - back_half * sine_term, back_half * cosine + front_half * sine_term],
        axis=-1,
    )


def absorb(state, query_rows, keys_block, values_block, allowed):
    running_peak, running_total, running_sum = state
    scores = jnp.einsum(
        "hrd,hnd->hrn", query_rows, keys_block, preferred_element_type=jnp.float32
    ) * query_rows.shape[2] ** (-0.5)
    if allowed is not None:
        scores = jnp.where(allowed[None], scores, -jnp.inf)
    new_peak = jnp.maximum(running_peak, jnp.max(scores, axis=-1))
    factor = jnp.exp(running_peak - new_peak)
    exponent = jnp.exp(scores - new_peak[..., None])
    weights = exponent.astype(jnp.bfloat16)
    new_total = running_total * factor + jnp.sum(exponent, axis=-1)
    new_sum = running_sum * factor[..., None] + jnp.einsum(
        "hrn,hnd->hrd", weights, values_block, preferred_element_type=jnp.float32
    )
    return (new_peak, new_total, new_sum)


def plain_body(
    queries,
    request_keys,
    request_values,
    cache_keys,
    cache_values,
    passage_ids,
    passage_order,
    out_weight,
):
    owned, kv_local, pass_len, head_dim = cache_keys.shape
    query_len = queries.shape[1]
    groups = queries.shape[2] // (kv_local * head_dim)
    row_count = query_len * groups
    query_rows = (
        queries[0]
        .reshape(query_len, kv_local, groups, head_dim)
        .transpose(1, 0, 2, 3)
        .reshape(kv_local, row_count, head_dim)
    )
    own_keys = request_keys[0].reshape(query_len, kv_local, head_dim).transpose(1, 0, 2)
    own_values = request_values[0].reshape(query_len, kv_local, head_dim).transpose(1, 0, 2)
    query_token = jnp.arange(row_count) // groups
    causal = jnp.arange(query_len)[None, :] <= query_token[:, None]
    state = (
        jnp.full((kv_local, row_count), -jnp.inf, jnp.float32),
        jnp.zeros((kv_local, row_count), jnp.float32),
        jnp.zeros((kv_local, row_count, head_dim), jnp.float32),
    )
    state = absorb(state, query_rows, own_keys, own_values, causal)
    slots = passage_ids[0]
    offsets = passage_order[0] * pass_len
    piece_keys = lax.all_gather(cache_keys, "pool", axis=0, tiled=True)
    piece_values = lax.all_gather(cache_values, "pool", axis=0, tiled=True)

    def visit_one(position, current):
        matches = slots == position
        offset = jnp.sum(jnp.where(matches, offsets, 0))

        def absorb_one(inner):
            placed = reposition(piece_keys[position].astype(jnp.float32), offset, head_dim).astype(
                jnp.bfloat16
            )
            return absorb(inner, query_rows, placed, piece_values[position], None)

        return lax.cond(jnp.any(matches), absorb_one, lambda inner: inner, current)

    state = lax.fori_loop(0, piece_keys.shape[0], visit_one, state)
    running_peak, running_total, running_sum = state
    attended = (running_sum / running_total[..., None]).astype(jnp.bfloat16)
    attended = (
        attended.reshape(kv_local, query_len, groups, head_dim)
        .transpose(1, 0, 2, 3)
        .reshape(query_len, kv_local * groups * head_dim)
    )
    partial_value = jnp.dot(
        attended,
        lax.all_gather(out_weight, "pool", axis=0, tiled=True),
        preferred_element_type=jnp.float32,
    )
    summed = lax.psum_scatter(
        partial_value.astype(jnp.bfloat16), "head", scatter_dimension=1, tiled=True
    )
    return summed[None]


def ring_order(chips):
    columns = chips // ROWS
    cells = []
    for row in range(ROWS):
        across = range(1, columns) if row % 2 == 0 else range(columns - 1, 0, -1)
        cells += [row * columns + column for column in across]
    return cells + [row * columns for row in reversed(range(ROWS))]


def shift(value, order, step):
    chips = len(order)
    pairs = [
        (order[at] * CORES + core, order[(at + step) % chips] * CORES + core)
        for at in range(chips)
        for core in range(CORES)
    ]
    return lax.ppermute(value, "pool", pairs)


def onward(pieces, step, order):
    chips = len(order)
    pieces[step] = shift(pieces[step - 1], order, 1)
    pieces[chips - step] = shift(pieces[(chips - step + 1) % chips], order, -1)


def after(value, *earlier):
    return lax.optimization_barrier((value, earlier))[0]


def swap_core(value, pool):
    return lax.ppermute(value, "pool", [(at, at ^ 1) for at in range(pool)])


def swap_plane(value):
    return lax.ppermute(value, "head", [(0, 1), (1, 0)])


def holder(ring, me, back):
    chips = ring.shape[0] // 2
    chip = lax.div(me[0], CORES)
    place = lax.rem(ring[chips + chip] + chips - back, chips)
    return ring[place] * CORES + lax.rem(me[0], CORES)


def attend_kernel(pieces, owned, ids, ranks, ring, me, queries, cosine, sine, *refs):
    key_pieces, value_pieces, refs = refs[:pieces], refs[pieces : 2 * pieces], refs[2 * pieces :]
    stats, keys, values, within, rank_of, key_sem, value_sem = refs[-7:]
    slots = ids.shape[0]
    kv_local, _, head_dim = keys.shape
    near, sums = refs[: -7 - kv_local], refs[-7 - kv_local : -7]
    length = key_pieces[0].shape[2]
    tokens = queries.shape[0]
    groups = queries.shape[1] // (kv_local * head_dim)
    heads = kv_local * groups
    factor = math.log2(math.e) / math.sqrt(head_dim)
    across = (((1,), (1,)), ((), ()))

    for slot in range(slots):
        passage = ids[slot]
        home = lax.div(passage, owned)
        within[home] = passage - home * owned
        rank_of[home] = ranks[slot]
    homes = [holder(ring, me, piece) for piece in range(pieces)]

    def copy(source, target, sem, piece):
        rows = pl.ds(piece * length, length)
        return pltpu.make_async_copy(
            source[piece].at[within[homes[piece]]], target.at[:, rows], sem.at[piece]
        )

    key_copies = [copy(key_pieces, keys, key_sem, piece) for piece in range(pieces)]
    value_copies = [copy(value_pieces, values, value_sem, piece) for piece in range(pieces)]
    for each in key_copies + value_copies:
        each.start()
    for piece in range(pieces):
        key_copies[piece].wait()
        rank = rank_of[homes[piece]]
        cos = cosine[pl.ds(rank, 1), :]
        sin = sine[pl.ds(rank, 1), :]
        rows = pl.ds(piece * length, length)
        for head in range(kv_local):
            block = keys[head, rows, :].astype(jnp.float32)
            turned = block * cos + pltpu.roll(block, head_dim // 2, 1) * sin
            keys[head, rows, :] = turned.astype(jnp.bfloat16)
    for each in value_copies:
        each.wait()

    lane = lax.broadcasted_iota(jnp.int32, (tokens, LANES), 1)
    marks = jnp.zeros((tokens, LANES), jnp.float32)
    for head in range(kv_local):
        spans = [
            slice((head * groups + g) * head_dim, (head * groups + g + 1) * head_dim)
            for g in range(groups)
        ]
        rows = jnp.concatenate([queries[:, span] for span in spans], axis=0)
        scores = lax.dot_general(rows, keys[head], across, preferred_element_type=jnp.float32)
        peak = jnp.max(scores, axis=1, keepdims=True)
        if near:
            own = slice(head * head_dim, (head + 1) * head_dim)
            close = lax.dot_general(
                rows, near[0][:, own], across, preferred_element_type=jnp.float32
            )
            token = lax.rem(lax.broadcasted_iota(jnp.int32, close.shape, 0), tokens)
            column = lax.broadcasted_iota(jnp.int32, close.shape, 1)
            close = jnp.where(column <= token, close, -jnp.inf)
            peak = jnp.maximum(peak, jnp.max(close, axis=1, keepdims=True))
        exponent = jnp.exp2((scores - peak) * factor)
        total = jnp.sum(exponent, axis=1, keepdims=True)
        summed = jnp.dot(
            exponent.astype(jnp.bfloat16), values[head], preferred_element_type=jnp.float32
        )
        if near:
            exponent = jnp.exp2((close - peak) * factor)
            total = total + jnp.sum(exponent, axis=1, keepdims=True)
            summed = summed + jnp.dot(
                exponent.astype(jnp.bfloat16), near[1][:, own], preferred_element_type=jnp.float32
            )
        for g in range(groups):
            part = slice(g * tokens, (g + 1) * tokens)
            sums[head][:, g * head_dim : (g + 1) * head_dim] = summed[part]
            at = head * groups + g
            marks = jnp.where(lane == at, peak[part], marks)
            marks = jnp.where(lane == heads + at, total[part], marks)
    stats[...] = marks


def attend(ids, ranks, ring, me, queries, tables, near, passages, effort=24):
    pieces = len(passages[0])
    key_pieces, value_pieces = passages
    owned, kv_local, length, head_dim = key_pieces[0].shape
    tokens, features = queries.shape
    holders = ids.shape[0]
    smem = pl.BlockSpec(memory_space=pltpu.SMEM)
    vmem = pl.BlockSpec(memory_space=pltpu.VMEM)
    seen = pieces * length
    scores = tokens * (features // head_dim) * (seen + (length if near else 0))
    return pl.pallas_call(
        functools.partial(attend_kernel, pieces, owned),
        out_shape=[jax.ShapeDtypeStruct((tokens, features // kv_local), jnp.float32)] * kv_local
        + [jax.ShapeDtypeStruct((tokens, LANES), jnp.float32)],
        in_specs=[smem] * 4
        + [vmem] * 3
        + [pl.BlockSpec(memory_space=pl.ANY)] * (2 * pieces)
        + [vmem] * len(near),
        out_specs=[vmem] * (kv_local + 1),
        scratch_shapes=[
            pltpu.VMEM((kv_local, seen, head_dim), jnp.bfloat16),
            pltpu.VMEM((kv_local, seen, head_dim), jnp.bfloat16),
            pltpu.SMEM((holders,), jnp.int32),
            pltpu.SMEM((holders,), jnp.int32),
            pltpu.SemaphoreType.DMA((pieces,)),
            pltpu.SemaphoreType.DMA((pieces,)),
        ],
        compiler_params=pltpu.CompilerParams(vmem_limit_bytes=32 * MIB),
        cost_estimate=pl.CostEstimate(
            flops=effort * scores * head_dim, bytes_accessed=4 * MIB, transcendentals=scores
        ),
        name="attend",
    )(ids, ranks, ring, me, queries, *tables, *key_pieces, *value_pieces, *near)


def combine_kernel(head_dim, *refs):
    attended, refs = refs[-1], refs[:-1]
    count = len(refs) // 2
    sums, stats = refs[: count - 1], refs[count - 1]
    sums_in, stats_in = refs[count:-1], refs[-1]
    groups = sums[0].shape[1] // head_dim
    heads = groups * len(sums)
    factor = math.log2(math.e) / math.sqrt(head_dim)
    for head in range(heads):
        block, at = divmod(head, groups)
        columns = slice(at * head_dim, (at + 1) * head_dim)
        peak_a, peak_b = stats[:, head : head + 1], stats_in[:, head : head + 1]
        at = heads + head
        total_a, total_b = stats[:, at : at + 1], stats_in[:, at : at + 1]
        peak = jnp.maximum(peak_a, peak_b)
        part_a = jnp.exp2((peak_a - peak) * factor)
        part_b = jnp.exp2((peak_b - peak) * factor)
        total = total_a * part_a + total_b * part_b
        value = sums[block][:, columns] * part_a + sums_in[block][:, columns] * part_b
        columns = slice(head * head_dim, (head + 1) * head_dim)
        attended[:, columns] = (value / total).astype(attended.dtype)


def combine(head_dim, state, state_in):
    tokens, width = state[0].shape
    size = tokens * width * (len(state) - 1)
    vmem = pl.BlockSpec(memory_space=pltpu.VMEM)
    return pl.pallas_call(
        functools.partial(combine_kernel, head_dim),
        out_shape=jax.ShapeDtypeStruct((tokens, size // tokens), jnp.bfloat16),
        in_specs=[vmem] * (2 * len(state)),
        out_specs=vmem,
        compiler_params=pltpu.CompilerParams(vmem_limit_bytes=24 * MIB),
        cost_estimate=pl.CostEstimate(flops=4 * size, bytes_accessed=10 * size, transcendentals=0),
        name="combine",
    )(*state, *state_in)


def project_kernel(items, based, direct, ring, me, own_rows, other_rows, *refs):
    count = sum(len(heights) for _, _, heights in items)
    blocks, refs = refs[:count], refs[count:]
    base = None
    if based:
        base, refs = refs[0], refs[1:]
    results, (held, total, sems) = refs[:-3], refs[-3:]
    span = held.shape[1] // 2
    copies, at = [], 0
    for item, (_, _, heights) in enumerate(items):
        copies.append([])
        if direct:
            continue
        for i, height in enumerate(heights):
            target = held.at[item, pl.ds(sum(heights[:i]), height)]
            copies[-1].append(pltpu.make_async_copy(blocks[at], target, sems.at[at]))
            at += 1
    for group in copies:
        for copy in group:
            copy.start()
    for item, (place, crossed, _) in enumerate(items):
        for copy in copies[item]:
            copy.wait()
        home = holder(ring, me, place)
        if crossed:
            home = home + 1 - 2 * lax.rem(home, CORES)
        columns = pl.ds(pl.multiple_of(home * span, span), span)
        value = jnp.dot(
            jnp.concatenate([rows[:, columns] for rows in (own_rows, other_rows)], axis=1),
            jnp.concatenate([block[...] for block in blocks], axis=0) if direct else held[item],
            preferred_element_type=jnp.float32,
        )
        if item:
            value = value + total[...]
        elif base is not None:
            value = value + base[...]
        if item + 1 < len(items):
            total[...] = value
    tokens = results[0].shape[0]
    for part, result in enumerate(results):
        result[...] = value[part * tokens : (part + 1) * tokens].astype(result.dtype)


def project(ring, me, rows, blocks, base, shapes, direct=False):
    flat = [part.reshape(-1, part.shape[-1]) for parts in blocks.values() for part in parts]
    heights = iter([part.shape[0] for part in flat])
    items = tuple(
        (place, crossed, tuple(next(heights) for _ in parts))
        for (place, crossed), parts in blocks.items()
    )
    tokens, width = rows[0].shape[0], flat[0].shape[1]
    height = sum(items[0][2])
    size = len(items) * height * width
    smem = pl.BlockSpec(memory_space=pltpu.SMEM)
    vmem = pl.BlockSpec(memory_space=pltpu.VMEM)
    return pl.pallas_call(
        functools.partial(project_kernel, items, base is not None, direct),
        out_shape=shapes,
        in_specs=[smem] * 2
        + [vmem] * 2
        + [vmem if direct else pl.BlockSpec(memory_space=pl.ANY)] * len(flat)
        + ([vmem] if base is not None else []),
        out_specs=[vmem] * len(shapes),
        scratch_shapes=[
            pltpu.VMEM((len(items), height, width), jnp.bfloat16),
            pltpu.VMEM((tokens, width), jnp.float32),
            pltpu.SemaphoreType.DMA((len(flat),)),
        ],
        compiler_params=pltpu.CompilerParams(vmem_limit_bytes=32 * MIB),
        cost_estimate=pl.CostEstimate(
            flops=2 * tokens * size, bytes_accessed=2 * size + 4 * tokens * width, transcendentals=0
        ),
        name="project",
    )(ring, me, *rows, *flat, *([base] if base is not None else []))


def rotation_tables(ranks, length, head_dim):
    offsets = (jnp.arange(ranks) * length).astype(jnp.float32)
    angles = offsets[:, None] * frequency_table(head_dim)[None, :]
    cosine, sine = jnp.cos(angles), jnp.sin(angles)
    return (
        jnp.concatenate([cosine, cosine], axis=1),
        jnp.concatenate([-sine, sine], axis=1),
    )


def ring_body(
    pool,
    queries,
    request_keys,
    request_values,
    cache_keys,
    cache_values,
    passage_ids,
    passage_order,
    out_weight,
):
    _, _, pass_len, head_dim = cache_keys.shape
    tokens = queries.shape[1]
    chips = pool // CORES
    half = chips // 2
    order = ring_order(chips)
    ring = jnp.asarray(order + [order.index(chip) for chip in range(chips)], jnp.int32)
    index = lax.axis_index("pool")
    me = jnp.reshape(index, (1,))
    core = lax.rem(index, CORES)
    plane = lax.axis_index("head")

    span = out_weight.shape[1] // 2
    width = span // CORES
    other_queries = swap_core(queries[0], pool)
    weight, other_queries = lax.optimization_barrier((out_weight, other_queries))
    across = swap_plane(
        lax.dynamic_slice_in_dim(weight, (1 - plane) * span, span, axis=1)
    )

    kept = {0: cache_keys}, {0: cache_values}
    for pieces in kept:
        onward(pieces, 1, order)
    for step in range(2, half):
        for pieces in kept:
            onward(pieces, step, order)

    out_weight, across = after(
        (out_weight, across),
        kept[0][2], kept[0][chips - 2],
    )

    def columns(to_core):
        first = to_core * width
        return jnp.stack(
            [
                lax.dynamic_slice_in_dim(out_weight, plane * span + first, width, axis=1),
                lax.dynamic_slice_in_dim(across, first, width, axis=1),
            ]
        )

    near, far = heavy = {0: columns(core)}, {0: swap_core(columns(1 - core), pool)}
    near[0] = after(near[0], *[kept[1][at] for at in (2, chips - 2)])
    far[0] = after(far[0], *[kept[0][at] for at in (half - 1, half + 1)])
    for step in range(1, half):
        for pieces in heavy:
            onward(pieces, step, order)

    queries, picks, last_keys, last_values = after(
        (
            queries[0],
            jnp.concatenate([passage_ids, passage_order], axis=0),
            kept[0][half - 1],
            kept[1][half + 1],
        ),
        near[1],
        near[chips - 1],
    )
    kept[0][half] = shift(last_keys, order, 1)
    kept[1][half] = shift(last_values, order, -1)
    passages = [[pieces[at] for at in range(chips)] for pieces in kept]

    picks_in = swap_core(picks, pool)
    other_queries = after(
        other_queries, far[1], far[chips - 1]
    )
    tables = rotation_tables(passage_ids.shape[1], pass_len, head_dim)
    other = attend(picks_in[0], picks_in[1], ring, me, other_queries, tables, (), passages)
    own_block = (request_keys[0], request_values[0])
    other_in = [swap_core(value, pool) for value in other]
    queries, other_in = after((queries, other_in), near[2], near[chips - 2])
    own = attend(picks[0], picks[1], ring, me, queries, tables, own_block, passages, 1)
    own = after(own, far[2], far[chips - 2])

    attended = combine(head_dim, own, other_in)
    turned = after(swap_plane(attended), near[3], near[chips - 3])
    quarters = {}

    def last(crossed, cut):
        ahead, back = (
            heavy[crossed][at].reshape(-1, width) for at in (half - 1, half + 1)
        )
        quarters[(half, crossed)] = (shift(ahead[:cut], order, 1), shift(back[cut:], order, -1))

    rows_held = CORES * heavy[0][0].shape[1]
    last(0, rows_held * 9 // 16)
    last(1, rows_held * 8 // 16)
    crossed_rows = swap_core(turned, pool)
    crossed_rows = after(crossed_rows, far[3], far[chips - 3])
    rows = [
        jnp.concatenate([attended, swap_core(attended, pool)], axis=0),
        jnp.concatenate([turned, crossed_rows], axis=0),
    ]

    def blocks(places):
        return {(at, part): (heavy[part][at],) for at in places for part in range(2)}

    sums = [jax.ShapeDtypeStruct((CORES * tokens, width), jnp.float32)]
    early = [0] + [at for step in range(1, half - 1) for at in (step, chips - step)]
    total = project(ring, me, rows, blocks(early), None, sums)[0]
    middle = blocks([half - 1, half + 1]) | {(half, 0): quarters[half, 0]}
    total = project(ring, me, rows, middle, total, sums)[0]
    own_out, other_out = project(
        ring,
        me,
        rows,
        {(half, 1): quarters[half, 1]},
        total,
        [jax.ShapeDtypeStruct((tokens, width), jnp.bfloat16)] * 2,
        direct=True,
    )
    beside = swap_core(other_out, pool)
    result = jnp.where(
        core == 0,
        jnp.concatenate([own_out, beside], axis=1),
        jnp.concatenate([beside, own_out], axis=1),
    )
    return result[None]


def solution(mesh):
    pool, heads_axis = mesh.shape["pool"], mesh.shape["head"]

    def body(*args):
        weight = args[-1]
        tiled = weight.shape[0] % LANES == 0 and weight.shape[1] % (2 * CORES * LANES) == 0
        if tiled and heads_axis == 2 and pool % (2 * ROWS * CORES) == 0:
            return ring_body(pool, *args)
        return plain_body(*args)

    placed = (
        P("pool", None, "head"),
        P("pool", None, "head"),
        P("pool", None, "head"),
        P("pool", "head", None, None),
        P("pool", "head", None, None),
        P("pool", None),
        P("pool", None),
        P(("head", "pool"), None),
    )
    return jax.shard_map(
        body, mesh=mesh, in_specs=placed, out_specs=P("pool", None, "head"), check_vma=False
    )
```
